512 devices in a mesh: dp: 32 (over x, z_lo, core), owner: 16 (over z_hi, y).
Axes of the slice: x: 4, y: 4, z: 16 (z_hi: 4, z_lo: 4; z = z_hi * 4 + z_lo), core: 2. Of those that a mesh axis runs over, the one named last changes fastest.
Arguments:
- feats: bfloat16 [4, 32, 32, 80, 128], P(None, 'dp', 'owner'), may hold values from -16 to 16
- top_grad: bfloat16 [32, 32, 80, 128], P('dp', 'owner'), may hold values from -6 to 6
- weights: bfloat16 [4, 1152, 128], replicated, may hold values from -0.1875 to 0.1875
- table: int32 [4], replicated, may hold values from 0 to 15, as said below
- a_inv: bfloat16 [16, 1152, 1152], P('owner', 'dp'), may hold values from -3 to 3
- g_inv: float32 [16, 128, 128], P('owner'), may hold values from -3 to 3
Outputs:
- step: bfloat16 [4, 1152, 128], P(None, 'dp')
- a_stat: float32 [16, 1152, 1152], P('owner', 'dp')
- g_stat: float32 [16, 128, 128], P('owner')
- in_grad: bfloat16 [32, 32, 80, 128], P('dp', 'owner')
The draws below stay inside these ranges and needn't reach their ends.
Inputs may be any that keep to these rules, and one draw needn't show every extreme that they name: `table`: 4 distinct owner indices; 0 and 15 are always among them.
All inputs are finite; a program needn't handle non-finite values.
Results may differ from the reference program's by a relative error of at most 0.023.
Values may be sent and summed in bfloat16 or wider, within the bound.
No kernel may reach another device: no remote copies, remote signals or barrier semaphores. Data moves between devices by JAX's collectives and lax.ppermute only.
A program may use at most 64 MiB of HBM per device.

```python
import jax
import jax.numpy as jnp
from jax import lax

C = 128
W = 80
L = 4
K9 = 1152
H = 32
N_DP = 32
N_OWNER = 16


def sample_levels(key, spread):
    grid = jnp.linspace(-spread, spread, N_DP).astype(jnp.float32)
    levels = grid[jax.random.permutation(key, N_DP)]
    amps = jnp.exp(levels)
    amps = amps / jnp.sqrt(jnp.mean(amps * amps))
    return amps.reshape(1, N_DP, 1, 1, 1)


def draw_feats(key, part):
    key = jax.random.fold_in(key, 11)
    keys = jax.random.split(key, 5)
    base = jax.random.normal(keys[0], (L, N_DP, H, W, C), jnp.float32)
    amps = sample_levels(keys[4], 0.55)
    common = jax.random.normal(keys[1], (L, N_DP, H, W, 1), jnp.float32)
    loads = jax.random.normal(keys[2], (L, 1, 1, 1, C), jnp.float32)
    scales = jnp.exp(jax.random.uniform(keys[3], (L, 1, 1, 1, C), jnp.float32, jnp.log(0.3), jnp.log(3.0)))
    return jnp.clip((base + 0.7 * common * loads) * scales * amps, -16.0, 16.0).astype(jnp.bfloat16)


def draw_table(key, part):
    key = jax.random.fold_in(key, 12)
    keys = jax.random.split(key, 2)
    middle = 1 + jax.random.permutation(keys[0], N_OWNER - 2)[:L - 2]
    values = jnp.concatenate([jnp.array([0, N_OWNER - 1], jnp.int32), middle.astype(jnp.int32)])
    return values[jax.random.permutation(keys[1], L)].astype(jnp.int32)


def dominant(key, count, order):
    keys = jax.random.split(key, 2)
    diag = jax.random.uniform(keys[0], (count, order), jnp.float32, 0.5, 2.0)
    off = jax.random.normal(keys[1], (count, order, order), jnp.float32)
    eye = (jnp.arange(order)[:, None] == jnp.arange(order)[None, :]).astype(jnp.float32)
    return jnp.clip(eye[None] * diag[:, :, None] + 0.5 / order ** 0.5 * off, -3.0, 3.0)


def draw_a_inv(key, part):
    key = jax.random.fold_in(key, 13)
    return dominant(key, N_OWNER, K9).astype(jnp.bfloat16)


def draw_g_inv(key, part):
    key = jax.random.fold_in(key, 14)
    return dominant(key, N_OWNER, C)


def steps_of(own_key, dims, shards, low, largest):
    level = 1.0
    for dim, parts in shards:
        heights = jax.random.uniform(jax.random.fold_in(jax.random.fold_in(own_key, 6), dim), (parts,), jnp.float32, low / len(shards), largest / len(shards))
        level = level * jnp.repeat(jnp.exp(heights), dims[dim] // parts).reshape((-1,) + (1,) * (len(dims) - 1 - dim))
    return level


def noise(stream_key, extent, scale, limit, cuts=(), held_as=jnp.bfloat16):
    gain = steps_of(stream_key, extent, cuts, -0.22, 0.18) if cuts else 1.0
    result = jax.random.normal(stream_key, extent, jnp.float32) * scale * gain
    return jnp.minimum(jnp.maximum(result, -limit), limit).astype(held_as)


def setup_inputs(seed: int = 0) -> dict:
    splits = jax.random.split(jax.random.key(seed), 7)
    feats = draw_feats(jax.random.fold_in(splits[6], 71), 0)
    top_grad = noise(splits[1], (N_DP, H, W, C), 1.0, 6.0, ((0, 32), (1, 16)))
    weights = noise(splits[2], (L, K9, C), K9 ** -0.5, 0.1875)
    table = draw_table(jax.random.fold_in(splits[6], 71), 0)
    a_inv = draw_a_inv(jax.random.fold_in(splits[6], 71), 0)
    g_inv = draw_g_inv(jax.random.fold_in(splits[6], 71), 0)
    return dict(feats=feats, top_grad=top_grad, weights=weights, table=table, a_inv=a_inv, g_inv=g_inv)


def to_columns(padded, rows, width):
    taps = [padded[:, ky:ky + rows, kx:kx + width] for ky in range(3) for kx in range(3)]
    joined = jnp.concatenate(taps, axis=-1)
    return joined.reshape(joined.shape[0], rows * width, joined.shape[-1])

def back_columns(padded, rows, width):
    taps = [padded[:, 2 - ky:2 - ky + rows, 2 - kx:2 - kx + width] for ky in range(3) for kx in range(3)]
    joined = jnp.concatenate(taps, axis=-1)
    return joined.reshape(joined.shape[0], rows * width, joined.shape[-1])

def silu_slope(value):
    sig = jax.nn.sigmoid(value)
    return sig * (1.0 + value * (1.0 - sig))

def reference(feats, top_grad, weights, table, a_inv, g_inv):
    chans = feats.shape[-1]
    npos = N_DP * H * W
    grad_in = top_grad.reshape(N_DP, H * W, chans)
    grads = [None] * L
    gfacs = [None] * L
    afacs = [None] * L
    for step_idx in range(L):
        lay = L - 1 - step_idx
        padded = jnp.pad(feats[lay], ((0, 0), (1, 1), (1, 1), (0, 0)))
        cols = to_columns(padded, H, W)
        pre = jnp.einsum('npk,kc->npc', cols.astype(jnp.float32), weights[lay].astype(jnp.float32))
        dpre = (grad_in.astype(jnp.float32) * silu_slope(pre)).astype(jnp.bfloat16)
        grads[lay] = jnp.einsum('npk,npc->kc', cols.astype(jnp.float32), dpre.astype(jnp.float32)) / jnp.sqrt(jnp.float32(npos))
        gfacs[lay] = jnp.einsum('npc,npd->cd', dpre.astype(jnp.float32), dpre.astype(jnp.float32)) / npos
        persample = jnp.einsum('npk,npq->nkq', cols.astype(jnp.float32), cols.astype(jnp.float32)).astype(jnp.bfloat16)
        afacs[lay] = lax.optimization_barrier(jnp.sum(persample.astype(jnp.float32), axis=0)) / npos
        dimg = jnp.pad(dpre.reshape(N_DP, H, W, chans), ((0, 0), (1, 1), (1, 1), (0, 0)))
        bcols = back_columns(dimg, H, W)
        flipped = jnp.transpose(weights[lay].reshape(9, chans, chans), (0, 2, 1)).reshape(9 * chans, chans)
        grad_in = jnp.einsum('npk,kc->npc', bcols.astype(jnp.float32), flipped.astype(jnp.float32)).astype(jnp.bfloat16)
    in_grad = grad_in.reshape(N_DP, H, W, chans)
    a_stat = jnp.zeros((N_OWNER, 9 * chans, 9 * chans), jnp.float32).at[table].set(jnp.stack(afacs))
    g_stat = jnp.zeros((N_OWNER, chans, chans), jnp.float32).at[table].set(jnp.stack(gfacs))
    panels = []
    for lay in range(L):
        mixed = jnp.dot(grads[lay], g_inv[table[lay]], precision=lax.Precision.HIGHEST)
        panels.append(jnp.dot(a_inv[table[lay]].astype(jnp.float32), mixed, precision=lax.Precision.HIGHEST).astype(jnp.bfloat16))
    return (jnp.stack(panels), a_stat, g_stat, in_grad)
```

```python
import jax
import jax.numpy as jnp
from jax import lax
from jax.sharding import PartitionSpec as P

Y = 4
Z_HI = 4


def halo(cells, width, dim):
    count = lax.axis_size("owner")
    head = lax.slice_in_dim(cells, 0, width, axis=dim)
    tail = lax.slice_in_dim(cells, cells.shape[dim] - width, cells.shape[dim], axis=dim)
    above = lax.ppermute(tail, "owner", [(i, i + 1) for i in range(count - 1)])
    below = lax.ppermute(head, "owner", [(i + 1, i) for i in range(count - 1)])
    return jnp.concatenate([above, cells, below], axis=dim)


def along_y(x, shift):
    pairs = [(z * Y + y, z * Y + (y + shift) % Y) for z in range(Z_HI) for y in range(Y)]
    return lax.ppermute(x, "owner", pairs)


def along_z(x, shift):
    pairs = [(z * Y + y, (z + shift) % Z_HI * Y + y) for z in range(Z_HI) for y in range(Y)]
    return lax.ppermute(x, "owner", pairs)


def to_columns(padded, rows, width):
    taps = [padded[ky : ky + rows, kx : kx + width] for ky in range(3) for kx in range(3)]
    joined = jnp.concatenate(taps, axis=-1)
    return joined.reshape(rows * width, joined.shape[-1])


def back_columns(padded, rows, width):
    taps = [
        padded[2 - ky : 2 - ky + rows, 2 - kx : 2 - kx + width]
        for ky in range(3)
        for kx in range(3)
    ]
    joined = jnp.concatenate(taps, axis=-1)
    return joined.reshape(rows * width, joined.shape[-1])


def silu_slope(value):
    sig = jax.nn.sigmoid(value)
    return sig * (1.0 + value * (1.0 - sig))


def inner_rows(left, right):
    return lax.dot_general(
        left, right, (((0,), (0,)), ((), ())), preferred_element_type=jnp.float32
    )


def block_classes():
    found = {}
    pairs = []
    where = {}
    for a in range(9):
        for b in range(9):
            first, second, flip = a, b, False
            dy, dx = b // 3 - a // 3, b % 3 - a % 3
            if dy < 0 or (dy == 0 and dx < 0):
                first, second, flip = b, a, True
                dy, dx = -dy, -dx
            key = (dy, dx, first // 3 if dy == 0 else -1, first % 3 if dx == 0 else -1)
            if key not in found:
                found[key] = len(pairs)
                pairs.append((first, second))
            where[a, b] = (found[key], flip)
    return pairs, where


PAIRS, WHERE = block_classes()
NG = len(PAIRS)
NBLOCKS = 40


def shards(feats, top_grad, weights, table, a_inv, g_inv):
    num_layers, _, rows_dev, width, chans = feats.shape
    owners = lax.axis_size("owner")
    samples = lax.axis_size("dp")
    owner_id = lax.axis_index("owner")
    dp_id = lax.axis_index("dp")
    y_id = owner_id % Y
    z_id = owner_id // Y
    npos = samples * rows_dev * owners * width
    patch = 9 * chans
    strips = halo(feats[:, 0], 1, 1)
    strips = jnp.pad(strips, ((0, 0), (0, 0), (1, 1), (0, 0)))
    layer_strips = [lax.dynamic_index_in_dim(strips, y_id, 0, keepdims=False)]
    for s in range(1, Y):
        out = lax.dynamic_index_in_dim(strips, (y_id + s) % Y, 0, keepdims=False)
        layer_strips.append(along_y(out, s))

    flipped = jnp.transpose(weights.reshape(num_layers, 9, chans, chans), (0, 1, 3, 2)).reshape(
        num_layers, patch, chans
    )
    grad_in = top_grad[0].reshape(rows_dev * width, chans)
    dpres = [None] * num_layers
    for step_idx in range(num_layers):
        layer = num_layers - 1 - step_idx
        cols = to_columns(strips[layer], rows_dev, width)
        pre = jnp.dot(cols, weights[layer], preferred_element_type=jnp.float32)
        dpre = (grad_in.astype(jnp.float32) * silu_slope(pre)).astype(jnp.bfloat16)
        dpres[layer] = dpre
        rimmed = halo(dpre.reshape(rows_dev, width, chans), 1, 0)
        rimmed = jnp.pad(rimmed, ((0, 0), (1, 1), (0, 0)))
        grad_in = jnp.dot(
            back_columns(rimmed, rows_dev, width),
            flipped[layer],
            preferred_element_type=jnp.float32,
        ).astype(jnp.bfloat16)
    in_grad = grad_in.reshape(1, rows_dev, width, chans)

    all_dpre = jnp.stack(dpres)
    layer_dpre = [lax.dynamic_index_in_dim(all_dpre, y_id, 0, keepdims=False)]
    for s in range(1, Y):
        out = lax.dynamic_index_in_dim(all_dpre, (y_id + s) % Y, 0, keepdims=False)
        layer_dpre.append(along_y(out, s))

    big_cols = jnp.concatenate([to_columns(s, rows_dev, width) for s in layer_strips], axis=0)
    big_dpre = jnp.concatenate(layer_dpre, axis=0)
    gram = inner_rows(big_cols, big_cols).astype(jnp.bfloat16)
    grad = inner_rows(big_cols, big_dpre).astype(jnp.bfloat16)
    gfac = inner_rows(big_dpre, big_dpre).astype(jnp.bfloat16)
    blocks = [
        gram[a * chans : (a + 1) * chans, b * chans : (b + 1) * chans] for a, b in PAIRS
    ]
    pad = jnp.zeros(((NBLOCKS - NG - 10) * chans, chans), jnp.bfloat16)
    parts = jnp.concatenate(blocks + [grad, gfac, pad], axis=0)

    piece = lax.psum_scatter(parts, "dp", scatter_dimension=0, tiled=True)

    held = jnp.stack([piece] + [along_y(piece, s) for s in range(1, Y)])
    layer_ids = jnp.arange(num_layers, dtype=jnp.int32)

    def pick(z):
        owned = table == (z % Z_HI) * Y + y_id
        lay = jnp.sum(jnp.where(owned, layer_ids, 0))
        return lax.dynamic_index_in_dim(held, (y_id - lay) % Y, 0, keepdims=False)

    total = pick(z_id).astype(jnp.float32)
    for t in range(1, Z_HI):
        total = total + along_z(pick(z_id + t), t).astype(jnp.float32)
    summed = lax.all_gather(total.astype(jnp.bfloat16), "dp", axis=0, tiled=True)

    summed = summed.reshape(NBLOCKS, chans, chans)
    have = jnp.any(table == owner_id).astype(jnp.float32)
    turned = jnp.swapaxes(summed[:NG], 1, 2)
    factor = jnp.concatenate(
        [
            jnp.concatenate(
                [turned[WHERE[a, b][0]] if WHERE[a, b][1] else summed[WHERE[a, b][0]] for b in range(9)],
                axis=1,
            )
            for a in range(9)
        ],
        axis=0,
    )
    rows_out = patch // samples
    a_rows = lax.dynamic_slice_in_dim(factor, dp_id * rows_out, rows_out, 0).astype(jnp.float32)
    a_out = (a_rows * (have / npos))[None]
    g_out = (summed[NG + 9].astype(jnp.float32) * (have / npos))[None]
    grad_sum = summed[NG : NG + 9].reshape(patch, chans).astype(jnp.float32)
    grad_scaled = grad_sum / jnp.sqrt(jnp.float32(npos))
    mixed = jnp.dot(grad_scaled, g_inv[0], precision=lax.Precision.HIGHEST)
    panel = jnp.dot(a_inv[0].astype(jnp.float32), mixed, precision=lax.Precision.HIGHEST)
    panels = lax.all_gather(panel.astype(jnp.bfloat16), "owner", axis=0)
    step_out = panels[table]
    return (step_out, a_out, g_out, in_grad)


def solution(mesh):
    placed = (
        P(None, "dp", "owner", None, None),
        P("dp", "owner", None, None),
        P(),
        P(),
        P("owner", "dp", None),
        P("owner", None, None),
    )
    return jax.shard_map(
        shards,
        mesh=mesh,
        in_specs=placed,
        out_specs=(
            P(None, "dp", None),
            P("owner", "dp", None),
            P("owner", None, None),
            P("dp", "owner", None, None),
        ),
        check_vma=False,
    )
```

```python
import jax
import jax.numpy as jnp
from jax import lax
from jax.sharding import Mesh, PartitionSpec as P

X, ZL, CORE, ZH, Y = 4, 4, 2, 4, 4
OWNER = ("zh", "y")
DP = ("x", "zl", "core")


def shifted(x, shift, cyclic):
    count = ZH * Y
    pairs = [(i, (i + shift) % count) for i in range(count)]
    if not cyclic:
        pairs = [(a, b) for a, b in pairs if b - a == shift]
    return lax.ppermute(x, OWNER, pairs)


def exchange(x, axis):
    return lax.all_to_all(x, axis, split_axis=0, concat_axis=0, tiled=True)


def spread(x, axis):
    count = lax.axis_size(axis)
    return exchange(jnp.broadcast_to(x[None], (count,) + x.shape), axis)


def scatter_sum(x, axis):
    count = lax.axis_size(axis)
    got = exchange(x.reshape((count, x.shape[0] // count) + x.shape[1:]), axis)
    return jnp.sum(got.astype(jnp.float32), axis=0).astype(jnp.bfloat16)


def windows(rows):
    rows = jnp.pad(rows, ((0, 0), (1, 1), (0, 0)))
    return jnp.stack([rows[i : i + 3] for i in range(rows.shape[0] - 2)])


def cut_windows(rows, whole):
    first, second = rows[:3], rows[1:]
    first = jnp.where(whole, first, first * jnp.array([1, 1, 0], rows.dtype)[:, None, None])
    second = jnp.where(whole, second, second * jnp.array([0, 1, 1], rows.dtype)[:, None, None])
    return jnp.pad(jnp.stack([first, second]), ((0, 0), (0, 0), (1, 1), (0, 0)))


def to_columns(win):
    width = win.shape[2] - 2
    taps = [win[:, ky, kx : kx + width] for ky in range(3) for kx in range(3)]
    return jnp.concatenate(taps, axis=-1).reshape(-1, 9 * win.shape[-1])


def back_columns(win):
    width = win.shape[2] - 2
    taps = [win[:, 2 - ky, 2 - kx : 2 - kx + width] for ky in range(3) for kx in range(3)]
    return jnp.concatenate(taps, axis=-1).reshape(-1, 9 * win.shape[-1])


def silu_slope(value):
    sig = jax.nn.sigmoid(value)
    return sig * (1.0 + value * (1.0 - sig))


def inner_rows(left, right):
    return lax.dot_general(
        left, right, (((0,), (0,)), ((), ())), preferred_element_type=jnp.float32
    )


def block_classes():
    found = {}
    pairs = []
    where = {}
    for a in range(9):
        for b in range(9):
            first, second, flip = a, b, False
            dy, dx = b // 3 - a // 3, b % 3 - a % 3
            if dy < 0 or (dy == 0 and dx < 0):
                first, second, flip = b, a, True
                dy, dx = -dy, -dx
            key = (dy, dx, first // 3 if dy == 0 else -1, first % 3 if dx == 0 else -1)
            if key not in found:
                found[key] = len(pairs)
                pairs.append((first, second))
            where[a, b] = (found[key], flip)
    return pairs, where


PAIRS, WHERE = block_classes()
NG = len(PAIRS)
NBLOCKS = 40


def shards(feats, top_grad, weights, table, a_inv, g_inv):
    num_layers, _, rows_dev, width, chans = feats.shape
    owners = lax.axis_size(OWNER)
    samples = lax.axis_size(DP)
    owner_id = lax.axis_index(OWNER)
    dp_id = lax.axis_index(DP)
    y_id = lax.axis_index("y")
    z_id = lax.axis_index("zh")
    npos = samples * rows_dev * owners * width
    patch = 9 * chans
    inner = owner_id < owners - 1
    f = feats[:, 0]
    top = top_grad[0]

    above = shifted(jnp.concatenate([f[3], f[2, 1:], f[0, 1:], top[1:]]), 1, False)
    below = shifted(jnp.concatenate([f[3], f[2, :1], f[0, :1], top[:1], f[1]]), -1, True)
    below1 = below[5:]
    below = jnp.where(inner, below[:5], jnp.zeros_like(below[:5]))
    wide3 = jnp.concatenate([above[:2], f[3], below[:2]])
    strips = [
        jnp.concatenate([above[3:4], f[0], below[3:4]]),
        jnp.concatenate([f[1], below1]),
        jnp.concatenate([above[2:3], f[2], below[2:3]]),
        wide3[1:5],
    ]
    layer_strips = exchange(jnp.stack(strips), "y")

    flipped = jnp.transpose(weights.reshape(num_layers, 9, chans, chans), (0, 1, 3, 2)).reshape(
        num_layers, patch, chans
    )

    def slope(layer, win):
        pre = jnp.dot(to_columns(win), weights[layer], preferred_element_type=jnp.float32)
        return silu_slope(pre)

    def times(grad_in, slopes):
        return (grad_in.reshape(slopes.shape).astype(jnp.float32) * slopes).astype(jnp.bfloat16)

    def back(layer, win):
        return jnp.dot(
            back_columns(win), flipped[layer], preferred_element_type=jnp.float32
        ).astype(jnp.bfloat16)

    image = (rows_dev, width, chans)
    top_wide = jnp.concatenate([above[4:5], top, below[4:5]])
    dpre3 = times(top_wide, slope(3, windows(wide3))).reshape((rows_dev + 2, width, chans))
    dpre2 = times(back(3, windows(dpre3)), slope(2, windows(strips[2]))).reshape(image)
    after = shifted(dpre2, -1, True)
    dy1 = back(2, cut_windows(jnp.concatenate([dpre2, after]), inner))
    dpre1 = times(dy1, slope(1, cut_windows(strips[1], inner))).reshape(image)
    before = shifted(dpre1, 1, True)
    edge_top = jnp.where(owner_id > 0, before[:1], jnp.zeros_like(before[:1]))
    edge_end = jnp.where(inner, dpre1[1:], jnp.zeros_like(dpre1[1:]))
    dy0 = back(1, windows(jnp.concatenate([edge_top, before[1:], dpre1[:1], edge_end])))
    dpre0 = times(dy0, slope(0, windows(strips[0]))).reshape(image)

    layer_dpre = exchange(jnp.stack([dpre0, dpre1, dpre2, dpre3[1:3]]), "y")
    big_dpre = layer_dpre.reshape(-1, chans)
    last_one = (y_id == 1) & (z_id == ZH - 1)
    big_cols = jnp.concatenate(
        [
            to_columns(
                windows(layer_strips[j])
                if j < Y - 1
                else cut_windows(layer_strips[j], jnp.logical_not(last_one))
            )
            for j in range(Y)
        ]
    )
    gram = inner_rows(big_cols, big_cols).astype(jnp.bfloat16)
    grad = inner_rows(big_cols, big_dpre).astype(jnp.bfloat16)
    gfac = inner_rows(big_dpre, big_dpre).astype(jnp.bfloat16)
    blocks = [
        gram[a * chans : (a + 1) * chans, b * chans : (b + 1) * chans] for a, b in PAIRS
    ]
    pad = jnp.zeros(((NBLOCKS - NG - 10) * chans, chans), jnp.bfloat16)
    parts = jnp.concatenate(blocks + [grad, gfac, pad], axis=0)

    piece = scatter_sum(scatter_sum(scatter_sum(parts, "core"), "x"), "zl")
    held = spread(piece, "y")
    layer_ids = jnp.arange(num_layers, dtype=jnp.int32)

    def pick(z):
        lay = jnp.sum(jnp.where(table == z * Y + y_id, layer_ids, 0))
        return lax.dynamic_index_in_dim(held, lay, 0, keepdims=False)

    total = exchange(jnp.stack([pick(z) for z in range(ZH)]), "zh")
    total = jnp.sum(total.astype(jnp.float32), axis=0).astype(jnp.bfloat16)
    summed = spread(spread(spread(total, "zl"), "x"), "core")

    in_grad_win = jnp.concatenate([shifted(dpre0[1:], 1, False), dpre0, shifted(dpre0[:1], -1, False)])
    in_grad = back(0, windows(in_grad_win)).reshape((1,) + image)

    summed = summed.reshape(NBLOCKS, chans, chans)
    have = jnp.any(table == owner_id).astype(jnp.float32)
    turned = jnp.swapaxes(summed[:NG], 1, 2)
    factor = jnp.concatenate(
        [
            jnp.concatenate(
                [turned[WHERE[a, b][0]] if WHERE[a, b][1] else summed[WHERE[a, b][0]] for b in range(9)],
                axis=1,
            )
            for a in range(9)
        ],
        axis=0,
    )
    rows_out = patch // samples
    a_rows = lax.dynamic_slice_in_dim(factor, dp_id * rows_out, rows_out, 0).astype(jnp.float32)
    a_out = (a_rows * (have / npos))[None]
    g_out = (summed[NG + 9].astype(jnp.float32) * (have / npos))[None]
    grad_sum = summed[NG : NG + 9].reshape(patch, chans).astype(jnp.float32)
    grad_scaled = grad_sum / jnp.sqrt(jnp.float32(npos))
    mixed = jnp.dot(grad_scaled, g_inv[0], precision=lax.Precision.HIGHEST)
    panel = jnp.dot(a_inv[0].astype(jnp.float32), mixed, precision=lax.Precision.HIGHEST)
    panels = spread(panel.astype(jnp.bfloat16), OWNER)
    step_out = panels[table]
    return (step_out, a_out, g_out, in_grad)


def solution(mesh):
    fine = Mesh(mesh.devices.reshape(X, ZL, CORE, ZH, Y), DP + OWNER)
    placed = (
        P(None, DP, OWNER, None, None),
        P(DP, OWNER, None, None),
        P(),
        P(),
        P(OWNER, DP, None),
        P(OWNER, None, None),
    )
    return jax.shard_map(
        shards,
        mesh=fine,
        in_specs=placed,
        out_specs=(
            P(None, DP, None),
            P(OWNER, DP, None),
            P(OWNER, None, None),
            P(DP, OWNER, None, None),
        ),
        check_vma=False,
    )
```

```python
import jax
import jax.numpy as jnp
from jax import lax
from jax.experimental import pallas as pl
from jax.experimental.pallas import tpu as pltpu
from jax.sharding import Mesh, PartitionSpec as P

X, ZL, CORE, ZH, Y = 4, 4, 2, 4, 4
OWNER = ("zh", "y")
DP = ("x", "zl", "core")


def shifted(x, shift, cyclic):
    count = ZH * Y
    pairs = [(i, (i + shift) % count) for i in range(count)]
    if not cyclic:
        pairs = [(a, b) for a, b in pairs if b - a == shift]
    return lax.ppermute(x, OWNER, pairs)


def swapped(x, first):
    count = ZH * Y
    pairs = []
    for i in range(0 if first else 1, count, 2):
        pairs += [(i, (i + 1) % count), ((i + 1) % count, i)]
    return lax.ppermute(x, OWNER, pairs)


def both_sides(to_above, to_below):
    even = lax.axis_index(OWNER) % 2 == 0
    one = swapped(jnp.where(even, to_below, to_above), True)
    two = swapped(jnp.where(even, to_above, to_below), False)
    return jnp.where(even, two, one), jnp.where(even, one, two)


def exchange(x, axis):
    return lax.all_to_all(x, axis, split_axis=0, concat_axis=0, tiled=True)


def spread(x, axis):
    count = lax.axis_size(axis)
    return exchange(jnp.broadcast_to(x[None], (count,) + x.shape), axis)


def scatter_sum(x, axis):
    count = lax.axis_size(axis)
    got = exchange(x.reshape((count, x.shape[0] // count) + x.shape[1:]), axis)
    return jnp.sum(got.astype(jnp.float32), axis=0).astype(jnp.bfloat16)


def windows(rows):
    rows = jnp.pad(rows, ((0, 0), (1, 1), (0, 0)))
    return jnp.stack([rows[i : i + 3] for i in range(rows.shape[0] - 2)])


def cut_windows(rows, whole):
    first, second = rows[:3], rows[1:]
    first = jnp.where(whole, first, first * jnp.array([1, 1, 0], rows.dtype)[:, None, None])
    second = jnp.where(whole, second, second * jnp.array([0, 1, 1], rows.dtype)[:, None, None])
    return jnp.pad(jnp.stack([first, second]), ((0, 0), (0, 0), (1, 1), (0, 0)))


def to_columns(win):
    width = win.shape[2] - 2
    taps = [win[:, ky, kx : kx + width] for ky in range(3) for kx in range(3)]
    return jnp.concatenate(taps, axis=-1).reshape(-1, 9 * win.shape[-1])


def back_columns(win):
    width = win.shape[2] - 2
    taps = [win[:, 2 - ky, 2 - kx : 2 - kx + width] for ky in range(3) for kx in range(3)]
    return jnp.concatenate(taps, axis=-1).reshape(-1, 9 * win.shape[-1])


def silu_slope(value):
    sig = jax.nn.sigmoid(value)
    return sig * (1.0 + value * (1.0 - sig))


def inner_rows(left, right):
    return lax.dot_general(
        left, right, (((0,), (0,)), ((), ())), preferred_element_type=jnp.float32
    )


def block_classes():
    found = {}
    pairs = []
    where = {}
    for a in range(9):
        for b in range(9):
            first, second, flip = a, b, False
            dy, dx = b // 3 - a // 3, b % 3 - a % 3
            if dy < 0 or (dy == 0 and dx < 0):
                first, second, flip = b, a, True
                dy, dx = -dy, -dx
            key = (dy, dx, first // 3 if dy == 0 else -1, first % 3 if dx == 0 else -1)
            if key not in found:
                found[key] = len(pairs)
                pairs.append((first, second))
            where[a, b] = (found[key], flip)
    return pairs, where


PAIRS, WHERE = block_classes()
NG = len(PAIRS)


def factor_rows(blocks, first_row, scale, rows):
    chans = blocks.shape[-1]
    index = jnp.array([WHERE[a, b][0] for a in range(9) for b in range(9)], jnp.int32)
    flips = jnp.array([int(WHERE[a, b][1]) for a in range(9) for b in range(9)], jnp.int32)

    def kernel(index_ref, flip_ref, row_ref, scale_ref, blocks_ref, out_ref, band):
        start = row_ref[0]
        tap = lax.div(start, chans)
        for t in range(2):
            a = jnp.minimum(tap + t, 8)
            for b in range(9):
                block = blocks_ref[index_ref[a * 9 + b]].astype(jnp.float32)
                flip = flip_ref[a * 9 + b] != 0
                band[t * chans : (t + 1) * chans, b * chans : (b + 1) * chans] = jnp.where(
                    flip, block.T, block
                )
        inside = start - tap * chans
        base = pl.multiple_of(lax.div(inside, 8) * 8, 8)
        got = band[pl.ds(base, rows + 4), :]
        odd = inside != base
        out_ref[...] = jnp.where(odd, got[4:], got[:rows]) * scale_ref[0]

    smem = pl.BlockSpec(memory_space=pltpu.SMEM)
    vmem = pl.BlockSpec(memory_space=pltpu.VMEM)
    return pl.pallas_call(
        kernel,
        out_shape=jax.ShapeDtypeStruct((rows, 9 * chans), jnp.float32),
        in_specs=[smem, smem, smem, smem, vmem],
        out_specs=vmem,
        scratch_shapes=[pltpu.VMEM((2 * chans, 9 * chans), jnp.float32)],
        compiler_params=pltpu.CompilerParams(vmem_limit_bytes=16 * 2**20),
        cost_estimate=pl.CostEstimate(flops=10**6, bytes_accessed=2 * 10**6, transcendentals=0),
    )(index, flips, first_row.reshape(1), scale.reshape(1), blocks)


def shards(feats, top_grad, weights, table, a_inv, g_inv):
    num_layers, _, rows_dev, width, chans = feats.shape
    owners = lax.axis_size(OWNER)
    samples = lax.axis_size(DP)
    owner_id = lax.axis_index(OWNER)
    dp_id = lax.axis_index(DP)
    y_id = lax.axis_index("y")
    z_id = lax.axis_index("zh")
    npos = samples * rows_dev * owners * width
    patch = 9 * chans
    inner = owner_id < owners - 1
    f = feats[:, 0]
    top = top_grad[0]

    def picked(x):
        source = table[y_id]
        near = lax.dynamic_index_in_dim(lax.all_gather(x, "y"), source % Y, 0, keepdims=False)
        return lax.dynamic_index_in_dim(lax.all_gather(near, "zh"), source // Y, 0, keepdims=False)

    a_mine = picked(a_inv[0])
    g_mine = picked(g_inv[0])

    above, below = both_sides(
        jnp.concatenate([f[3], f[2, :1], f[0, :1], top[:1], f[1]]),
        jnp.concatenate([f[3], f[2, 1:], f[0, 1:], top[1:], f[1]]),
    )
    below1 = below[5:]
    above = jnp.where(owner_id > 0, above[:5], jnp.zeros_like(above[:5]))
    below = jnp.where(inner, below[:5], jnp.zeros_like(below[:5]))
    wide3 = jnp.concatenate([above[:2], f[3], below[:2]])
    strips = [
        jnp.concatenate([above[3:4], f[0], below[3:4]]),
        jnp.concatenate([f[1], below1]),
        jnp.concatenate([above[2:3], f[2], below[2:3]]),
        wide3[1:5],
    ]
    layer_strips = exchange(jnp.stack(strips), "y")

    flipped = jnp.transpose(weights.reshape(num_layers, 9, chans, chans), (0, 1, 3, 2)).reshape(
        num_layers, patch, chans
    )

    def slope(layer, win):
        pre = jnp.dot(to_columns(win), weights[layer], preferred_element_type=jnp.float32)
        return silu_slope(pre)

    def times(grad_in, slopes):
        return (grad_in.reshape(slopes.shape).astype(jnp.float32) * slopes).astype(jnp.bfloat16)

    def back(layer, win):
        return jnp.dot(
            back_columns(win), flipped[layer], preferred_element_type=jnp.float32
        ).astype(jnp.bfloat16)

    image = (rows_dev, width, chans)
    top_wide = jnp.concatenate([above[4:5], top, below[4:5]])
    dpre3 = times(top_wide, slope(3, windows(wide3))).reshape((rows_dev + 2, width, chans))
    dpre2 = times(back(3, windows(dpre3)), slope(2, windows(strips[2]))).reshape(image)
    after = shifted(dpre2, -1, True)
    dy1 = back(2, cut_windows(jnp.concatenate([dpre2, after]), inner))
    dpre1 = times(dy1, slope(1, cut_windows(strips[1], inner))).reshape(image)
    before = shifted(dpre1, 1, True)
    edge_top = jnp.where(owner_id > 0, before[:1], jnp.zeros_like(before[:1]))
    edge_end = jnp.where(inner, dpre1[1:], jnp.zeros_like(dpre1[1:]))
    dy0 = back(1, windows(jnp.concatenate([edge_top, before[1:], dpre1[:1], edge_end])))
    dpre0 = times(dy0, slope(0, windows(strips[0]))).reshape(image)

    layer_dpre = exchange(jnp.stack([dpre0, dpre1, dpre2, dpre3[1:3]]), "y")
    big_dpre = layer_dpre.reshape(-1, chans)
    last_one = (y_id == 1) & (z_id == ZH - 1)
    big_cols = jnp.concatenate(
        [
            to_columns(
                windows(layer_strips[j])
                if j < Y - 1
                else cut_windows(layer_strips[j], jnp.logical_not(last_one))
            )
            for j in range(Y)
        ]
    )
    gram = inner_rows(big_cols, big_cols).astype(jnp.bfloat16)
    grad = inner_rows(big_cols, big_dpre).astype(jnp.bfloat16)
    gfac = inner_rows(big_dpre, big_dpre).astype(jnp.bfloat16)
    blocks = [
        gram[a * chans : (a + 1) * chans, b * chans : (b + 1) * chans] for a, b in PAIRS
    ]
    pad = jnp.zeros((chans, chans), jnp.bfloat16)
    parts = jnp.concatenate(
        [
            jnp.concatenate(blocks + [gfac]).reshape(samples, -1, chans),
            jnp.concatenate([grad, pad]).reshape(samples, -1, chans),
        ],
        axis=1,
    ).reshape(-1, chans)
    cut = (NG + 1) * chans // samples

    piece = scatter_sum(scatter_sum(scatter_sum(parts, "core"), "x"), "zl")
    held = spread(piece[:cut], "y")
    layer_ids = jnp.arange(num_layers, dtype=jnp.int32)

    def pick(z):
        lay = jnp.sum(jnp.where(table == z * Y + y_id, layer_ids, 0))
        return lax.dynamic_index_in_dim(held, lay, 0, keepdims=False)

    sent = jnp.stack([jnp.concatenate([pick(z), piece[cut:]]) for z in range(ZH)])
    sent, dpre0, a_mine, g_mine = lax.optimization_barrier((sent, dpre0, a_mine, g_mine))
    total = exchange(sent, "zh")
    total = jnp.sum(total.astype(jnp.float32), axis=0).astype(jnp.bfloat16)

    up, down = both_sides(dpre0[:1], dpre0[1:])
    up = jnp.where(owner_id > 0, up, jnp.zeros_like(up))
    down = jnp.where(inner, down, jnp.zeros_like(down))
    in_grad = back(0, windows(jnp.concatenate([up, dpre0, down]))).reshape((1,) + image)

    summed = spread(spread(spread(total, "zl"), "x"), "core").reshape(samples, -1, chans)
    grad_sum = summed[:, cut:].reshape(-1, chans)[:patch].astype(jnp.float32)
    grad_scaled = grad_sum / jnp.sqrt(jnp.float32(npos))
    mixed = jnp.dot(grad_scaled, g_mine, precision=lax.Precision.HIGHEST)
    panel = jnp.dot(a_mine.astype(jnp.float32), mixed, precision=lax.Precision.HIGHEST)
    step_out = spread(panel.astype(jnp.bfloat16), "y")

    stats = summed[:, :cut].reshape(NG + 1, chans, chans)
    have = jnp.any(table == owner_id).astype(jnp.float32)
    scale = have / npos
    rows_out = patch // samples
    a_out = factor_rows(stats, dp_id * rows_out, scale, rows_out)[None]
    g_out = (stats[NG].astype(jnp.float32) * scale)[None]
    return (step_out, a_out, g_out, in_grad)


def solution(mesh):
    fine = Mesh(mesh.devices.reshape(X, ZL, CORE, ZH, Y), DP + OWNER)
    placed = (
        P(None, DP, OWNER, None, None),
        P(DP, OWNER, None, None),
        P(),
        P(),
        P(OWNER, DP, None),
        P(OWNER, None, None),
    )
    return jax.shard_map(
        shards,
        mesh=fine,
        in_specs=placed,
        out_specs=(
            P(None, DP, None),
            P(OWNER, DP, None),
            P(OWNER, None, None),
            P(DP, OWNER, None, None),
        ),
        check_vma=False,
    )
```

```python
import jax
import jax.numpy as jnp
from jax import lax
from jax.experimental import pallas as pl
from jax.experimental.pallas import tpu as pltpu
from jax.sharding import Mesh, PartitionSpec as P

X, ZL, CORE, ZH, Y = 4, 4, 2, 4, 4
OWNER = ("zh", "y")
DP = ("x", "zl", "core")


def shifted(x, shift, cyclic):
    count = ZH * Y
    pairs = [(i, (i + shift) % count) for i in range(count)]
    if not cyclic:
        pairs = [(a, b) for a, b in pairs if b - a == shift]
    return lax.ppermute(x, OWNER, pairs)


def exchange(x, axis):
    return lax.all_to_all(x, axis, split_axis=0, concat_axis=0, tiled=True)


def spread(x, axis):
    count = lax.axis_size(axis)
    return exchange(jnp.broadcast_to(x[None], (count,) + x.shape), axis)


def scatter_sum(x, axis):
    count = lax.axis_size(axis)
    got = exchange(x.reshape((count, x.shape[0] // count) + x.shape[1:]), axis)
    return jnp.sum(got.astype(jnp.float32), axis=0).astype(jnp.bfloat16)


def windows(rows):
    rows = jnp.pad(rows, ((0, 0), (1, 1), (0, 0)))
    return jnp.stack([rows[i : i + 3] for i in range(rows.shape[0] - 2)])


def cut_windows(rows, whole):
    first, second = rows[:3], rows[1:]
    first = jnp.where(whole, first, first * jnp.array([1, 1, 0], rows.dtype)[:, None, None])
    second = jnp.where(whole, second, second * jnp.array([0, 1, 1], rows.dtype)[:, None, None])
    return jnp.pad(jnp.stack([first, second]), ((0, 0), (0, 0), (1, 1), (0, 0)))


def to_columns(win):
    width = win.shape[2] - 2
    taps = [win[:, ky, kx : kx + width] for ky in range(3) for kx in range(3)]
    return jnp.concatenate(taps, axis=-1).reshape(-1, 9 * win.shape[-1])


def back_columns(win):
    width = win.shape[2] - 2
    taps = [win[:, 2 - ky, 2 - kx : 2 - kx + width] for ky in range(3) for kx in range(3)]
    return jnp.concatenate(taps, axis=-1).reshape(-1, 9 * win.shape[-1])


def silu_slope(value):
    sig = jax.nn.sigmoid(value)
    return sig * (1.0 + value * (1.0 - sig))


def inner_rows(left, right):
    return lax.dot_general(
        left, right, (((0,), (0,)), ((), ())), preferred_element_type=jnp.float32
    )


def block_classes():
    found = {}
    pairs = []
    where = {}
    for a in range(9):
        for b in range(9):
            first, second, flip = a, b, False
            dy, dx = b // 3 - a // 3, b % 3 - a % 3
            if dy < 0 or (dy == 0 and dx < 0):
                first, second, flip = b, a, True
                dy, dx = -dy, -dx
            key = (dy, dx, first // 3 if dy == 0 else -1, first % 3 if dx == 0 else -1)
            if key not in found:
                found[key] = len(pairs)
                pairs.append((first, second))
            where[a, b] = (found[key], flip)
    return pairs, where


PAIRS, WHERE = block_classes()
NG = len(PAIRS)
NBLOCKS = 40


def factor_rows(blocks, first_row, scale, rows):
    chans = blocks.shape[-1]
    index = jnp.array([WHERE[a, b][0] for a in range(9) for b in range(9)], jnp.int32)
    flips = jnp.array([int(WHERE[a, b][1]) for a in range(9) for b in range(9)], jnp.int32)

    def kernel(index_ref, flip_ref, row_ref, scale_ref, blocks_ref, out_ref, band):
        start = row_ref[0]
        tap = lax.div(start, chans)
        for t in range(2):
            a = jnp.minimum(tap + t, 8)
            for b in range(9):
                block = blocks_ref[index_ref[a * 9 + b]].astype(jnp.float32)
                flip = flip_ref[a * 9 + b] != 0
                band[t * chans : (t + 1) * chans, b * chans : (b + 1) * chans] = jnp.where(
                    flip, block.T, block
                )
        inside = start - tap * chans
        base = pl.multiple_of(lax.div(inside, 8) * 8, 8)
        got = band[pl.ds(base, rows + 4), :]
        odd = inside != base
        out_ref[...] = jnp.where(odd, got[4:], got[:rows]) * scale_ref[0]

    smem = pl.BlockSpec(memory_space=pltpu.SMEM)
    vmem = pl.BlockSpec(memory_space=pltpu.VMEM)
    return pl.pallas_call(
        kernel,
        out_shape=jax.ShapeDtypeStruct((rows, 9 * chans), jnp.float32),
        in_specs=[smem, smem, smem, smem, vmem],
        out_specs=vmem,
        scratch_shapes=[pltpu.VMEM((2 * chans, 9 * chans), jnp.float32)],
        compiler_params=pltpu.CompilerParams(vmem_limit_bytes=16 * 2**20),
        cost_estimate=pl.CostEstimate(flops=10**6, bytes_accessed=2 * 10**6, transcendentals=0),
    )(index, flips, first_row.reshape(1), scale.reshape(1), blocks)


def shards(feats, top_grad, weights, table, a_inv, g_inv):
    num_layers, _, rows_dev, width, chans = feats.shape
    owners = lax.axis_size(OWNER)
    samples = lax.axis_size(DP)
    owner_id = lax.axis_index(OWNER)
    dp_id = lax.axis_index(DP)
    y_id = lax.axis_index("y")
    z_id = lax.axis_index("zh")
    npos = samples * rows_dev * owners * width
    patch = 9 * chans
    inner = owner_id < owners - 1
    f = feats[:, 0]
    top = top_grad[0]

    above = shifted(jnp.concatenate([f[3], f[2, 1:], f[0, 1:], top[1:]]), 1, False)
    below = shifted(jnp.concatenate([f[3], f[2, :1], f[0, :1], top[:1], f[1]]), -1, True)
    below1 = below[5:]
    below = jnp.where(inner, below[:5], jnp.zeros_like(below[:5]))
    wide3 = jnp.concatenate([above[:2], f[3], below[:2]])
    strips = [
        jnp.concatenate([above[3:4], f[0], below[3:4]]),
        jnp.concatenate([f[1], below1]),
        jnp.concatenate([above[2:3], f[2], below[2:3]]),
        wide3[1:5],
    ]
    layer_strips = exchange(jnp.stack(strips), "y")

    flipped = jnp.transpose(weights.reshape(num_layers, 9, chans, chans), (0, 1, 3, 2)).reshape(
        num_layers, patch, chans
    )

    def slope(layer, win):
        pre = jnp.dot(to_columns(win), weights[layer], preferred_element_type=jnp.float32)
        return silu_slope(pre)

    def times(grad_in, slopes):
        return (grad_in.reshape(slopes.shape).astype(jnp.float32) * slopes).astype(jnp.bfloat16)

    def back(layer, win):
        return jnp.dot(
            back_columns(win), flipped[layer], preferred_element_type=jnp.float32
        ).astype(jnp.bfloat16)

    image = (rows_dev, width, chans)
    top_wide = jnp.concatenate([above[4:5], top, below[4:5]])
    dpre3 = times(top_wide, slope(3, windows(wide3))).reshape((rows_dev + 2, width, chans))
    dpre2 = times(back(3, windows(dpre3)), slope(2, windows(strips[2]))).reshape(image)
    after = shifted(dpre2, -1, True)
    dy1 = back(2, cut_windows(jnp.concatenate([dpre2, after]), inner))
    dpre1 = times(dy1, slope(1, cut_windows(strips[1], inner))).reshape(image)
    before = shifted(dpre1, 1, True)
    edge_top = jnp.where(owner_id > 0, before[:1], jnp.zeros_like(before[:1]))
    edge_end = jnp.where(inner, dpre1[1:], jnp.zeros_like(dpre1[1:]))
    dy0 = back(1, windows(jnp.concatenate([edge_top, before[1:], dpre1[:1], edge_end])))
    dpre0 = times(dy0, slope(0, windows(strips[0]))).reshape(image)

    layer_dpre = exchange(jnp.stack([dpre0, dpre1, dpre2, dpre3[1:3]]), "y")
    big_dpre = layer_dpre.reshape(-1, chans)
    last_one = (y_id == 1) & (z_id == ZH - 1)
    big_cols = jnp.concatenate(
        [
            to_columns(
                windows(layer_strips[j])
                if j < Y - 1
                else cut_windows(layer_strips[j], jnp.logical_not(last_one))
            )
            for j in range(Y)
        ]
    )
    gram = inner_rows(big_cols, big_cols).astype(jnp.bfloat16)
    grad = inner_rows(big_cols, big_dpre).astype(jnp.bfloat16)
    gfac = inner_rows(big_dpre, big_dpre).astype(jnp.bfloat16)
    blocks = [
        gram[a * chans : (a + 1) * chans, b * chans : (b + 1) * chans] for a, b in PAIRS
    ]
    pad = jnp.zeros(((NBLOCKS - NG - 10) * chans, chans), jnp.bfloat16)
    parts = jnp.concatenate(blocks + [grad, gfac, pad], axis=0)

    piece = scatter_sum(scatter_sum(parts, "core"), ("x", "zl"))
    held = spread(piece, "y")
    layer_ids = jnp.arange(num_layers, dtype=jnp.int32)

    def pick(z):
        lay = jnp.sum(jnp.where(table == z * Y + y_id, layer_ids, 0))
        return lax.dynamic_index_in_dim(held, lay, 0, keepdims=False)

    total = exchange(jnp.stack([pick(z) for z in range(ZH)]), "zh")
    total = jnp.sum(total.astype(jnp.float32), axis=0).astype(jnp.bfloat16)
    summed = spread(spread(spread(total, "zl"), "x"), "core")

    in_grad_win = jnp.concatenate([shifted(dpre0[1:], 1, False), dpre0, shifted(dpre0[:1], -1, False)])
    in_grad = back(0, windows(in_grad_win)).reshape((1,) + image)

    summed = summed.reshape(NBLOCKS, chans, chans)
    have = jnp.any(table == owner_id).astype(jnp.float32)
    scale = have / npos
    rows_out = patch // samples
    a_out = factor_rows(summed, dp_id * rows_out, scale, rows_out)[None]
    g_out = (summed[NG + 9].astype(jnp.float32) * scale)[None]
    grad_sum = summed[NG : NG + 9].reshape(patch, chans).astype(jnp.float32)
    grad_scaled = grad_sum / jnp.sqrt(jnp.float32(npos))
    mixed = jnp.dot(grad_scaled, g_inv[0], precision=lax.Precision.HIGHEST)
    panel = jnp.dot(a_inv[0].astype(jnp.float32), mixed, precision=lax.Precision.HIGHEST)
    panels = spread(panel.astype(jnp.bfloat16), OWNER)
    step_out = panels[table]
    return (step_out, a_out, g_out, in_grad)


def solution(mesh):
    fine = Mesh(mesh.devices.reshape(X, ZL, CORE, ZH, Y), DP + OWNER)
    placed = (
        P(None, DP, OWNER, None, None),
        P(DP, OWNER, None, None),
        P(),
        P(),
        P(OWNER, DP, None),
        P(OWNER, None, None),
    )
    return jax.shard_map(
        shards,
        mesh=fine,
        in_specs=placed,
        out_specs=(
            P(None, DP, None),
            P(OWNER, DP, None),
            P(OWNER, None, None),
            P(DP, OWNER, None, None),
        ),
        check_vma=False,
    )
```

```python
import jax
import jax.numpy as jnp
from jax import lax
from jax.experimental import pallas as pl
from jax.experimental.pallas import tpu as pltpu
from jax.sharding import Mesh, PartitionSpec as P

X, ZL, CORE, ZH, Y = 4, 4, 2, 4, 4
OWNER = ("zh", "y")
DP = ("x", "zl", "core")


def shifted(x, shift, cyclic):
    count = ZH * Y
    pairs = [(i, (i + shift) % count) for i in range(count)]
    if not cyclic:
        pairs = [(a, b) for a, b in pairs if b - a == shift]
    return lax.ppermute(x, OWNER, pairs)


def exchange(x, axis):
    return lax.all_to_all(x, axis, split_axis=0, concat_axis=0, tiled=True)


def spread(x, axis):
    count = lax.axis_size(axis)
    return exchange(jnp.broadcast_to(x[None], (count,) + x.shape), axis)


def scatter_sum(x, axis):
    count = lax.axis_size(axis)
    got = exchange(x.reshape((count, x.shape[0] // count) + x.shape[1:]), axis)
    return jnp.sum(got.astype(jnp.float32), axis=0).astype(jnp.bfloat16)


def windows(rows):
    rows = jnp.pad(rows, ((0, 0), (1, 1), (0, 0)))
    return jnp.stack([rows[i : i + 3] for i in range(rows.shape[0] - 2)])


def cut_windows(rows, whole):
    first, second = rows[:3], rows[1:]
    first = jnp.where(whole, first, first * jnp.array([1, 1, 0], rows.dtype)[:, None, None])
    second = jnp.where(whole, second, second * jnp.array([0, 1, 1], rows.dtype)[:, None, None])
    return jnp.pad(jnp.stack([first, second]), ((0, 0), (0, 0), (1, 1), (0, 0)))


def to_columns(win):
    width = win.shape[2] - 2
    taps = [win[:, ky, kx : kx + width] for ky in range(3) for kx in range(3)]
    return jnp.concatenate(taps, axis=-1).reshape(-1, 9 * win.shape[-1])


def back_columns(win):
    width = win.shape[2] - 2
    taps = [win[:, 2 - ky, 2 - kx : 2 - kx + width] for ky in range(3) for kx in range(3)]
    return jnp.concatenate(taps, axis=-1).reshape(-1, 9 * win.shape[-1])


def silu_slope(value):
    sig = jax.nn.sigmoid(value)
    return sig * (1.0 + value * (1.0 - sig))


def inner_rows(left, right):
    return lax.dot_general(
        left, right, (((0,), (0,)), ((), ())), preferred_element_type=jnp.float32
    )


def block_classes():
    found = {}
    pairs = []
    where = {}
    for a in range(9):
        for b in range(9):
            first, second, flip = a, b, False
            dy, dx = b // 3 - a // 3, b % 3 - a % 3
            if dy < 0 or (dy == 0 and dx < 0):
                first, second, flip = b, a, True
                dy, dx = -dy, -dx
            key = (dy, dx, first // 3 if dy == 0 else -1, first % 3 if dx == 0 else -1)
            if key not in found:
                found[key] = len(pairs)
                pairs.append((first, second))
            where[a, b] = (found[key], flip)
    return pairs, where


PAIRS, WHERE = block_classes()
NG = len(PAIRS)


def factor_rows(blocks, first_row, scale, rows):
    chans = blocks.shape[-1]
    index = jnp.array([WHERE[a, b][0] for a in range(9) for b in range(9)], jnp.int32)
    flips = jnp.array([int(WHERE[a, b][1]) for a in range(9) for b in range(9)], jnp.int32)

    def kernel(index_ref, flip_ref, row_ref, scale_ref, blocks_ref, out_ref, band):
        start = row_ref[0]
        tap = lax.div(start, chans)
        for t in range(2):
            a = jnp.minimum(tap + t, 8)
            for b in range(9):
                block = blocks_ref[index_ref[a * 9 + b]].astype(jnp.float32)
                flip = flip_ref[a * 9 + b] != 0
                band[t * chans : (t + 1) * chans, b * chans : (b + 1) * chans] = jnp.where(
                    flip, block.T, block
                )
        inside = start - tap * chans
        base = pl.multiple_of(lax.div(inside, 8) * 8, 8)
        got = band[pl.ds(base, rows + 4), :]
        odd = inside != base
        out_ref[...] = jnp.where(odd, got[4:], got[:rows]) * scale_ref[0]

    smem = pl.BlockSpec(memory_space=pltpu.SMEM)
    vmem = pl.BlockSpec(memory_space=pltpu.VMEM)
    return pl.pallas_call(
        kernel,
        out_shape=jax.ShapeDtypeStruct((rows, 9 * chans), jnp.float32),
        in_specs=[smem, smem, smem, smem, vmem],
        out_specs=vmem,
        scratch_shapes=[pltpu.VMEM((2 * chans, 9 * chans), jnp.float32)],
        compiler_params=pltpu.CompilerParams(vmem_limit_bytes=16 * 2**20),
        cost_estimate=pl.CostEstimate(flops=10**6, bytes_accessed=2 * 10**6, transcendentals=0),
    )(index, flips, first_row.reshape(1), scale.reshape(1), blocks)


def shards(feats, top_grad, weights, table, a_inv, g_inv):
    num_layers, _, rows_dev, width, chans = feats.shape
    owners = lax.axis_size(OWNER)
    samples = lax.axis_size(DP)
    owner_id = lax.axis_index(OWNER)
    dp_id = lax.axis_index(DP)
    y_id = lax.axis_index("y")
    z_id = lax.axis_index("zh")
    npos = samples * rows_dev * owners * width
    patch = 9 * chans
    inner = owner_id < owners - 1
    f = feats[:, 0]
    top = top_grad[0]

    above = shifted(jnp.concatenate([f[3], f[2, 1:], f[0, 1:], top[1:]]), 1, False)
    below = shifted(jnp.concatenate([f[3], f[2, :1], f[0, :1], top[:1], f[1]]), -1, True)
    below1 = below[5:]
    below = jnp.where(inner, below[:5], jnp.zeros_like(below[:5]))
    wide3 = jnp.concatenate([above[:2], f[3], below[:2]])
    strips = [
        jnp.concatenate([above[3:4], f[0], below[3:4]]),
        jnp.concatenate([f[1], below1]),
        jnp.concatenate([above[2:3], f[2], below[2:3]]),
        wide3[1:5],
    ]
    local = jnp.concatenate(
        [
            a_inv.reshape(-1, chans),
            g_inv[0].astype(jnp.bfloat16),
            jnp.zeros((12, chans), jnp.bfloat16),
        ]
    )
    inverses = lax.all_gather(local, OWNER, axis=0, tiled=True).reshape((owners,) + local.shape)

    flipped = jnp.transpose(weights.reshape(num_layers, 9, chans, chans), (0, 1, 3, 2)).reshape(
        num_layers, patch, chans
    )

    def slope(layer, win):
        pre = jnp.dot(to_columns(win), weights[layer], preferred_element_type=jnp.float32)
        return silu_slope(pre)

    def times(grad_in, slopes):
        return (grad_in.reshape(slopes.shape).astype(jnp.float32) * slopes).astype(jnp.bfloat16)

    def back(layer, win):
        return jnp.dot(
            back_columns(win), flipped[layer], preferred_element_type=jnp.float32
        ).astype(jnp.bfloat16)

    image = (rows_dev, width, chans)
    top_wide = jnp.concatenate([above[4:5], top, below[4:5]])
    dpre3 = times(top_wide, slope(3, windows(wide3))).reshape((rows_dev + 2, width, chans))
    dpre2 = times(back(3, windows(dpre3)), slope(2, windows(strips[2]))).reshape(image)
    after = shifted(dpre2, -1, True)
    dy1 = back(2, cut_windows(jnp.concatenate([dpre2, after]), inner))
    dpre1 = times(dy1, slope(1, cut_windows(strips[1], inner))).reshape(image)
    stacked, dpre1 = lax.optimization_barrier((jnp.stack(strips), dpre1))
    before = shifted(dpre1, 1, True)
    layer_strips = exchange(stacked, "y")
    edge_top = jnp.where(owner_id > 0, before[:1], jnp.zeros_like(before[:1]))
    edge_end = jnp.where(inner, dpre1[1:], jnp.zeros_like(dpre1[1:]))
    dy0 = back(1, windows(jnp.concatenate([edge_top, before[1:], dpre1[:1], edge_end])))
    dpre0 = times(dy0, slope(0, windows(strips[0]))).reshape(image)

    layer_dpre = exchange(jnp.stack([dpre0, dpre1, dpre2, dpre3[1:3]]), "y")
    big_dpre = layer_dpre.reshape(-1, chans)
    last_one = (y_id == 1) & (z_id == ZH - 1)
    big_cols = jnp.concatenate(
        [
            to_columns(
                windows(layer_strips[j])
                if j < Y - 1
                else cut_windows(layer_strips[j], jnp.logical_not(last_one))
            )
            for j in range(Y)
        ]
    )
    gram = inner_rows(big_cols, big_cols).astype(jnp.bfloat16)
    grad = inner_rows(big_cols, big_dpre).astype(jnp.bfloat16)
    gfac = inner_rows(big_dpre, big_dpre).astype(jnp.bfloat16)
    blocks = [
        gram[a * chans : (a + 1) * chans, b * chans : (b + 1) * chans] for a, b in PAIRS
    ]
    half = (NG + 1) // 2
    dense = jnp.concatenate([grad, jnp.zeros((chans, chans), jnp.bfloat16)])
    cut = dense.shape[0] // 2
    parts = jnp.concatenate(blocks[:half] + [dense[:cut]] + blocks[half:] + [gfac, dense[cut:]])

    mine = scatter_sum(parts, "core")
    rest = ("x", "zl")
    count = lax.axis_size(rest)
    fac_rows = half * chans // count
    mine = jnp.concatenate(
        [
            mine[: half * chans].reshape(count, -1, chans),
            mine[half * chans :].reshape(count, -1, chans),
        ],
        axis=1,
    )
    piece = scatter_sum(mine.reshape(-1, chans), rest)
    held = spread(piece[:fac_rows], "y")
    layer_ids = jnp.arange(num_layers, dtype=jnp.int32)

    def pick(z):
        lay = jnp.sum(jnp.where(table == z * Y + y_id, layer_ids, 0))
        return lax.dynamic_index_in_dim(held, lay, 0, keepdims=False)

    sent = jnp.stack([jnp.concatenate([pick(z), piece[fac_rows:]]) for z in range(ZH)])
    total = exchange(sent, "zh")
    total = jnp.sum(total.astype(jnp.float32), axis=0).astype(jnp.bfloat16)
    summed = spread(spread(spread(total, "zl"), "x"), "core").reshape(samples, -1, chans)

    in_grad_win = jnp.concatenate([shifted(dpre0[1:], 1, False), dpre0, shifted(dpre0[:1], -1, False)])
    in_grad = back(0, windows(in_grad_win)).reshape((1,) + image)

    mine_inv = lax.dynamic_index_in_dim(inverses, table[y_id], 0, keepdims=False)
    rows_out = patch // samples
    a_mine = mine_inv[: rows_out * 9].reshape(rows_out, patch)
    g_mine = mine_inv[rows_out * 9 : rows_out * 9 + chans]
    grad_sum = summed[:, fac_rows:].reshape(-1, chans)[:patch]
    mixed = jnp.dot(grad_sum, g_mine, preferred_element_type=jnp.float32)
    mixed = mixed / jnp.sqrt(jnp.float32(npos))
    panel = jnp.dot(a_mine.astype(jnp.float32), mixed, precision=lax.Precision.HIGHEST)
    step_out = spread(panel.astype(jnp.bfloat16), "y")

    stats = summed[:, :fac_rows].reshape(NG + 1, chans, chans)
    have = jnp.any(table == owner_id).astype(jnp.float32)
    scale = have / npos
    a_out = factor_rows(stats, dp_id * rows_out, scale, rows_out)[None]
    g_out = (stats[NG].astype(jnp.float32) * scale)[None]
    return (step_out, a_out, g_out, in_grad)


def solution(mesh):
    fine = Mesh(mesh.devices.reshape(X, ZL, CORE, ZH, Y), DP + OWNER)
    placed = (
        P(None, DP, OWNER, None, None),
        P(DP, OWNER, None, None),
        P(),
        P(),
        P(OWNER, DP, None),
        P(OWNER, None, None),
    )
    return jax.shard_map(
        shards,
        mesh=fine,
        in_specs=placed,
        out_specs=(
            P(None, DP, None),
            P(OWNER, DP, None),
            P(OWNER, None, None),
            P(DP, OWNER, None, None),
        ),
        check_vma=False,
    )
```

```python
import jax
import jax.numpy as jnp
from jax import lax
from jax.experimental import pallas as pl
from jax.experimental.pallas import tpu as pltpu
from jax.sharding import Mesh, PartitionSpec as P

X, ZL, CORE, ZH, Y = 4, 4, 2, 4, 4
OWNER = ("zh", "y")
DP = ("x", "zl", "core")


def shifted(x, shift, cyclic):
    count = ZH * Y
    pairs = [(i, (i + shift) % count) for i in range(count)]
    if not cyclic:
        pairs = [(a, b) for a, b in pairs if b - a == shift]
    return lax.ppermute(x, OWNER, pairs)


def exchange(x, axis):
    return lax.all_to_all(x, axis, split_axis=0, concat_axis=0, tiled=True)


def spread(x, axis):
    count = lax.axis_size(axis)
    return exchange(jnp.broadcast_to(x[None], (count,) + x.shape), axis)


def scatter_sum(x, axis):
    count = lax.axis_size(axis)
    got = exchange(x.reshape((count, x.shape[0] // count) + x.shape[1:]), axis)
    return jnp.sum(got.astype(jnp.float32), axis=0).astype(jnp.bfloat16)


def windows(rows):
    rows = jnp.pad(rows, ((0, 0), (1, 1), (0, 0)))
    return jnp.stack([rows[i : i + 3] for i in range(rows.shape[0] - 2)])


def cut_windows(rows, whole):
    first, second = rows[:3], rows[1:]
    first = jnp.where(whole, first, first * jnp.array([1, 1, 0], rows.dtype)[:, None, None])
    second = jnp.where(whole, second, second * jnp.array([0, 1, 1], rows.dtype)[:, None, None])
    return jnp.pad(jnp.stack([first, second]), ((0, 0), (0, 0), (1, 1), (0, 0)))


def to_columns(win):
    width = win.shape[2] - 2
    taps = [win[:, ky, kx : kx + width] for ky in range(3) for kx in range(3)]
    return jnp.concatenate(taps, axis=-1).reshape(-1, 9 * win.shape[-1])


def back_columns(win):
    width = win.shape[2] - 2
    taps = [win[:, 2 - ky, 2 - kx : 2 - kx + width] for ky in range(3) for kx in range(3)]
    return jnp.concatenate(taps, axis=-1).reshape(-1, 9 * win.shape[-1])


def silu_slope(value):
    sig = jax.nn.sigmoid(value)
    return sig * (1.0 + value * (1.0 - sig))


def inner_rows(left, right):
    return lax.dot_general(
        left, right, (((0,), (0,)), ((), ())), preferred_element_type=jnp.float32
    )


def block_classes():
    found = {}
    pairs = []
    where = {}
    for a in range(9):
        for b in range(9):
            first, second, flip = a, b, False
            dy, dx = b // 3 - a // 3, b % 3 - a % 3
            if dy < 0 or (dy == 0 and dx < 0):
                first, second, flip = b, a, True
                dy, dx = -dy, -dx
            key = (dy, dx, first // 3 if dy == 0 else -1, first % 3 if dx == 0 else -1)
            if key not in found:
                found[key] = len(pairs)
                pairs.append((first, second))
            where[a, b] = (found[key], flip)
    return pairs, where


PAIRS, WHERE = block_classes()
NG = len(PAIRS)


def factor_rows(blocks, first_row, scale, rows):
    chans = blocks.shape[-1]
    index = jnp.array([WHERE[a, b][0] for a in range(9) for b in range(9)], jnp.int32)
    flips = jnp.array([int(WHERE[a, b][1]) for a in range(9) for b in range(9)], jnp.int32)

    def kernel(index_ref, flip_ref, row_ref, scale_ref, blocks_ref, out_ref, band):
        start = row_ref[0]
        tap = lax.div(start, chans)
        for t in range(2):
            a = jnp.minimum(tap + t, 8)
            for b in range(9):
                block = blocks_ref[index_ref[a * 9 + b]].astype(jnp.float32)
                flip = flip_ref[a * 9 + b] != 0
                band[t * chans : (t + 1) * chans, b * chans : (b + 1) * chans] = jnp.where(
                    flip, block.T, block
                )
        inside = start - tap * chans
        base = pl.multiple_of(lax.div(inside, 8) * 8, 8)
        got = band[pl.ds(base, rows + 4), :]
        odd = inside != base
        out_ref[...] = jnp.where(odd, got[4:], got[:rows]) * scale_ref[0]

    smem = pl.BlockSpec(memory_space=pltpu.SMEM)
    vmem = pl.BlockSpec(memory_space=pltpu.VMEM)
    return pl.pallas_call(
        kernel,
        out_shape=jax.ShapeDtypeStruct((rows, 9 * chans), jnp.float32),
        in_specs=[smem, smem, smem, smem, vmem],
        out_specs=vmem,
        scratch_shapes=[pltpu.VMEM((2 * chans, 9 * chans), jnp.float32)],
        compiler_params=pltpu.CompilerParams(vmem_limit_bytes=16 * 2**20),
        cost_estimate=pl.CostEstimate(flops=10**6, bytes_accessed=2 * 10**6, transcendentals=0),
    )(index, flips, first_row.reshape(1), scale.reshape(1), blocks)


def local_sums(gram, cols, dpre):
    chans = dpre.shape[-1]
    half = (NG + 1) // 2

    def kernel(gram_ref, cols_ref, dpre_ref, out_ref):
        def put(kind, index, value):
            per = half if kind == 0 else 5
            slot = index // per * (half + 5) + index % per + (half if kind else 0)
            out_ref[slot * chans : (slot + 1) * chans, :] = value.astype(out_ref.dtype)

        for i, (a, b) in enumerate(PAIRS):
            put(0, i, gram_ref[a * chans : (a + 1) * chans, b * chans : (b + 1) * chans])
        across = (((0,), (0,)), ((), ()))
        mine = dpre_ref[...]
        put(0, NG, lax.dot_general(mine, mine, across, preferred_element_type=jnp.float32))
        grad = lax.dot_general(mine, cols_ref[...], across, preferred_element_type=jnp.float32)
        for t in range(9):
            put(1, t, grad[:, t * chans : (t + 1) * chans].T)
        put(1, 9, jnp.zeros((chans, chans), jnp.float32))

    vmem = pl.BlockSpec(memory_space=pltpu.VMEM)
    return pl.pallas_call(
        kernel,
        out_shape=jax.ShapeDtypeStruct(((NG + 11) * chans, chans), jnp.bfloat16),
        in_specs=[vmem] * 3,
        out_specs=vmem,
        compiler_params=pltpu.CompilerParams(vmem_limit_bytes=24 * 2**20),
        cost_estimate=pl.CostEstimate(
            flops=2 * cols.size * chans, bytes_accessed=6 * 10**6, transcendentals=0
        ),
    )(gram, cols, dpre)


def shards(feats, top_grad, weights, table, a_inv, g_inv):
    num_layers, _, rows_dev, width, chans = feats.shape
    owners = lax.axis_size(OWNER)
    samples = lax.axis_size(DP)
    owner_id = lax.axis_index(OWNER)
    dp_id = lax.axis_index(DP)
    y_id = lax.axis_index("y")
    z_id = lax.axis_index("zh")
    npos = samples * rows_dev * owners * width
    patch = 9 * chans
    inner = owner_id < owners - 1
    f = feats[:, 0]
    top = top_grad[0]

    above = shifted(jnp.concatenate([f[3], f[2, 1:], f[0, 1:], top[1:]]), 1, False)
    below = shifted(jnp.concatenate([f[3], f[2, :1], f[0, :1], top[:1], f[1]]), -1, True)
    below1 = below[5:]
    below = jnp.where(inner, below[:5], jnp.zeros_like(below[:5]))
    wide3 = jnp.concatenate([above[:2], f[3], below[:2]])
    strips = [
        jnp.concatenate([above[3:4], f[0], below[3:4]]),
        jnp.concatenate([f[1], below1]),
        jnp.concatenate([above[2:3], f[2], below[2:3]]),
        wide3[1:5],
    ]
    flipped = jnp.transpose(weights.reshape(num_layers, 9, chans, chans), (0, 1, 3, 2)).reshape(
        num_layers, patch, chans
    )

    def slope(layer, win):
        pre = jnp.dot(to_columns(win), weights[layer], preferred_element_type=jnp.float32)
        return silu_slope(pre)

    def times(grad_in, slopes):
        return (grad_in.reshape(slopes.shape).astype(jnp.float32) * slopes).astype(jnp.bfloat16)

    def back(layer, win):
        return jnp.dot(
            back_columns(win), flipped[layer], preferred_element_type=jnp.float32
        ).astype(jnp.bfloat16)

    image = (rows_dev, width, chans)
    top_wide = jnp.concatenate([above[4:5], top, below[4:5]])
    dpre3 = times(top_wide, slope(3, windows(wide3))).reshape((rows_dev + 2, width, chans))
    dpre2 = times(back(3, windows(dpre3)), slope(2, windows(strips[2]))).reshape(image)
    after = shifted(dpre2, -1, True)
    dy1 = back(2, cut_windows(jnp.concatenate([dpre2, after]), inner))
    dpre1 = times(dy1, slope(1, cut_windows(strips[1], inner))).reshape(image)
    strip_rows = (rows_dev + 2) * width
    local = jnp.concatenate([a_inv.reshape(-1, chans), g_inv[0].astype(jnp.bfloat16)])
    local = jnp.broadcast_to(local[None], (num_layers,) + local.shape)
    stacked = jnp.stack(strips).reshape(num_layers, strip_rows, chans)
    pad = jnp.zeros((num_layers, -local.shape[1] % 16, chans), jnp.bfloat16)
    stacked, dpre1 = lax.optimization_barrier(
        (jnp.concatenate([stacked, local, pad], axis=1), dpre1)
    )
    before = shifted(dpre1, 1, True)
    from_y = exchange(stacked, "y")
    layer_strips = from_y[:, :strip_rows].reshape(num_layers, rows_dev + 2, width, chans)
    source = table[y_id]
    near = lax.dynamic_index_in_dim(from_y, source % Y, 0, keepdims=False)[strip_rows:]
    inverses = spread(near, "zh")
    edge_top = jnp.where(owner_id > 0, before[:1], jnp.zeros_like(before[:1]))
    edge_end = jnp.where(inner, dpre1[1:], jnp.zeros_like(dpre1[1:]))
    dy0 = back(1, windows(jnp.concatenate([edge_top, before[1:], dpre1[:1], edge_end])))
    dpre0 = times(dy0, slope(0, windows(strips[0]))).reshape(image)

    layer_dpre = exchange(jnp.stack([dpre0, dpre1, dpre2, dpre3[1:3]]), "y")
    big_dpre = layer_dpre.reshape(-1, chans)
    last_one = (y_id == 1) & (z_id == ZH - 1)
    big_cols = jnp.concatenate(
        [
            to_columns(
                windows(layer_strips[j])
                if j < Y - 1
                else cut_windows(layer_strips[j], jnp.logical_not(last_one))
            )
            for j in range(Y)
        ]
    )
    gram = inner_rows(big_cols, big_cols).astype(jnp.bfloat16)
    half = (NG + 1) // 2
    parts = local_sums(gram, big_cols, big_dpre)

    mine = scatter_sum(parts, "core")
    rest = ("x", "zl")
    count = lax.axis_size(rest)
    fac_rows = half * chans // count
    mine = jnp.concatenate(
        [
            mine[: half * chans].reshape(count, -1, chans),
            mine[half * chans :].reshape(count, -1, chans),
        ],
        axis=1,
    )
    piece = scatter_sum(mine.reshape(-1, chans), rest)
    piece, inverses = lax.optimization_barrier((piece, inverses))
    held = spread(piece[:fac_rows], "y")
    layer_ids = jnp.arange(num_layers, dtype=jnp.int32)

    def pick(z):
        lay = jnp.sum(jnp.where(table == z * Y + y_id, layer_ids, 0))
        return lax.dynamic_index_in_dim(held, lay, 0, keepdims=False)

    sent = jnp.stack([jnp.concatenate([pick(z), piece[fac_rows:]]) for z in range(ZH)])
    total = exchange(sent, "zh")
    total = jnp.sum(total.astype(jnp.float32), axis=0).astype(jnp.bfloat16)
    summed = spread(spread(spread(total, "zl"), "x"), "core").reshape(samples, -1, chans)

    in_grad_win = jnp.concatenate([shifted(dpre0[1:], 1, False), dpre0, shifted(dpre0[:1], -1, False)])
    in_grad = back(0, windows(in_grad_win)).reshape((1,) + image)

    mine_inv = lax.dynamic_index_in_dim(inverses, source // Y, 0, keepdims=False)
    rows_out = patch // samples
    a_mine = mine_inv[: rows_out * 9].reshape(rows_out, patch)
    g_mine = mine_inv[rows_out * 9 : rows_out * 9 + chans]
    grad_sum = summed[:, fac_rows:].reshape(-1, chans)[:patch]
    mixed = jnp.dot(grad_sum, g_mine, preferred_element_type=jnp.float32)
    mixed = mixed / jnp.sqrt(jnp.float32(npos))
    panel = jnp.dot(a_mine.astype(jnp.float32), mixed, precision=lax.Precision.HIGHEST)
    step_out = spread(panel.astype(jnp.bfloat16), "y")

    stats = summed[:, :fac_rows].reshape(NG + 1, chans, chans)
    have = jnp.any(table == owner_id).astype(jnp.float32)
    scale = have / npos
    a_out = factor_rows(stats, dp_id * rows_out, scale, rows_out)[None]
    g_out = (stats[NG].astype(jnp.float32) * scale)[None]
    return (step_out, a_out, g_out, in_grad)


def solution(mesh):
    fine = Mesh(mesh.devices.reshape(X, ZL, CORE, ZH, Y), DP + OWNER)
    placed = (
        P(None, DP, OWNER, None, None),
        P(DP, OWNER, None, None),
        P(),
        P(),
        P(OWNER, DP, None),
        P(OWNER, None, None),
    )
    return jax.shard_map(
        shards,
        mesh=fine,
        in_specs=placed,
        out_specs=(
            P(None, DP, None),
            P(OWNER, DP, None),
            P(OWNER, None, None),
            P(DP, OWNER, None, None),
        ),
        check_vma=False,
    )
```

```python
import jax
import jax.numpy as jnp
from jax import lax
from jax.experimental import pallas as pl
from jax.experimental.pallas import tpu as pltpu
from jax.sharding import Mesh, PartitionSpec as P

X, ZL, CORE, ZH, Y = 4, 4, 2, 4, 4
OWNER = ("zh", "y")
DP = ("x", "zl", "core")


def shifted(x, shift, cyclic):
    count = ZH * Y
    pairs = [(i, (i + shift) % count) for i in range(count)]
    if not cyclic:
        pairs = [(a, b) for a, b in pairs if b - a == shift]
    return lax.ppermute(x, OWNER, pairs)


def exchange(x, axis):
    return lax.all_to_all(x, axis, split_axis=0, concat_axis=0, tiled=True)


def spread(x, axis):
    count = lax.axis_size(axis)
    return exchange(jnp.broadcast_to(x[None], (count,) + x.shape), axis)


def scatter_sum(x, axis):
    count = lax.axis_size(axis)
    got = exchange(x.reshape((count, x.shape[0] // count) + x.shape[1:]), axis)
    return jnp.sum(got.astype(jnp.float32), axis=0).astype(jnp.bfloat16)


def over_y(x, shift):
    return lax.ppermute(x, "y", [(y, (y + shift) % Y) for y in range(Y)])


def traded(keep, send):
    got = lax.ppermute(send, "core", [(c, (c + 1) % CORE) for c in range(CORE)])
    return (keep.astype(jnp.float32) + got.astype(jnp.float32)).astype(jnp.bfloat16)


def windows(rows):
    rows = jnp.pad(rows, ((0, 0), (1, 1), (0, 0)))
    return jnp.stack([rows[i : i + 3] for i in range(rows.shape[0] - 2)])


def cut_windows(rows, whole):
    first, second = rows[:3], rows[1:]
    first = jnp.where(whole, first, first * jnp.array([1, 1, 0], rows.dtype)[:, None, None])
    second = jnp.where(whole, second, second * jnp.array([0, 1, 1], rows.dtype)[:, None, None])
    return jnp.pad(jnp.stack([first, second]), ((0, 0), (0, 0), (1, 1), (0, 0)))


def to_columns(win):
    width = win.shape[2] - 2
    taps = [win[:, ky, kx : kx + width] for ky in range(3) for kx in range(3)]
    return jnp.concatenate(taps, axis=-1).reshape(-1, 9 * win.shape[-1])


def back_columns(win):
    width = win.shape[2] - 2
    taps = [win[:, 2 - ky, 2 - kx : 2 - kx + width] for ky in range(3) for kx in range(3)]
    return jnp.concatenate(taps, axis=-1).reshape(-1, 9 * win.shape[-1])


def silu_slope(value):
    sig = jax.nn.sigmoid(value)
    return sig * (1.0 + value * (1.0 - sig))


def inner_rows(left, right):
    return lax.dot_general(
        left, right, (((0,), (0,)), ((), ())), preferred_element_type=jnp.float32
    )


def block_classes():
    found = {}
    pairs = []
    where = {}
    for a in range(9):
        for b in range(9):
            first, second, flip = a, b, False
            dy, dx = b // 3 - a // 3, b % 3 - a % 3
            if dy < 0 or (dy == 0 and dx < 0):
                first, second, flip = b, a, True
                dy, dx = -dy, -dx
            key = (dy, dx, first // 3 if dy == 0 else -1, first % 3 if dx == 0 else -1)
            if key not in found:
                found[key] = len(pairs)
                pairs.append((first, second))
            where[a, b] = (found[key], flip)
    return pairs, where


PAIRS, WHERE = block_classes()
NG = len(PAIRS)
NB = 32
ND = 10


def put_halves(blocks, core, keep_ref, send_ref):
    chans = blocks[0].shape[-1]
    half = len(blocks) // 2
    for i in range(half):
        rows = slice(i * chans, (i + 1) * chans)
        low, high = blocks[i], blocks[half + i]
        keep_ref[rows, :] = jnp.where(core == 0, low, high)
        send_ref[rows, :] = jnp.where(core == 0, high, low)


def gram_halves(cols, core):
    chans = cols.shape[1] // 9

    def kernel(core_ref, cols_ref, keep_ref, send_ref, done):
        for a in range(9):
            wanted = [b for first, b in PAIRS if first == a]
            if not wanted:
                continue
            low = min(wanted)
            left = cols_ref[:, a * chans : (a + 1) * chans].T
            right = cols_ref[:, low * chans : (max(wanted) + 1) * chans]
            product = jnp.dot(left, right, preferred_element_type=jnp.float32)
            for i, (first, b) in enumerate(PAIRS):
                if first == a:
                    part = product[:, (b - low) * chans : (b - low + 1) * chans]
                    done[i] = part.astype(done.dtype)
        for i in range(NG, NB):
            done[i] = jnp.zeros(done.shape[1:], done.dtype)
        put_halves([done[i] for i in range(NB)], core_ref[0], keep_ref, send_ref)

    vmem = pl.BlockSpec(memory_space=pltpu.VMEM)
    half = jax.ShapeDtypeStruct((NB // 2 * chans, chans), jnp.bfloat16)
    return pl.pallas_call(
        kernel,
        out_shape=(half, half),
        in_specs=[pl.BlockSpec(memory_space=pltpu.SMEM), vmem],
        out_specs=(vmem, vmem),
        scratch_shapes=[pltpu.VMEM((NB, chans, chans), jnp.bfloat16)],
        compiler_params=pltpu.CompilerParams(vmem_limit_bytes=24 * 2**20),
        cost_estimate=pl.CostEstimate(
            flops=2 * NB * cols.size * chans // 9, bytes_accessed=4 * 10**6, transcendentals=0
        ),
    )(core.reshape(1), cols)


def grad_halves(cols, dpre, core):
    chans = dpre.shape[-1]

    def kernel(core_ref, cols_ref, dpre_ref, keep_ref, send_ref):
        across = (((0,), (0,)), ((), ()))
        mine = dpre_ref[...]
        own = lax.dot_general(mine, mine, across, preferred_element_type=jnp.float32)
        grad = lax.dot_general(mine, cols_ref[...], across, preferred_element_type=jnp.float32)
        blocks = [grad[:, t * chans : (t + 1) * chans].T.astype(jnp.bfloat16) for t in range(9)]
        put_halves(blocks + [own.astype(jnp.bfloat16)], core_ref[0], keep_ref, send_ref)

    vmem = pl.BlockSpec(memory_space=pltpu.VMEM)
    half = jax.ShapeDtypeStruct((ND // 2 * chans, chans), jnp.bfloat16)
    return pl.pallas_call(
        kernel,
        out_shape=(half, half),
        in_specs=[pl.BlockSpec(memory_space=pltpu.SMEM), vmem, vmem],
        out_specs=(vmem, vmem),
        compiler_params=pltpu.CompilerParams(vmem_limit_bytes=24 * 2**20),
        cost_estimate=pl.CostEstimate(
            flops=2 * cols.size * chans, bytes_accessed=3 * 10**6, transcendentals=0
        ),
    )(core.reshape(1), cols, dpre)


def factor_rows(blocks, first_row, scale, rows):
    chans = blocks.shape[-1]
    count = blocks.shape[0]
    order = [i % (count // 2) * 2 + i // (count // 2) for i in range(count)]
    index = jnp.array([order[WHERE[a, b][0]] for a in range(9) for b in range(9)], jnp.int32)
    flips = jnp.array([int(WHERE[a, b][1]) for a in range(9) for b in range(9)], jnp.int32)

    def kernel(index_ref, flip_ref, row_ref, scale_ref, blocks_ref, out_ref, band):
        start = row_ref[0]
        tap = lax.div(start, chans)
        for t in range(2):
            a = jnp.minimum(tap + t, 8)
            for b in range(9):
                block = blocks_ref[index_ref[a * 9 + b]].astype(jnp.float32)
                flip = flip_ref[a * 9 + b] != 0
                band[t * chans : (t + 1) * chans, b * chans : (b + 1) * chans] = jnp.where(
                    flip, block.T, block
                )
        inside = start - tap * chans
        base = pl.multiple_of(lax.div(inside, 8) * 8, 8)
        got = band[pl.ds(base, rows + 4), :]
        odd = inside != base
        out_ref[...] = jnp.where(odd, got[4:], got[:rows]) * scale_ref[0]

    smem = pl.BlockSpec(memory_space=pltpu.SMEM)
    vmem = pl.BlockSpec(memory_space=pltpu.VMEM)
    return pl.pallas_call(
        kernel,
        out_shape=jax.ShapeDtypeStruct((rows, 9 * chans), jnp.float32),
        in_specs=[smem, smem, smem, smem, vmem],
        out_specs=vmem,
        scratch_shapes=[pltpu.VMEM((2 * chans, 9 * chans), jnp.float32)],
        compiler_params=pltpu.CompilerParams(vmem_limit_bytes=16 * 2**20),
        cost_estimate=pl.CostEstimate(flops=10**6, bytes_accessed=2 * 10**6, transcendentals=0),
    )(index, flips, first_row.reshape(1), scale.reshape(1), blocks)


def shards(feats, top_grad, weights, table, a_inv, g_inv):
    num_layers, _, rows_dev, width, chans = feats.shape
    owners = lax.axis_size(OWNER)
    samples = lax.axis_size(DP)
    owner_id = lax.axis_index(OWNER)
    dp_id = lax.axis_index(DP)
    y_id = lax.axis_index("y")
    z_id = lax.axis_index("zh")
    npos = samples * rows_dev * owners * width
    patch = 9 * chans
    inner = owner_id < owners - 1
    f = feats[:, 0]
    top = top_grad[0]

    above = shifted(jnp.concatenate([f[3], f[2, 1:], f[0, 1:], top[1:]]), 1, False)
    below = shifted(jnp.concatenate([f[3], f[2, :1], f[0, :1], top[:1], f[1]]), -1, True)
    below1 = below[5:]
    below = jnp.where(inner, below[:5], jnp.zeros_like(below[:5]))
    wide3 = jnp.concatenate([above[:2], f[3], below[:2]])
    strips = [
        jnp.concatenate([above[3:4], f[0], below[3:4]]),
        jnp.concatenate([f[1], below1]),
        jnp.concatenate([above[2:3], f[2], below[2:3]]),
        wide3[1:5],
    ]
    layer_strips = exchange(jnp.stack(strips), "y")
    last_one = (y_id == 1) & (z_id == ZH - 1)
    big_cols = jnp.concatenate(
        [
            to_columns(
                windows(layer_strips[j])
                if j < Y - 1
                else cut_windows(layer_strips[j], jnp.logical_not(last_one))
            )
            for j in range(Y)
        ]
    )
    core_id = lax.axis_index("core")
    rest = ("x", "zl")
    fac_core = traded(*gram_halves(big_cols, core_id))

    flipped = jnp.transpose(weights.reshape(num_layers, 9, chans, chans), (0, 1, 3, 2)).reshape(
        num_layers, patch, chans
    )

    def slope(layer, win):
        pre = jnp.dot(to_columns(win), weights[layer], preferred_element_type=jnp.float32)
        return silu_slope(pre)

    def times(grad_in, slopes):
        return (grad_in.reshape(slopes.shape).astype(jnp.float32) * slopes).astype(jnp.bfloat16)

    def back(layer, win):
        return jnp.dot(
            back_columns(win), flipped[layer], preferred_element_type=jnp.float32
        ).astype(jnp.bfloat16)

    image = (rows_dev, width, chans)
    top_wide = jnp.concatenate([above[4:5], top, below[4:5]])
    dpre3 = times(top_wide, slope(3, windows(wide3))).reshape((rows_dev + 2, width, chans))
    dpre2 = times(back(3, windows(dpre3)), slope(2, windows(strips[2]))).reshape(image)
    after = shifted(dpre2, -1, True)
    dy1 = back(2, cut_windows(jnp.concatenate([dpre2, after]), inner))
    dpre1 = times(dy1, slope(1, cut_windows(strips[1], inner))).reshape(image)
    before = shifted(dpre1, 1, True)
    edge_top = jnp.where(owner_id > 0, before[:1], jnp.zeros_like(before[:1]))
    edge_end = jnp.where(inner, dpre1[1:], jnp.zeros_like(dpre1[1:]))
    dy0 = back(1, windows(jnp.concatenate([edge_top, before[1:], dpre1[:1], edge_end])))
    dpre0 = times(dy0, slope(0, windows(strips[0]))).reshape(image)

    fac_core, dpre0 = lax.optimization_barrier((fac_core, dpre0))
    fac_piece = scatter_sum(fac_core, rest)

    all_dpre = jnp.stack([dpre0, dpre1, dpre2, dpre3[1:3]]).reshape(num_layers, -1, chans)

    def dpre_of(lay):
        return lax.dynamic_index_in_dim(all_dpre, lay % num_layers, 0, keepdims=False)

    got = jnp.stack([dpre_of(y_id)] + [over_y(dpre_of(y_id + s), s) for s in range(1, Y)])
    got = [lax.dynamic_index_in_dim(got, (y_id - j) % Y, 0, keepdims=False) for j in range(Y)]
    grad_core = traded(*grad_halves(big_cols, jnp.concatenate(got), core_id))
    grad_core, fac_piece = lax.optimization_barrier((grad_core, fac_piece))
    grad_held = spread(scatter_sum(grad_core, rest), "y")
    fac_held = jnp.stack([fac_piece] + [over_y(fac_piece, s) for s in range(1, Y)])
    layer_ids = jnp.arange(num_layers, dtype=jnp.int32)

    def pick(z):
        lay = jnp.sum(jnp.where(table == z * Y + y_id, layer_ids, 0))
        fac = lax.dynamic_index_in_dim(fac_held, (y_id - lay) % Y, 0, keepdims=False)
        return jnp.concatenate([fac, lax.dynamic_index_in_dim(grad_held, lay, 0, keepdims=False)])

    total = exchange(jnp.stack([pick(z) for z in range(ZH)]), "zh")
    total = jnp.sum(total.astype(jnp.float32), axis=0).astype(jnp.bfloat16)
    fac_rows = fac_piece.shape[0]
    stats = lax.all_gather(total[:fac_rows], DP, axis=0, tiled=True).reshape(-1, chans, chans)
    grads = spread(spread(spread(total[fac_rows:], "zl"), "x"), "core").reshape(-1, chans)

    in_grad_win = jnp.concatenate([shifted(dpre0[1:], 1, False), dpre0, shifted(dpre0[:1], -1, False)])
    in_grad = back(0, windows(in_grad_win)).reshape((1,) + image)

    mixed = jnp.dot(
        grads[:patch].astype(jnp.float32) / jnp.sqrt(jnp.float32(npos)),
        g_inv[0],
        precision=lax.Precision.HIGHEST,
    )
    panel = jnp.dot(a_inv[0].astype(jnp.float32), mixed, precision=lax.Precision.HIGHEST)
    panels = spread(panel.astype(jnp.bfloat16), OWNER)
    step_out = panels[table]

    have = jnp.any(table == owner_id).astype(jnp.float32)
    scale = have / npos
    rows_out = patch // samples
    a_out = factor_rows(stats, dp_id * rows_out, scale, rows_out)[None]
    g_out = (grads[patch:].astype(jnp.float32) * scale)[None]
    return (step_out, a_out, g_out, in_grad)


def solution(mesh):
    fine = Mesh(mesh.devices.reshape(X, ZL, CORE, ZH, Y), DP + OWNER)
    placed = (
        P(None, DP, OWNER, None, None),
        P(DP, OWNER, None, None),
        P(),
        P(),
        P(OWNER, DP, None),
        P(OWNER, None, None),
    )
    return jax.shard_map(
        shards,
        mesh=fine,
        in_specs=placed,
        out_specs=(
            P(None, DP, None),
            P(OWNER, DP, None),
            P(OWNER, None, None),
            P(DP, OWNER, None, None),
        ),
        check_vma=False,
    )
```

```python
import jax
import jax.numpy as jnp
from jax import lax
from jax.experimental import pallas as pl
from jax.experimental.pallas import tpu as pltpu
from jax.sharding import Mesh, PartitionSpec as P

X, ZL, CORE, ZH, Y = 4, 4, 2, 4, 4
OWNER = ("zh", "y")
DP = ("x", "zl", "core")


def shifted(x, shift, cyclic):
    count = ZH * Y
    pairs = [(i, (i + shift) % count) for i in range(count)]
    if not cyclic:
        pairs = [(a, b) for a, b in pairs if b - a == shift]
    return lax.ppermute(x, OWNER, pairs)


def exchange(x, axis):
    return lax.all_to_all(x, axis, split_axis=0, concat_axis=0, tiled=True)


def spread(x, axis):
    count = lax.axis_size(axis)
    return exchange(jnp.broadcast_to(x[None], (count,) + x.shape), axis)


def scatter_sum(x, axis):
    count = lax.axis_size(axis)
    got = exchange(x.reshape((count, x.shape[0] // count) + x.shape[1:]), axis)
    return jnp.sum(got.astype(jnp.float32), axis=0).astype(jnp.bfloat16)


def windows(rows):
    rows = jnp.pad(rows, ((0, 0), (1, 1), (0, 0)))
    return jnp.stack([rows[i : i + 3] for i in range(rows.shape[0] - 2)])


def cut_windows(rows, whole):
    first, second = rows[:3], rows[1:]
    first = jnp.where(whole, first, first * jnp.array([1, 1, 0], rows.dtype)[:, None, None])
    second = jnp.where(whole, second, second * jnp.array([0, 1, 1], rows.dtype)[:, None, None])
    return jnp.pad(jnp.stack([first, second]), ((0, 0), (0, 0), (1, 1), (0, 0)))


def to_columns(win):
    width = win.shape[2] - 2
    taps = [win[:, ky, kx : kx + width] for ky in range(3) for kx in range(3)]
    return jnp.concatenate(taps, axis=-1).reshape(-1, 9 * win.shape[-1])


def back_columns(win):
    width = win.shape[2] - 2
    taps = [win[:, 2 - ky, 2 - kx : 2 - kx + width] for ky in range(3) for kx in range(3)]
    return jnp.concatenate(taps, axis=-1).reshape(-1, 9 * win.shape[-1])


def silu_slope(value):
    sig = jax.nn.sigmoid(value)
    return sig * (1.0 + value * (1.0 - sig))


def inner_rows(left, right):
    return lax.dot_general(
        left, right, (((0,), (0,)), ((), ())), preferred_element_type=jnp.float32
    )


def block_classes():
    found = {}
    pairs = []
    where = {}
    for a in range(9):
        for b in range(9):
            first, second, flip = a, b, False
            dy, dx = b // 3 - a // 3, b % 3 - a % 3
            if dy < 0 or (dy == 0 and dx < 0):
                first, second, flip = b, a, True
                dy, dx = -dy, -dx
            key = (dy, dx, first // 3 if dy == 0 else -1, first % 3 if dx == 0 else -1)
            if key not in found:
                found[key] = len(pairs)
                pairs.append((first, second))
            where[a, b] = (found[key], flip)
    return pairs, where


PAIRS, WHERE = block_classes()
NG = len(PAIRS)
HALF_G = 15
HALF_D = 5
HALF = HALF_G + HALF_D
SMEM = pl.BlockSpec(memory_space=pltpu.SMEM)
VMEM = pl.BlockSpec(memory_space=pltpu.VMEM)


def halo_rows(f, top):
    def kernel(f_ref, top_ref, up_ref, down_ref):
        for ref, edge in ((up_ref, 0), (down_ref, 1)):
            ref[0:2] = f_ref[3]
            ref[2] = f_ref[2, edge]
            ref[3] = f_ref[0, edge]
            ref[4] = top_ref[edge]
        up_ref[5:7] = f_ref[1]

    row = f.shape[2:]
    return pl.pallas_call(
        kernel,
        out_shape=(
            jax.ShapeDtypeStruct((7,) + row, f.dtype),
            jax.ShapeDtypeStruct((5,) + row, f.dtype),
        ),
        in_specs=[VMEM, VMEM],
        out_specs=(VMEM, VMEM),
        cost_estimate=pl.CostEstimate(flops=0, bytes_accessed=10**6, transcendentals=0),
    )(f, top)


def gram_half(cols, core):
    chans = cols.shape[1] // 9

    def kernel(core_ref, cols_ref, out_ref):
        def some(mine):
            for a in sorted({first for first, _ in mine}):
                wanted = [b for first, b in mine if first == a]
                low = min(wanted)
                left = cols_ref[:, a * chans : (a + 1) * chans].T
                right = cols_ref[:, low * chans : (max(wanted) + 1) * chans]
                product = jnp.dot(left, right, preferred_element_type=jnp.float32)
                for b in wanted:
                    i = mine.index((a, b))
                    part = product[:, (b - low) * chans : (b - low + 1) * chans]
                    out_ref[i * chans : (i + 1) * chans, :] = part.astype(out_ref.dtype)
            for i in range(len(mine), HALF_G):
                out_ref[i * chans : (i + 1) * chans, :] = jnp.zeros((chans, chans), out_ref.dtype)

        @pl.when(core_ref[0] == 0)
        def _():
            some(PAIRS[:HALF_G])

        @pl.when(core_ref[0] != 0)
        def _():
            some(PAIRS[HALF_G:])

    return pl.pallas_call(
        kernel,
        out_shape=jax.ShapeDtypeStruct((HALF_G * chans, chans), jnp.bfloat16),
        in_specs=[SMEM, VMEM],
        out_specs=VMEM,
        compiler_params=pltpu.CompilerParams(vmem_limit_bytes=24 * 2**20),
        cost_estimate=pl.CostEstimate(
            flops=2 * HALF * cols.shape[0] * chans * chans,
            bytes_accessed=5 * 10**6,
            transcendentals=0,
        ),
    )(core.reshape(1), cols)


def all_half(gram, cols, dpre, core):
    chans = dpre.shape[-1]

    def kernel(core_ref, gram_ref, cols_ref, dpre_ref, out_ref):
        out_ref[: HALF_G * chans, :] = gram_ref[...]

        def put(i, value):
            out_ref[(HALF_G + i) * chans : (HALF_G + i + 1) * chans, :] = value.astype(out_ref.dtype)

        def some(first, last, own):
            turned = dpre_ref[...].T
            right = cols_ref[:, first * chans : last * chans]
            grad = jnp.dot(turned, right, preferred_element_type=jnp.float32)
            for i in range(last - first):
                put(i, grad[:, i * chans : (i + 1) * chans].T)
            if own:
                put(last - first, jnp.dot(turned, dpre_ref[...], preferred_element_type=jnp.float32))

        @pl.when(core_ref[0] == 0)
        def _():
            some(0, HALF_D, False)

        @pl.when(core_ref[0] != 0)
        def _():
            some(HALF_D, 9, True)

    return pl.pallas_call(
        kernel,
        out_shape=jax.ShapeDtypeStruct((HALF * chans, chans), jnp.bfloat16),
        in_specs=[SMEM, VMEM, VMEM, VMEM],
        out_specs=VMEM,
        compiler_params=pltpu.CompilerParams(vmem_limit_bytes=24 * 2**20),
        cost_estimate=pl.CostEstimate(
            flops=2 * HALF_D * cols.shape[0] * chans * chans,
            bytes_accessed=5 * 10**6,
            transcendentals=0,
        ),
    )(core.reshape(1), gram, cols, dpre)


def factor_rows(blocks, first_row, scale, rows):
    chans = blocks.shape[-1]
    slots = [i // HALF_G * HALF + i % HALF_G for i in range(NG)]
    index = jnp.array([slots[WHERE[a, b][0]] for a in range(9) for b in range(9)], jnp.int32)
    flips = jnp.array([int(WHERE[a, b][1]) for a in range(9) for b in range(9)], jnp.int32)

    def kernel(index_ref, flip_ref, row_ref, scale_ref, blocks_ref, out_ref, band):
        start = row_ref[0]
        tap = lax.div(start, chans)
        for t in range(2):
            a = jnp.minimum(tap + t, 8)
            for b in range(9):
                block = blocks_ref[index_ref[a * 9 + b]].astype(jnp.float32)
                flip = flip_ref[a * 9 + b] != 0
                band[t * chans : (t + 1) * chans, b * chans : (b + 1) * chans] = jnp.where(
                    flip, block.T, block
                )
        inside = start - tap * chans
        base = pl.multiple_of(lax.div(inside, 8) * 8, 8)
        got = band[pl.ds(base, rows + 4), :]
        odd = inside != base
        out_ref[...] = jnp.where(odd, got[4:], got[:rows]) * scale_ref[0]

    return pl.pallas_call(
        kernel,
        out_shape=jax.ShapeDtypeStruct((rows, 9 * chans), jnp.float32),
        in_specs=[SMEM, SMEM, SMEM, SMEM, VMEM],
        out_specs=VMEM,
        scratch_shapes=[pltpu.VMEM((2 * chans, 9 * chans), jnp.float32)],
        compiler_params=pltpu.CompilerParams(vmem_limit_bytes=16 * 2**20),
        cost_estimate=pl.CostEstimate(flops=10**6, bytes_accessed=2 * 10**6, transcendentals=0),
    )(index, flips, first_row.reshape(1), scale.reshape(1), blocks)


def shards(feats, top_grad, weights, table, a_inv, g_inv):
    num_layers, _, rows_dev, width, chans = feats.shape
    owners = lax.axis_size(OWNER)
    samples = lax.axis_size(DP)
    owner_id = lax.axis_index(OWNER)
    dp_id = lax.axis_index(DP)
    y_id = lax.axis_index("y")
    z_id = lax.axis_index("zh")
    npos = samples * rows_dev * owners * width
    patch = 9 * chans
    inner = owner_id < owners - 1
    f = feats[:, 0]
    top = top_grad[0]

    to_above, to_below = halo_rows(f, top)
    below = shifted(to_above, -1, True)
    above = shifted(to_below, 1, False)
    below1 = below[5:]
    below = jnp.where(inner, below[:5], jnp.zeros_like(below[:5]))
    wide3 = jnp.concatenate([above[:2], f[3], below[:2]])
    strips = [
        jnp.concatenate([above[3:4], f[0], below[3:4]]),
        jnp.concatenate([f[1], below1]),
        jnp.concatenate([above[2:3], f[2], below[2:3]]),
        wide3[1:5],
    ]
    core_id = lax.axis_index("core")

    def to_layers(x):
        return exchange(jnp.broadcast_to(x[None], (CORE,) + x.shape).reshape((-1,) + x.shape[1:]), ("core", "y"))

    flipped = jnp.transpose(weights.reshape(num_layers, 9, chans, chans), (0, 1, 3, 2)).reshape(
        num_layers, patch, chans
    )

    def slope(layer, win):
        pre = jnp.dot(to_columns(win), weights[layer], preferred_element_type=jnp.float32)
        return silu_slope(pre)

    def times(grad_in, slopes):
        return (grad_in.reshape(slopes.shape).astype(jnp.float32) * slopes).astype(jnp.bfloat16)

    def back(layer, win):
        return jnp.dot(
            back_columns(win), flipped[layer], preferred_element_type=jnp.float32
        ).astype(jnp.bfloat16)

    image = (rows_dev, width, chans)
    top_wide = jnp.concatenate([above[4:5], top, below[4:5]])
    dpre3 = times(top_wide, slope(3, windows(wide3))).reshape((rows_dev + 2, width, chans))
    dpre2 = times(back(3, windows(dpre3)), slope(2, windows(strips[2]))).reshape(image)
    after = shifted(dpre2, -1, True)
    dy1 = back(2, cut_windows(jnp.concatenate([dpre2, after]), inner))
    dpre1 = times(dy1, slope(1, cut_windows(strips[1], inner))).reshape(image)
    stacked, dpre1 = lax.optimization_barrier((jnp.stack(strips), dpre1))
    before = shifted(dpre1, 1, True)
    layer_strips = to_layers(stacked)
    edge_top = jnp.where(owner_id > 0, before[:1], jnp.zeros_like(before[:1]))
    edge_end = jnp.where(inner, dpre1[1:], jnp.zeros_like(dpre1[1:]))
    dy0 = back(1, windows(jnp.concatenate([edge_top, before[1:], dpre1[:1], edge_end])))
    dpre0 = times(dy0, slope(0, windows(strips[0]))).reshape(image)

    last_one = (y_id == 1) & (z_id == ZH - 1)
    cols = jnp.concatenate(
        [
            to_columns(
                windows(layer_strips[j])
                if j % Y < Y - 1
                else cut_windows(layer_strips[j], jnp.logical_not(last_one))
            )
            for j in range(CORE * Y)
        ]
    )
    gram = gram_half(cols, core_id)
    layer_dpre = to_layers(jnp.stack([dpre0, dpre1, dpre2, dpre3[1:3]]))
    parts = all_half(gram, cols, layer_dpre.reshape(-1, chans), core_id)

    piece = scatter_sum(parts, ("x", "zl"))
    held = spread(piece, "y")
    layer_ids = jnp.arange(num_layers, dtype=jnp.int32)

    def pick(z):
        lay = jnp.sum(jnp.where(table == z * Y + y_id, layer_ids, 0))
        return lax.dynamic_index_in_dim(held, lay, 0, keepdims=False)

    total = exchange(jnp.stack([pick(z) for z in range(ZH)]), "zh")
    total = jnp.sum(total.astype(jnp.float32), axis=0).astype(jnp.bfloat16)
    summed = spread(spread(spread(total, "zl"), "x"), "core")

    in_grad_win = jnp.concatenate([shifted(dpre0[1:], 1, False), dpre0, shifted(dpre0[:1], -1, False)])
    in_grad = back(0, windows(in_grad_win)).reshape((1,) + image)

    summed = summed.reshape(CORE, HALF * chans, chans)
    grad_sum = jnp.concatenate(
        [summed[0, HALF_G * chans :], summed[1, HALF_G * chans : (HALF - 1) * chans]]
    )
    grad_scaled = grad_sum.astype(jnp.float32) / jnp.sqrt(jnp.float32(npos))
    mixed = jnp.dot(grad_scaled, g_inv[0], precision=lax.Precision.HIGHEST)
    panel = jnp.dot(a_inv[0].astype(jnp.float32), mixed, precision=lax.Precision.HIGHEST)
    panels = spread(spread(panel.astype(jnp.bfloat16), "zh"), "y")
    step_out = panels[table % Y, table // Y]

    stats = summed.reshape(-1, chans, chans)
    have = jnp.any(table == owner_id).astype(jnp.float32)
    scale = have / npos
    rows_out = patch // samples
    a_out = factor_rows(stats, dp_id * rows_out, scale, rows_out)[None]
    g_out = (stats[-1].astype(jnp.float32) * scale)[None]
    return (step_out, a_out, g_out, in_grad)


def solution(mesh):
    fine = Mesh(mesh.devices.reshape(X, ZL, CORE, ZH, Y), DP + OWNER)
    placed = (
        P(None, DP, OWNER, None, None),
        P(DP, OWNER, None, None),
        P(),
        P(),
        P(OWNER, DP, None),
        P(OWNER, None, None),
    )
    return jax.shard_map(
        shards,
        mesh=fine,
        in_specs=placed,
        out_specs=(
            P(None, DP, None),
            P(OWNER, DP, None),
            P(OWNER, None, None),
            P(DP, OWNER, None, None),
        ),
        check_vma=False,
    )
```

```python
import jax
import jax.numpy as jnp
from jax import lax
from jax.experimental import pallas as pl
from jax.experimental.pallas import tpu as pltpu
from jax.sharding import Mesh, PartitionSpec as P

X, ZL, CORE, ZH, Y = 4, 4, 2, 4, 4
OWNER = ("zh", "y")
DP = ("x", "zl", "core")


def shifted(x, shift, cyclic):
    count = ZH * Y
    pairs = [(i, (i + shift) % count) for i in range(count)]
    if not cyclic:
        pairs = [(a, b) for a, b in pairs if b - a == shift]
    return lax.ppermute(x, OWNER, pairs)


def paired(x, axis, step):
    return lax.ppermute(x, axis, [(i, i ^ 1 if step == 0 else 3 - i) for i in range(4)])


def exchange(x, axis):
    return lax.all_to_all(x, axis, split_axis=0, concat_axis=0, tiled=True)


def spread(x, axis):
    count = lax.axis_size(axis)
    return exchange(jnp.broadcast_to(x[None], (count,) + x.shape), axis)


def scatter_sum(x, axis):
    count = lax.axis_size(axis)
    got = exchange(x.reshape((count, x.shape[0] // count) + x.shape[1:]), axis)
    return jnp.sum(got.astype(jnp.float32), axis=0).astype(jnp.bfloat16)


def windows(rows):
    rows = jnp.pad(rows, ((0, 0), (1, 1), (0, 0)))
    return jnp.stack([rows[i : i + 3] for i in range(rows.shape[0] - 2)])


def cut_windows(rows, whole):
    first, second = rows[:3], rows[1:]
    first = jnp.where(whole, first, first * jnp.array([1, 1, 0], rows.dtype)[:, None, None])
    second = jnp.where(whole, second, second * jnp.array([0, 1, 1], rows.dtype)[:, None, None])
    return jnp.pad(jnp.stack([first, second]), ((0, 0), (0, 0), (1, 1), (0, 0)))


def to_columns(win):
    width = win.shape[2] - 2
    taps = [win[:, ky, kx : kx + width] for ky in range(3) for kx in range(3)]
    return jnp.concatenate(taps, axis=-1).reshape(-1, 9 * win.shape[-1])


def back_columns(win):
    width = win.shape[2] - 2
    taps = [win[:, 2 - ky, 2 - kx : 2 - kx + width] for ky in range(3) for kx in range(3)]
    return jnp.concatenate(taps, axis=-1).reshape(-1, 9 * win.shape[-1])


def silu_slope(value):
    sig = jax.nn.sigmoid(value)
    return sig * (1.0 + value * (1.0 - sig))


def inner_rows(left, right):
    return lax.dot_general(
        left, right, (((0,), (0,)), ((), ())), preferred_element_type=jnp.float32
    )


def block_classes():
    found = {}
    pairs = []
    where = {}
    for a in range(9):
        for b in range(9):
            first, second, flip = a, b, False
            dy, dx = b // 3 - a // 3, b % 3 - a % 3
            if dy < 0 or (dy == 0 and dx < 0):
                first, second, flip = b, a, True
                dy, dx = -dy, -dx
            key = (dy, dx, first // 3 if dy == 0 else -1, first % 3 if dx == 0 else -1)
            if key not in found:
                found[key] = len(pairs)
                pairs.append((first, second))
            where[a, b] = (found[key], flip)
    return pairs, where


PAIRS, WHERE = block_classes()
NG = len(PAIRS)
HALF_G = 16
HALF_D = 5
FAC_ROWS = 128
GRAD_ROWS = 40
PIECE_ROWS = 176
SMEM = pl.BlockSpec(memory_space=pltpu.SMEM)
VMEM = pl.BlockSpec(memory_space=pltpu.VMEM)


def halo_rows(f, top):
    def kernel(f_ref, top_ref, up_ref, down_ref):
        for ref, edge in ((up_ref, 0), (down_ref, 1)):
            ref[0:2] = f_ref[3]
            ref[2] = f_ref[2, edge]
            ref[3] = f_ref[0, edge]
            ref[4] = top_ref[edge]
        up_ref[5:7] = f_ref[1]

    row = f.shape[2:]
    return pl.pallas_call(
        kernel,
        out_shape=(
            jax.ShapeDtypeStruct((7,) + row, f.dtype),
            jax.ShapeDtypeStruct((5,) + row, f.dtype),
        ),
        in_specs=[VMEM, VMEM],
        out_specs=(VMEM, VMEM),
        cost_estimate=pl.CostEstimate(flops=0, bytes_accessed=10**6, transcendentals=0),
    )(f, top)


def gram_half(cols, core):
    chans = cols.shape[1] // 9

    def kernel(core_ref, cols_ref, out_ref):
        def some(mine):
            for a in sorted({first for first, _ in mine}):
                wanted = [b for first, b in mine if first == a]
                low = min(wanted)
                left = cols_ref[:, a * chans : (a + 1) * chans].T
                right = cols_ref[:, low * chans : (max(wanted) + 1) * chans]
                product = jnp.dot(left, right, preferred_element_type=jnp.float32)
                for b in wanted:
                    i = mine.index((a, b))
                    part = product[:, (b - low) * chans : (b - low + 1) * chans]
                    out_ref[i * chans : (i + 1) * chans, :] = part.astype(out_ref.dtype)
            for i in range(len(mine), HALF_G):
                out_ref[i * chans : (i + 1) * chans, :] = jnp.zeros((chans, chans), out_ref.dtype)

        @pl.when(core_ref[0] == 0)
        def _():
            some(PAIRS[:HALF_G])

        @pl.when(core_ref[0] != 0)
        def _():
            some(PAIRS[HALF_G:])

    return pl.pallas_call(
        kernel,
        out_shape=jax.ShapeDtypeStruct((HALF_G * chans, chans), jnp.bfloat16),
        in_specs=[SMEM, VMEM],
        out_specs=VMEM,
        compiler_params=pltpu.CompilerParams(vmem_limit_bytes=24 * 2**20),
        cost_estimate=pl.CostEstimate(
            flops=2 * (HALF_G + HALF_D) * cols.shape[0] * chans * chans,
            bytes_accessed=5 * 10**6,
            transcendentals=0,
        ),
    )(core.reshape(1), cols)


def all_half(gram, cols, dpre, core):
    chans = dpre.shape[-1]

    def kernel(core_ref, gram_ref, cols_ref, dpre_ref, out_ref, dense):
        for k in range(HALF_G):
            out_ref[k, :FAC_ROWS, :] = gram_ref[k * chans : (k + 1) * chans, :]
        dense[...] = jnp.zeros(dense.shape, dense.dtype)

        def some(first, last):
            turned = dpre_ref[...].T
            right = cols_ref[:, first * chans : last * chans]
            grad = jnp.dot(turned, right, preferred_element_type=jnp.float32)
            for i in range(last - first):
                dense[i * chans : (i + 1) * chans, :] = grad[:, i * chans : (i + 1) * chans].T
            return turned

        @pl.when(core_ref[0] == 0)
        def _():
            some(0, HALF_D)

        @pl.when(core_ref[0] != 0)
        def _():
            turned = some(HALF_D, 9)
            own = jnp.dot(turned, dpre_ref[...], preferred_element_type=jnp.float32)
            out_ref[NG - HALF_G, :FAC_ROWS, :] = own.astype(out_ref.dtype)

        for k in range(HALF_G):
            rows = dense[k * GRAD_ROWS : k * GRAD_ROWS + PIECE_ROWS - FAC_ROWS, :]
            out_ref[k, FAC_ROWS:, :] = rows.astype(out_ref.dtype)

    return pl.pallas_call(
        kernel,
        out_shape=jax.ShapeDtypeStruct((HALF_G, PIECE_ROWS, chans), jnp.bfloat16),
        in_specs=[SMEM, VMEM, VMEM, VMEM],
        out_specs=VMEM,
        scratch_shapes=[pltpu.VMEM((HALF_D * chans + 16, chans), jnp.float32)],
        compiler_params=pltpu.CompilerParams(vmem_limit_bytes=24 * 2**20),
        cost_estimate=pl.CostEstimate(
            flops=2 * HALF_D * cols.shape[0] * chans * chans,
            bytes_accessed=5 * 10**6,
            transcendentals=0,
        ),
    )(core.reshape(1), gram, cols, dpre)


def factor_rows(blocks, first_row, scale, rows):
    chans = blocks.shape[-1]
    index = jnp.array([WHERE[a, b][0] for a in range(9) for b in range(9)], jnp.int32)
    flips = jnp.array([int(WHERE[a, b][1]) for a in range(9) for b in range(9)], jnp.int32)

    def kernel(index_ref, flip_ref, row_ref, scale_ref, blocks_ref, out_ref, band):
        start = row_ref[0]
        tap = lax.div(start, chans)
        for t in range(2):
            a = jnp.minimum(tap + t, 8)
            for b in range(9):
                block = blocks_ref[index_ref[a * 9 + b], :chans, :].astype(jnp.float32)
                flip = flip_ref[a * 9 + b] != 0
                band[t * chans : (t + 1) * chans, b * chans : (b + 1) * chans] = jnp.where(
                    flip, block.T, block
                )
        inside = start - tap * chans
        base = pl.multiple_of(lax.div(inside, 8) * 8, 8)
        got = band[pl.ds(base, rows + 4), :]
        odd = inside != base
        out_ref[...] = jnp.where(odd, got[4:], got[:rows]) * scale_ref[0]

    return pl.pallas_call(
        kernel,
        out_shape=jax.ShapeDtypeStruct((rows, 9 * chans), jnp.float32),
        in_specs=[SMEM, SMEM, SMEM, SMEM, VMEM],
        out_specs=VMEM,
        scratch_shapes=[pltpu.VMEM((2 * chans, 9 * chans), jnp.float32)],
        compiler_params=pltpu.CompilerParams(vmem_limit_bytes=16 * 2**20),
        cost_estimate=pl.CostEstimate(flops=10**6, bytes_accessed=2 * 10**6, transcendentals=0),
    )(index, flips, first_row.reshape(1), scale.reshape(1), blocks)


def shards(feats, top_grad, weights, table, a_inv, g_inv):
    num_layers, _, rows_dev, width, chans = feats.shape
    owners = lax.axis_size(OWNER)
    samples = lax.axis_size(DP)
    owner_id = lax.axis_index(OWNER)
    dp_id = lax.axis_index(DP)
    y_id = lax.axis_index("y")
    z_id = lax.axis_index("zh")
    npos = samples * rows_dev * owners * width
    patch = 9 * chans
    inner = owner_id < owners - 1
    f = feats[:, 0]
    top = top_grad[0]

    to_above, to_below = halo_rows(f, top)
    below = shifted(to_above, -1, True)
    above = shifted(to_below, 1, False)
    below1 = below[5:]
    below = jnp.where(inner, below[:5], jnp.zeros_like(below[:5]))
    wide3 = jnp.concatenate([above[:2], f[3], below[:2]])
    strips = [
        jnp.concatenate([above[3:4], f[0], below[3:4]]),
        jnp.concatenate([f[1], below1]),
        jnp.concatenate([above[2:3], f[2], below[2:3]]),
        wide3[1:5],
    ]
    core_id = lax.axis_index("core")

    def to_layers(x):
        return exchange(jnp.broadcast_to(x[None], (CORE,) + x.shape).reshape((-1,) + x.shape[1:]), ("core", "y"))

    flipped = jnp.transpose(weights.reshape(num_layers, 9, chans, chans), (0, 1, 3, 2)).reshape(
        num_layers, patch, chans
    )

    def slope(layer, win):
        pre = jnp.dot(to_columns(win), weights[layer], preferred_element_type=jnp.float32)
        return silu_slope(pre)

    def times(grad_in, slopes):
        return (grad_in.reshape(slopes.shape).astype(jnp.float32) * slopes).astype(jnp.bfloat16)

    def back(layer, win):
        return jnp.dot(
            back_columns(win), flipped[layer], preferred_element_type=jnp.float32
        ).astype(jnp.bfloat16)

    image = (rows_dev, width, chans)
    top_wide = jnp.concatenate([above[4:5], top, below[4:5]])
    dpre3 = times(top_wide, slope(3, windows(wide3))).reshape((rows_dev + 2, width, chans))
    dpre2 = times(back(3, windows(dpre3)), slope(2, windows(strips[2]))).reshape(image)
    after = shifted(dpre2, -1, True)
    dy1 = back(2, cut_windows(jnp.concatenate([dpre2, after]), inner))
    dpre1 = times(dy1, slope(1, cut_windows(strips[1], inner))).reshape(image)
    local = jnp.concatenate([a_inv.reshape(-1, chans), g_inv[0].astype(jnp.bfloat16)])
    stacked, dpre1, local = lax.optimization_barrier((jnp.stack(strips), dpre1, local))
    before = shifted(dpre1, 1, True)
    layer_strips = to_layers(stacked)
    near = paired(local, "y", 0)
    edge_top = jnp.where(owner_id > 0, before[:1], jnp.zeros_like(before[:1]))
    edge_end = jnp.where(inner, dpre1[1:], jnp.zeros_like(dpre1[1:]))
    dy0 = back(1, windows(jnp.concatenate([edge_top, before[1:], dpre1[:1], edge_end])))
    dpre0 = times(dy0, slope(0, windows(strips[0]))).reshape(image)

    last_one = (y_id == 1) & (z_id == ZH - 1)
    cols = jnp.concatenate(
        [
            to_columns(
                windows(layer_strips[j])
                if j % Y < Y - 1
                else cut_windows(layer_strips[j], jnp.logical_not(last_one))
            )
            for j in range(CORE * Y)
        ]
    )
    gram = gram_half(cols, core_id)
    layer_dpre = to_layers(jnp.stack([dpre0, dpre1, dpre2, dpre3[1:3]]))
    parts = all_half(gram, cols, layer_dpre.reshape(-1, chans), core_id)

    parts, local, near = lax.optimization_barrier((parts, local, near))
    from_y, from_z = table % Y, table // Y
    far = paired(jnp.where(from_y[3 - y_id] == y_id, local, near), "y", 1)
    want = from_y[y_id]
    found = jnp.where(want == y_id, local, jnp.where(want == (y_id ^ 1), near, far))
    want = from_z[y_id]
    found = jnp.where(want == (z_id ^ 1), paired(found, "zh", 0), found)

    piece = scatter_sum(parts, ("x", "zl"))
    piece, found = lax.optimization_barrier((piece, found))
    inverses = jnp.where(want // 2 == z_id // 2, found, paired(found, "zh", 1))
    held = spread(piece[:, :FAC_ROWS], "y")
    layer_ids = jnp.arange(num_layers, dtype=jnp.int32)

    def pick(z):
        lay = jnp.sum(jnp.where(table == z * Y + y_id, layer_ids, 0))
        fac = lax.dynamic_index_in_dim(held, lay, 0, keepdims=False)
        return jnp.concatenate([fac, piece[:, FAC_ROWS:]], axis=1)

    total = exchange(jnp.stack([pick(z) for z in range(ZH)]), "zh")
    total = jnp.sum(total.astype(jnp.float32), axis=0).astype(jnp.bfloat16)
    summed = spread(spread(spread(total, "zl"), "x"), "core")

    in_grad_win = jnp.concatenate([shifted(dpre0[1:], 1, False), dpre0, shifted(dpre0[:1], -1, False)])
    in_grad = back(0, windows(in_grad_win)).reshape((1,) + image)

    stats = summed.reshape(CORE * HALF_G, PIECE_ROWS, chans)
    grad_sum = stats[:, FAC_ROWS : FAC_ROWS + GRAD_ROWS].reshape(-1, chans)[:patch]
    rows_out = patch // samples
    a_mine = inverses[: rows_out * 9].reshape(rows_out, patch)
    mixed = jnp.dot(grad_sum, inverses[rows_out * 9 :], preferred_element_type=jnp.float32)
    mixed = mixed / jnp.sqrt(jnp.float32(npos))
    panel = jnp.dot(a_mine.astype(jnp.float32), mixed, precision=lax.Precision.HIGHEST)
    step_out = spread(panel.astype(jnp.bfloat16), "y")

    have = jnp.any(table == owner_id).astype(jnp.float32)
    scale = have / npos
    a_out = factor_rows(stats, dp_id * rows_out, scale, rows_out)[None]
    g_out = (stats[NG, :FAC_ROWS].astype(jnp.float32) * scale)[None]
    return (step_out, a_out, g_out, in_grad)


def solution(mesh):
    fine = Mesh(mesh.devices.reshape(X, ZL, CORE, ZH, Y), DP + OWNER)
    placed = (
        P(None, DP, OWNER, None, None),
        P(DP, OWNER, None, None),
        P(),
        P(),
        P(OWNER, DP, None),
        P(OWNER, None, None),
    )
    return jax.shard_map(
        shards,
        mesh=fine,
        in_specs=placed,
        out_specs=(
            P(None, DP, None),
            P(OWNER, DP, None),
            P(OWNER, None, None),
            P(DP, OWNER, None, None),
        ),
        check_vma=False,
    )
```

```python
import jax
import jax.numpy as jnp
from jax import lax
from jax.experimental import pallas as pl
from jax.experimental.pallas import tpu as pltpu
from jax.sharding import Mesh, PartitionSpec as P

X, ZL, CORE, ZH, Y = 4, 4, 2, 4, 4
OWNER = ("zh", "y")
DP = ("x", "zl", "core")


def shifted(x, shift, cyclic):
    count = ZH * Y
    pairs = [(i, (i + shift) % count) for i in range(count)]
    if not cyclic:
        pairs = [(a, b) for a, b in pairs if b - a == shift]
    return lax.ppermute(x, OWNER, pairs)


def paired(x, axis, step):
    return lax.ppermute(x, axis, [(i, i ^ 1 if step == 0 else 3 - i) for i in range(4)])


def exchange(x, axis):
    return lax.all_to_all(x, axis, split_axis=0, concat_axis=0, tiled=True)


def spread(x, axis):
    count = lax.axis_size(axis)
    return exchange(jnp.broadcast_to(x[None], (count,) + x.shape), axis)


def scatter_sum(x, axis):
    count = lax.axis_size(axis)
    got = exchange(x.reshape((count, x.shape[0] // count) + x.shape[1:]), axis)
    return jnp.sum(got.astype(jnp.float32), axis=0).astype(jnp.bfloat16)


def windows(rows):
    rows = jnp.pad(rows, ((0, 0), (1, 1), (0, 0)))
    return jnp.stack([rows[i : i + 3] for i in range(rows.shape[0] - 2)])


def cut_windows(rows, whole):
    first, second = rows[:3], rows[1:]
    first = jnp.where(whole, first, first * jnp.array([1, 1, 0], rows.dtype)[:, None, None])
    second = jnp.where(whole, second, second * jnp.array([0, 1, 1], rows.dtype)[:, None, None])
    return jnp.pad(jnp.stack([first, second]), ((0, 0), (0, 0), (1, 1), (0, 0)))


def to_columns(win):
    width = win.shape[2] - 2
    taps = [win[:, ky, kx : kx + width] for ky in range(3) for kx in range(3)]
    return jnp.concatenate(taps, axis=-1).reshape(-1, 9 * win.shape[-1])


def back_columns(win):
    width = win.shape[2] - 2
    taps = [win[:, 2 - ky, 2 - kx : 2 - kx + width] for ky in range(3) for kx in range(3)]
    return jnp.concatenate(taps, axis=-1).reshape(-1, 9 * win.shape[-1])


def silu_slope(value):
    sig = jax.nn.sigmoid(value)
    return sig * (1.0 + value * (1.0 - sig))


def inner_rows(left, right):
    return lax.dot_general(
        left, right, (((0,), (0,)), ((), ())), preferred_element_type=jnp.float32
    )


def block_classes():
    found = {}
    pairs = []
    where = {}
    for a in range(9):
        for b in range(9):
            first, second, flip = a, b, False
            dy, dx = b // 3 - a // 3, b % 3 - a % 3
            if dy < 0 or (dy == 0 and dx < 0):
                first, second, flip = b, a, True
                dy, dx = -dy, -dx
            key = (dy, dx, first // 3 if dy == 0 else -1, first % 3 if dx == 0 else -1)
            if key not in found:
                found[key] = len(pairs)
                pairs.append((first, second))
            where[a, b] = (found[key], flip)
    return pairs, where


PAIRS, WHERE = block_classes()
NG = len(PAIRS)
HALF_G = 16
HALF_D = 5
FAC_ROWS = 128
GRAD_ROWS = 40
PIECE_ROWS = 176
SMEM = pl.BlockSpec(memory_space=pltpu.SMEM)
VMEM = pl.BlockSpec(memory_space=pltpu.VMEM)


def halo_rows(f, top):
    def kernel(f_ref, top_ref, up_ref, down_ref):
        for ref, edge in ((up_ref, 0), (down_ref, 1)):
            ref[0:2] = f_ref[3]
            ref[2] = f_ref[2, edge]
            ref[3] = f_ref[0, edge]
            ref[4] = top_ref[edge]
        up_ref[5:7] = f_ref[1]

    row = f.shape[2:]
    return pl.pallas_call(
        kernel,
        out_shape=(
            jax.ShapeDtypeStruct((7,) + row, f.dtype),
            jax.ShapeDtypeStruct((5,) + row, f.dtype),
        ),
        in_specs=[VMEM, VMEM],
        out_specs=(VMEM, VMEM),
        cost_estimate=pl.CostEstimate(flops=0, bytes_accessed=10**6, transcendentals=0),
    )(f, top)


def gram_half(cols, core):
    chans = cols.shape[1] // 9

    def kernel(core_ref, cols_ref, out_ref):
        def some(mine):
            for a in sorted({first for first, _ in mine}):
                wanted = [b for first, b in mine if first == a]
                low = min(wanted)
                left = cols_ref[:, a * chans : (a + 1) * chans].T
                right = cols_ref[:, low * chans : (max(wanted) + 1) * chans]
                product = jnp.dot(left, right, preferred_element_type=jnp.float32)
                for b in wanted:
                    i = mine.index((a, b))
                    part = product[:, (b - low) * chans : (b - low + 1) * chans]
                    out_ref[i * chans : (i + 1) * chans, :] = part.astype(out_ref.dtype)
            for i in range(len(mine), HALF_G):
                out_ref[i * chans : (i + 1) * chans, :] = jnp.zeros((chans, chans), out_ref.dtype)

        @pl.when(core_ref[0] == 0)
        def _():
            some(PAIRS[:HALF_G])

        @pl.when(core_ref[0] != 0)
        def _():
            some(PAIRS[HALF_G:])

    return pl.pallas_call(
        kernel,
        out_shape=jax.ShapeDtypeStruct((HALF_G * chans, chans), jnp.bfloat16),
        in_specs=[SMEM, VMEM],
        out_specs=VMEM,
        compiler_params=pltpu.CompilerParams(vmem_limit_bytes=24 * 2**20),
        cost_estimate=pl.CostEstimate(
            flops=2 * (HALF_G + HALF_D) * cols.shape[0] * chans * chans,
            bytes_accessed=5 * 10**6,
            transcendentals=0,
        ),
    )(core.reshape(1), cols)


def all_half(gram, cols, dpre, core):
    chans = dpre.shape[-1]

    def kernel(core_ref, gram_ref, cols_ref, dpre_ref, out_ref, dense):
        for k in range(HALF_G):
            out_ref[k, :FAC_ROWS, :] = gram_ref[k * chans : (k + 1) * chans, :]
        dense[...] = jnp.zeros(dense.shape, dense.dtype)

        def some(first, last):
            turned = dpre_ref[...].T
            right = cols_ref[:, first * chans : last * chans]
            grad = jnp.dot(turned, right, preferred_element_type=jnp.float32)
            for i in range(last - first):
                dense[i * chans : (i + 1) * chans, :] = grad[:, i * chans : (i + 1) * chans].T
            return turned

        @pl.when(core_ref[0] == 0)
        def _():
            some(0, HALF_D)

        @pl.when(core_ref[0] != 0)
        def _():
            turned = some(HALF_D, 9)
            own = jnp.dot(turned, dpre_ref[...], preferred_element_type=jnp.float32)
            out_ref[NG - HALF_G, :FAC_ROWS, :] = own.astype(out_ref.dtype)

        for k in range(HALF_G):
            rows = dense[k * GRAD_ROWS : k * GRAD_ROWS + PIECE_ROWS - FAC_ROWS, :]
            out_ref[k, FAC_ROWS:, :] = rows.astype(out_ref.dtype)

    return pl.pallas_call(
        kernel,
        out_shape=jax.ShapeDtypeStruct((HALF_G, PIECE_ROWS, chans), jnp.bfloat16),
        in_specs=[SMEM, VMEM, VMEM, VMEM],
        out_specs=VMEM,
        scratch_shapes=[pltpu.VMEM((HALF_D * chans + 16, chans), jnp.float32)],
        compiler_params=pltpu.CompilerParams(vmem_limit_bytes=24 * 2**20),
        cost_estimate=pl.CostEstimate(
            flops=2 * HALF_D * cols.shape[0] * chans * chans,
            bytes_accessed=5 * 10**6,
            transcendentals=0,
        ),
    )(core.reshape(1), gram, cols, dpre)


def factor_rows(blocks, first_row, scale, rows):
    chans = blocks.shape[-1]
    index = jnp.array([WHERE[a, b][0] for a in range(9) for b in range(9)], jnp.int32)
    flips = jnp.array([int(WHERE[a, b][1]) for a in range(9) for b in range(9)], jnp.int32)

    def kernel(index_ref, flip_ref, row_ref, scale_ref, blocks_ref, out_ref, band):
        start = row_ref[0]
        tap = lax.div(start, chans)
        for t in range(2):
            a = jnp.minimum(tap + t, 8)
            for b in range(9):
                block = blocks_ref[index_ref[a * 9 + b], :chans, :].astype(jnp.float32)
                flip = flip_ref[a * 9 + b] != 0
                band[t * chans : (t + 1) * chans, b * chans : (b + 1) * chans] = jnp.where(
                    flip, block.T, block
                )
        inside = start - tap * chans
        base = pl.multiple_of(lax.div(inside, 8) * 8, 8)
        got = band[pl.ds(base, rows + 4), :]
        odd = inside != base
        out_ref[...] = jnp.where(odd, got[4:], got[:rows]) * scale_ref[0]

    return pl.pallas_call(
        kernel,
        out_shape=jax.ShapeDtypeStruct((rows, 9 * chans), jnp.float32),
        in_specs=[SMEM, SMEM, SMEM, SMEM, VMEM],
        out_specs=VMEM,
        scratch_shapes=[pltpu.VMEM((2 * chans, 9 * chans), jnp.float32)],
        compiler_params=pltpu.CompilerParams(vmem_limit_bytes=16 * 2**20),
        cost_estimate=pl.CostEstimate(flops=10**6, bytes_accessed=2 * 10**6, transcendentals=0),
    )(index, flips, first_row.reshape(1), scale.reshape(1), blocks)


def shards(feats, top_grad, weights, table, a_inv, g_inv):
    num_layers, _, rows_dev, width, chans = feats.shape
    owners = lax.axis_size(OWNER)
    samples = lax.axis_size(DP)
    owner_id = lax.axis_index(OWNER)
    dp_id = lax.axis_index(DP)
    y_id = lax.axis_index("y")
    z_id = lax.axis_index("zh")
    npos = samples * rows_dev * owners * width
    patch = 9 * chans
    inner = owner_id < owners - 1
    f = feats[:, 0]
    top = top_grad[0]

    to_above, to_below = halo_rows(f, top)
    below = shifted(to_above, -1, True)
    above = shifted(to_below, 1, False)
    below1 = below[5:]
    below = jnp.where(inner, below[:5], jnp.zeros_like(below[:5]))
    wide3 = jnp.concatenate([above[:2], f[3], below[:2]])
    strips = [
        jnp.concatenate([above[3:4], f[0], below[3:4]]),
        jnp.concatenate([f[1], below1]),
        jnp.concatenate([above[2:3], f[2], below[2:3]]),
        wide3[1:5],
    ]
    core_id = lax.axis_index("core")

    def to_layers(x):
        return exchange(jnp.broadcast_to(x[None], (CORE,) + x.shape).reshape((-1,) + x.shape[1:]), ("core", "y"))

    flipped = jnp.transpose(weights.reshape(num_layers, 9, chans, chans), (0, 1, 3, 2)).reshape(
        num_layers, patch, chans
    )

    def slope(layer, win):
        pre = jnp.dot(to_columns(win), weights[layer], preferred_element_type=jnp.float32)
        return silu_slope(pre)

    def times(grad_in, slopes):
        return (grad_in.reshape(slopes.shape).astype(jnp.float32) * slopes).astype(jnp.bfloat16)

    def back(layer, win):
        return jnp.dot(
            back_columns(win), flipped[layer], preferred_element_type=jnp.float32
        ).astype(jnp.bfloat16)

    image = (rows_dev, width, chans)
    top_wide = jnp.concatenate([above[4:5], top, below[4:5]])
    dpre3 = times(top_wide, slope(3, windows(wide3))).reshape((rows_dev + 2, width, chans))
    dpre2 = times(back(3, windows(dpre3)), slope(2, windows(strips[2]))).reshape(image)
    after = shifted(dpre2, -1, True)
    dy1 = back(2, cut_windows(jnp.concatenate([dpre2, after]), inner))
    dpre1 = times(dy1, slope(1, cut_windows(strips[1], inner))).reshape(image)
    trimmed = [
        jnp.concatenate([jnp.where(y_id == 0, rows[:1], rows[3:]), rows[1:3]]) for rows in strips
    ]
    local = jnp.concatenate([a_inv.reshape(-1, chans), g_inv[0].astype(jnp.bfloat16)])
    stacked, dpre1, local = lax.optimization_barrier((jnp.stack(trimmed), dpre1, local))
    before = shifted(dpre1, 1, True)
    layer_strips = to_layers(stacked)
    from_y, from_z = table % Y, table // Y
    near = paired(local, "y", 0)
    far = paired(jnp.where(from_y[3 - y_id] == y_id, local, near), "y", 1)
    want = from_y[y_id]
    found = jnp.where(want == y_id, local, jnp.where(want == (y_id ^ 1), near, far))
    want = from_z[y_id]
    edge_top = jnp.where(owner_id > 0, before[:1], jnp.zeros_like(before[:1]))
    edge_end = jnp.where(inner, dpre1[1:], jnp.zeros_like(dpre1[1:]))
    dy0 = back(1, windows(jnp.concatenate([edge_top, before[1:], dpre1[:1], edge_end])))
    dpre0 = times(dy0, slope(0, windows(strips[0]))).reshape(image)

    images = layer_strips.reshape((CORE, Y) + layer_strips.shape[1:])
    last_one = (y_id == 1) & (z_id == ZH - 1)
    seam = jnp.zeros((Y * rows_dev, 3), bool).at[-2, 2].set(True).at[-1, 0].set(True)
    cols = []
    for image_rows in images:
        middle = image_rows[:, 1:].reshape((-1,) + image_rows.shape[2:])
        win = windows(jnp.concatenate([image_rows[0, :1], middle, image_rows[-1, :1]]))
        cut = (seam & last_one)[:, :, None, None]
        cols.append(to_columns(jnp.where(cut, jnp.zeros_like(win), win)))
    cols = jnp.concatenate(cols)
    gram = gram_half(cols, core_id)
    layer_dpre = to_layers(jnp.stack([dpre0, dpre1, dpre2, dpre3[1:3]]))
    parts = all_half(gram, cols, layer_dpre.reshape(-1, chans), core_id)

    parts, found = lax.optimization_barrier((parts, found))
    found = jnp.where(want == (z_id ^ 1), paired(found, "zh", 0), found)

    piece = scatter_sum(parts, ("x", "zl"))
    piece, found = lax.optimization_barrier((piece, found))
    inverses = jnp.where(want // 2 == z_id // 2, found, paired(found, "zh", 1))
    held = spread(piece[:, :FAC_ROWS], "y")
    layer_ids = jnp.arange(num_layers, dtype=jnp.int32)

    def pick(z):
        lay = jnp.sum(jnp.where(table == z * Y + y_id, layer_ids, 0))
        fac = lax.dynamic_index_in_dim(held, lay, 0, keepdims=False)
        return jnp.concatenate([fac, piece[:, FAC_ROWS:]], axis=1)

    total = exchange(jnp.stack([pick(z) for z in range(ZH)]), "zh")
    total = jnp.sum(total.astype(jnp.float32), axis=0).astype(jnp.bfloat16)
    summed = spread(spread(spread(total, "zl"), "x"), "core")

    in_grad_win = jnp.concatenate([shifted(dpre0[1:], 1, False), dpre0, shifted(dpre0[:1], -1, False)])
    in_grad = back(0, windows(in_grad_win)).reshape((1,) + image)

    stats = summed.reshape(CORE * HALF_G, PIECE_ROWS, chans)
    grad_sum = stats[:, FAC_ROWS : FAC_ROWS + GRAD_ROWS].reshape(-1, chans)[:patch]
    rows_out = patch // samples
    a_mine = inverses[: rows_out * 9].reshape(rows_out, patch)
    mixed = jnp.dot(grad_sum, inverses[rows_out * 9 :], preferred_element_type=jnp.float32)
    mixed = mixed / jnp.sqrt(jnp.float32(npos))
    panel = jnp.dot(a_mine.astype(jnp.float32), mixed, precision=lax.Precision.HIGHEST)
    step_out = spread(panel.astype(jnp.bfloat16), "y")

    have = jnp.any(table == owner_id).astype(jnp.float32)
    scale = have / npos
    a_out = factor_rows(stats, dp_id * rows_out, scale, rows_out)[None]
    g_out = (stats[NG, :FAC_ROWS].astype(jnp.float32) * scale)[None]
    return (step_out, a_out, g_out, in_grad)


def solution(mesh):
    fine = Mesh(mesh.devices.reshape(X, ZL, CORE, ZH, Y), DP + OWNER)
    placed = (
        P(None, DP, OWNER, None, None),
        P(DP, OWNER, None, None),
        P(),
        P(),
        P(OWNER, DP, None),
        P(OWNER, None, None),
    )
    return jax.shard_map(
        shards,
        mesh=fine,
        in_specs=placed,
        out_specs=(
            P(None, DP, None),
            P(OWNER, DP, None),
            P(OWNER, None, None),
            P(DP, OWNER, None, None),
        ),
        check_vma=False,
    )
```

```python
import jax
import jax.numpy as jnp
from jax import lax
from jax.experimental import pallas as pl
from jax.experimental.pallas import tpu as pltpu
from jax.sharding import Mesh, PartitionSpec as P

X, ZL, CORE, ZH, Y = 4, 4, 2, 4, 4
OWNER = ("zh", "y")
DP = ("x", "zl", "core")


def shifted(x, shift, cyclic):
    count = ZH * Y
    pairs = [(i, (i + shift) % count) for i in range(count)]
    if not cyclic:
        pairs = [(a, b) for a, b in pairs if b - a == shift]
    return lax.ppermute(x, OWNER, pairs)


def paired(x, axis, step):
    return lax.ppermute(x, axis, [(i, i ^ 1 if step == 0 else 3 - i) for i in range(4)])


def exchange(x, axis):
    return lax.all_to_all(x, axis, split_axis=0, concat_axis=0, tiled=True)


def spread(x, axis):
    count = lax.axis_size(axis)
    return exchange(jnp.broadcast_to(x[None], (count,) + x.shape), axis)


def scatter_sum(x, axis):
    count = lax.axis_size(axis)
    got = exchange(x.reshape((count, x.shape[0] // count) + x.shape[1:]), axis)
    return jnp.sum(got.astype(jnp.float32), axis=0).astype(jnp.bfloat16)


def windows(rows):
    rows = jnp.pad(rows, ((0, 0), (1, 1), (0, 0)))
    return jnp.stack([rows[i : i + 3] for i in range(rows.shape[0] - 2)])


def cut_windows(rows, whole):
    first, second = rows[:3], rows[1:]
    first = jnp.where(whole, first, first * jnp.array([1, 1, 0], rows.dtype)[:, None, None])
    second = jnp.where(whole, second, second * jnp.array([0, 1, 1], rows.dtype)[:, None, None])
    return jnp.pad(jnp.stack([first, second]), ((0, 0), (0, 0), (1, 1), (0, 0)))


def to_columns(win):
    width = win.shape[2] - 2
    taps = [win[:, ky, kx : kx + width] for ky in range(3) for kx in range(3)]
    return jnp.concatenate(taps, axis=-1).reshape(-1, 9 * win.shape[-1])


def back_columns(win):
    width = win.shape[2] - 2
    taps = [win[:, 2 - ky, 2 - kx : 2 - kx + width] for ky in range(3) for kx in range(3)]
    return jnp.concatenate(taps, axis=-1).reshape(-1, 9 * win.shape[-1])


def silu_slope(value):
    sig = jax.nn.sigmoid(value)
    return sig * (1.0 + value * (1.0 - sig))


def inner_rows(left, right):
    return lax.dot_general(
        left, right, (((0,), (0,)), ((), ())), preferred_element_type=jnp.float32
    )


def block_classes():
    found = {}
    pairs = []
    where = {}
    for a in range(9):
        for b in range(9):
            first, second, flip = a, b, False
            dy, dx = b // 3 - a // 3, b % 3 - a % 3
            if dy < 0 or (dy == 0 and dx < 0):
                first, second, flip = b, a, True
                dy, dx = -dy, -dx
            key = (dy, dx, first // 3 if dy == 0 else -1, first % 3 if dx == 0 else -1)
            if key not in found:
                found[key] = len(pairs)
                pairs.append((first, second))
            where[a, b] = (found[key], flip)
    return pairs, where


PAIRS, WHERE = block_classes()
NG = len(PAIRS)
HALF_G = 16
HALF_D = 5
FAC_ROWS = 128
GRAD_ROWS = 40
PIECE_ROWS = 176
SMEM = pl.BlockSpec(memory_space=pltpu.SMEM)
VMEM = pl.BlockSpec(memory_space=pltpu.VMEM)


def halo_rows(f, top):
    def kernel(f_ref, top_ref, up_ref, down_ref):
        for ref, edge in ((up_ref, 0), (down_ref, 1)):
            ref[0:2] = f_ref[3]
            ref[2] = f_ref[2, edge]
            ref[3] = f_ref[0, edge]
            ref[4] = top_ref[edge]
        up_ref[5:7] = f_ref[1]

    row = f.shape[2:]
    return pl.pallas_call(
        kernel,
        out_shape=(
            jax.ShapeDtypeStruct((7,) + row, f.dtype),
            jax.ShapeDtypeStruct((5,) + row, f.dtype),
        ),
        in_specs=[VMEM, VMEM],
        out_specs=(VMEM, VMEM),
        cost_estimate=pl.CostEstimate(flops=0, bytes_accessed=10**6, transcendentals=0),
    )(f, top)


def gram_half(cols, core):
    chans = cols.shape[1] // 9

    def kernel(core_ref, cols_ref, out_ref):
        def some(mine):
            for a in sorted({first for first, _ in mine}):
                wanted = [b for first, b in mine if first == a]
                low = min(wanted)
                left = cols_ref[:, a * chans : (a + 1) * chans].T
                right = cols_ref[:, low * chans : (max(wanted) + 1) * chans]
                product = jnp.dot(left, right, preferred_element_type=jnp.float32)
                for b in wanted:
                    i = mine.index((a, b))
                    part = product[:, (b - low) * chans : (b - low + 1) * chans]
                    out_ref[i * chans : (i + 1) * chans, :] = part.astype(out_ref.dtype)
            for i in range(len(mine), HALF_G):
                out_ref[i * chans : (i + 1) * chans, :] = jnp.zeros((chans, chans), out_ref.dtype)

        @pl.when(core_ref[0] == 0)
        def _():
            some(PAIRS[:HALF_G])

        @pl.when(core_ref[0] != 0)
        def _():
            some(PAIRS[HALF_G:])

    return pl.pallas_call(
        kernel,
        out_shape=jax.ShapeDtypeStruct((HALF_G * chans, chans), jnp.bfloat16),
        in_specs=[SMEM, VMEM],
        out_specs=VMEM,
        compiler_params=pltpu.CompilerParams(vmem_limit_bytes=24 * 2**20),
        cost_estimate=pl.CostEstimate(
            flops=2 * (HALF_G + HALF_D) * cols.shape[0] * chans * chans,
            bytes_accessed=5 * 10**6,
            transcendentals=0,
        ),
    )(core.reshape(1), cols)


def all_half(gram, cols, dpre, core):
    chans = dpre.shape[-1]

    def kernel(core_ref, gram_ref, cols_ref, dpre_ref, out_ref, dense):
        for k in range(HALF_G):
            out_ref[k, :FAC_ROWS, :] = gram_ref[k * chans : (k + 1) * chans, :]
        dense[...] = jnp.zeros(dense.shape, dense.dtype)

        def some(first, last):
            turned = dpre_ref[...].T
            right = cols_ref[:, first * chans : last * chans]
            grad = jnp.dot(turned, right, preferred_element_type=jnp.float32)
            for i in range(last - first):
                dense[i * chans : (i + 1) * chans, :] = grad[:, i * chans : (i + 1) * chans].T
            return turned

        @pl.when(core_ref[0] == 0)
        def _():
            some(0, HALF_D)

        @pl.when(core_ref[0] != 0)
        def _():
            turned = some(HALF_D, 9)
            own = jnp.dot(turned, dpre_ref[...], preferred_element_type=jnp.float32)
            out_ref[NG - HALF_G, :FAC_ROWS, :] = own.astype(out_ref.dtype)

        for k in range(HALF_G):
            rows = dense[k * GRAD_ROWS : k * GRAD_ROWS + PIECE_ROWS - FAC_ROWS, :]
            out_ref[k, FAC_ROWS:, :] = rows.astype(out_ref.dtype)

    return pl.pallas_call(
        kernel,
        out_shape=jax.ShapeDtypeStruct((HALF_G, PIECE_ROWS, chans), jnp.bfloat16),
        in_specs=[SMEM, VMEM, VMEM, VMEM],
        out_specs=VMEM,
        scratch_shapes=[pltpu.VMEM((HALF_D * chans + 16, chans), jnp.float32)],
        compiler_params=pltpu.CompilerParams(vmem_limit_bytes=24 * 2**20),
        cost_estimate=pl.CostEstimate(
            flops=2 * HALF_D * cols.shape[0] * chans * chans,
            bytes_accessed=5 * 10**6,
            transcendentals=0,
        ),
    )(core.reshape(1), gram, cols, dpre)


def choose(which, table, place, *arrays):
    def kernel(table_ref, place_ref, *refs):
        number = which(table_ref, place_ref[0], place_ref[1])
        for k, ref in enumerate(refs[:-1]):

            @pl.when(number == k)
            def _(ref=ref):
                refs[-1][...] = ref[...]

    return pl.pallas_call(
        kernel,
        out_shape=jax.ShapeDtypeStruct(arrays[0].shape, arrays[0].dtype),
        in_specs=[SMEM, SMEM] + [VMEM] * len(arrays),
        out_specs=VMEM,
        cost_estimate=pl.CostEstimate(flops=0, bytes_accessed=500000, transcendentals=0),
    )(table, place, *arrays)


def layer_at(table_ref, owner):
    lay = jnp.int32(0)
    for l in range(1, table_ref.shape[0]):
        lay = jnp.where(table_ref[l] == owner, l, lay)
    return lay


def for_groups(table, place, held, piece):
    def kernel(table_ref, place_ref, held_ref, piece_ref, out_ref):
        for z in range(ZH):
            out_ref[z, :, :FAC_ROWS, :] = held_ref[layer_at(table_ref, z * Y + place_ref[0])]
            out_ref[z, :, FAC_ROWS:, :] = piece_ref[:, FAC_ROWS:, :]

    return pl.pallas_call(
        kernel,
        out_shape=jax.ShapeDtypeStruct((ZH,) + piece.shape, piece.dtype),
        in_specs=[SMEM, SMEM, VMEM, VMEM],
        out_specs=VMEM,
        cost_estimate=pl.CostEstimate(flops=0, bytes_accessed=500000, transcendentals=0),
    )(table, place, held, piece)


def factor_rows(blocks, table, place, rows, count):
    chans = blocks.shape[-1]
    index = jnp.array([WHERE[a, b][0] for a in range(9) for b in range(9)], jnp.int32)
    flips = jnp.array([int(WHERE[a, b][1]) for a in range(9) for b in range(9)], jnp.int32)

    def kernel(index_ref, flip_ref, table_ref, place_ref, blocks_ref, out_ref, own_ref, band):
        owner = place_ref[1] * Y + place_ref[0]
        scale = jnp.float32(0.0)
        for l in range(table_ref.shape[0]):
            scale = jnp.where(table_ref[l] == owner, jnp.float32(1.0 / count), scale)
        start = place_ref[2] * rows
        tap = lax.div(start, chans)
        for t in range(2):
            a = jnp.minimum(tap + t, 8)
            for b in range(9):
                block = blocks_ref[index_ref[a * 9 + b], :chans, :].astype(jnp.float32)
                flip = flip_ref[a * 9 + b] != 0
                band[t * chans : (t + 1) * chans, b * chans : (b + 1) * chans] = jnp.where(
                    flip, block.T, block
                )
        inside = start - tap * chans
        base = pl.multiple_of(lax.div(inside, 8) * 8, 8)
        got = band[pl.ds(base, rows + 4), :]
        odd = inside != base
        out_ref[...] = jnp.where(odd, got[4:], got[:rows]) * scale
        own_ref[...] = blocks_ref[NG, :chans, :].astype(jnp.float32) * scale

    return pl.pallas_call(
        kernel,
        out_shape=(
            jax.ShapeDtypeStruct((rows, 9 * chans), jnp.float32),
            jax.ShapeDtypeStruct((chans, chans), jnp.float32),
        ),
        in_specs=[SMEM, SMEM, SMEM, SMEM, VMEM],
        out_specs=(VMEM, VMEM),
        scratch_shapes=[pltpu.VMEM((2 * chans, 9 * chans), jnp.float32)],
        compiler_params=pltpu.CompilerParams(vmem_limit_bytes=16 * 2**20),
        cost_estimate=pl.CostEstimate(flops=10**6, bytes_accessed=2 * 10**6, transcendentals=0),
    )(index, flips, table, place, blocks)


def shards(feats, top_grad, weights, table, a_inv, g_inv):
    num_layers, _, rows_dev, width, chans = feats.shape
    owners = lax.axis_size(OWNER)
    samples = lax.axis_size(DP)
    owner_id = lax.axis_index(OWNER)
    dp_id = lax.axis_index(DP)
    y_id = lax.axis_index("y")
    z_id = lax.axis_index("zh")
    npos = samples * rows_dev * owners * width
    patch = 9 * chans
    inner = owner_id < owners - 1
    f = feats[:, 0]
    top = top_grad[0]

    to_above, to_below = halo_rows(f, top)
    below = shifted(to_above, -1, True)
    above = shifted(to_below, 1, False)
    below1 = below[5:]
    below = jnp.where(inner, below[:5], jnp.zeros_like(below[:5]))
    wide3 = jnp.concatenate([above[:2], f[3], below[:2]])
    strips = [
        jnp.concatenate([above[3:4], f[0], below[3:4]]),
        jnp.concatenate([f[1], below1]),
        jnp.concatenate([above[2:3], f[2], below[2:3]]),
        wide3[1:5],
    ]
    core_id = lax.axis_index("core")

    def to_layers(x):
        return exchange(jnp.broadcast_to(x[None], (CORE,) + x.shape).reshape((-1,) + x.shape[1:]), ("core", "y"))

    flipped = jnp.transpose(weights.reshape(num_layers, 9, chans, chans), (0, 1, 3, 2)).reshape(
        num_layers, patch, chans
    )

    def slope(layer, win):
        pre = jnp.dot(to_columns(win), weights[layer], preferred_element_type=jnp.float32)
        return silu_slope(pre)

    def times(grad_in, slopes):
        return (grad_in.reshape(slopes.shape).astype(jnp.float32) * slopes).astype(jnp.bfloat16)

    def back(layer, win):
        return jnp.dot(
            back_columns(win), flipped[layer], preferred_element_type=jnp.float32
        ).astype(jnp.bfloat16)

    image = (rows_dev, width, chans)
    top_wide = jnp.concatenate([above[4:5], top, below[4:5]])
    dpre3 = times(top_wide, slope(3, windows(wide3))).reshape((rows_dev + 2, width, chans))
    dpre2 = times(back(3, windows(dpre3)), slope(2, windows(strips[2]))).reshape(image)
    after = shifted(dpre2, -1, True)
    dy1 = back(2, cut_windows(jnp.concatenate([dpre2, after]), inner))
    dpre1 = times(dy1, slope(1, cut_windows(strips[1], inner))).reshape(image)
    trimmed = [
        jnp.concatenate([jnp.where(y_id == 0, rows[:1], rows[3:]), rows[1:3]]) for rows in strips
    ]
    local = jnp.concatenate([a_inv.reshape(-1, chans), g_inv[0].astype(jnp.bfloat16)])
    stacked, dpre1, local = lax.optimization_barrier((jnp.stack(trimmed), dpre1, local))
    before = shifted(dpre1, 1, True)
    layer_strips = to_layers(stacked)
    near = paired(local, "y", 0)
    edge_top = jnp.where(owner_id > 0, before[:1], jnp.zeros_like(before[:1]))
    edge_end = jnp.where(inner, dpre1[1:], jnp.zeros_like(dpre1[1:]))
    dy0 = back(1, windows(jnp.concatenate([edge_top, before[1:], dpre1[:1], edge_end])))
    dpre0 = times(dy0, slope(0, windows(strips[0]))).reshape(image)

    images = layer_strips.reshape((CORE, Y) + layer_strips.shape[1:])
    last_one = (y_id == 1) & (z_id == ZH - 1)
    seam = jnp.zeros((Y * rows_dev, 3), bool).at[-2, 2].set(True).at[-1, 0].set(True)
    cols = []
    for image_rows in images:
        middle = image_rows[:, 1:].reshape((-1,) + image_rows.shape[2:])
        win = windows(jnp.concatenate([image_rows[0, :1], middle, image_rows[-1, :1]]))
        cut = (seam & last_one)[:, :, None, None]
        cols.append(to_columns(jnp.where(cut, jnp.zeros_like(win), win)))
    cols = jnp.concatenate(cols)
    gram = gram_half(cols, core_id)

    def for_partner(table_ref, y, z):
        return jnp.where((table_ref[3 - y] & 3) == y, 0, 1)

    def in_group(table_ref, y, z):
        want = table_ref[y] & 3
        return jnp.where(want == y, 0, jnp.where(want == (y ^ 1), 1, 2))

    def beside(table_ref, y, z):
        return jnp.where((table_ref[y] >> 2) == (z ^ 1), 1, 0)

    def across(table_ref, y, z):
        return jnp.where((table_ref[y] >> 3) == (z >> 1), 0, 1)

    place = jnp.stack([y_id, z_id, dp_id]).astype(jnp.int32)
    away = choose(for_partner, table, place, local, near)
    gram, away = lax.optimization_barrier((gram, away))
    found = choose(in_group, table, place, local, near, paired(away, "y", 1))
    layer_dpre = to_layers(jnp.stack([dpre0, dpre1, dpre2, dpre3[1:3]]))
    parts = all_half(gram, cols, layer_dpre.reshape(-1, chans), core_id)

    parts, found = lax.optimization_barrier((parts, found))
    found = choose(beside, table, place, found, paired(found, "zh", 0))
    piece = scatter_sum(parts, ("x", "zl"))
    piece, found = lax.optimization_barrier((piece, found))
    inverses = choose(across, table, place, found, paired(found, "zh", 1))
    held = spread(piece[:, :FAC_ROWS], "y")
    total = exchange(for_groups(table, place, held, piece), "zh")
    total = jnp.sum(total.astype(jnp.float32), axis=0).astype(jnp.bfloat16)
    summed = spread(spread(spread(total, "zl"), "x"), "core")

    in_grad_win = jnp.concatenate([shifted(dpre0[1:], 1, False), dpre0, shifted(dpre0[:1], -1, False)])
    in_grad = back(0, windows(in_grad_win)).reshape((1,) + image)

    stats = summed.reshape(CORE * HALF_G, PIECE_ROWS, chans)
    grad_sum = stats[:, FAC_ROWS : FAC_ROWS + GRAD_ROWS].reshape(-1, chans)[:patch]
    rows_out = patch // samples
    a_mine = inverses[: rows_out * 9].reshape(rows_out, patch)
    mixed = jnp.dot(grad_sum, inverses[rows_out * 9 :], preferred_element_type=jnp.float32)
    mixed = mixed / jnp.sqrt(jnp.float32(npos))
    panel = jnp.dot(a_mine.astype(jnp.float32), mixed, precision=lax.Precision.HIGHEST)
    step_out = spread(panel.astype(jnp.bfloat16), "y")

    a_out, g_out = factor_rows(stats, table, place, rows_out, npos)
    a_out, g_out = a_out[None], g_out[None]
    return (step_out, a_out, g_out, in_grad)


def solution(mesh):
    fine = Mesh(mesh.devices.reshape(X, ZL, CORE, ZH, Y), DP + OWNER)
    placed = (
        P(None, DP, OWNER, None, None),
        P(DP, OWNER, None, None),
        P(),
        P(),
        P(OWNER, DP, None),
        P(OWNER, None, None),
    )
    return jax.shard_map(
        shards,
        mesh=fine,
        in_specs=placed,
        out_specs=(
            P(None, DP, None),
            P(OWNER, DP, None),
            P(OWNER, None, None),
            P(DP, OWNER, None, None),
        ),
        check_vma=False,
    )
```

```python
import jax
import jax.numpy as jnp
from jax import lax
from jax.experimental import pallas as pl
from jax.experimental.pallas import tpu as pltpu
from jax.sharding import Mesh, PartitionSpec as P

X, ZL, CORE, ZH, Y = 4, 4, 2, 4, 4
OWNER = ("zh", "y")
DP = ("x", "zl", "core")


def shifted(x, shift, cyclic):
    count = ZH * Y
    pairs = [(i, (i + shift) % count) for i in range(count)]
    if not cyclic:
        pairs = [(a, b) for a, b in pairs if b - a == shift]
    return lax.ppermute(x, OWNER, pairs)


def exchange(x, axis):
    return lax.all_to_all(x, axis, split_axis=0, concat_axis=0, tiled=True)


def spread(x, axis):
    count = lax.axis_size(axis)
    return exchange(jnp.broadcast_to(x[None], (count,) + x.shape), axis)


def scatter_sum(x, axis):
    count = lax.axis_size(axis)
    got = exchange(x.reshape((count, x.shape[0] // count) + x.shape[1:]), axis)
    return jnp.sum(got.astype(jnp.float32), axis=0).astype(jnp.bfloat16)


def windows(rows):
    rows = jnp.pad(rows, ((0, 0), (1, 1), (0, 0)))
    return jnp.stack([rows[i : i + 3] for i in range(rows.shape[0] - 2)])


def cut_windows(rows, whole):
    first, second = rows[:3], rows[1:]
    first = jnp.where(whole, first, first * jnp.array([1, 1, 0], rows.dtype)[:, None, None])
    second = jnp.where(whole, second, second * jnp.array([0, 1, 1], rows.dtype)[:, None, None])
    return jnp.pad(jnp.stack([first, second]), ((0, 0), (0, 0), (1, 1), (0, 0)))


def to_columns(win):
    width = win.shape[2] - 2
    taps = [win[:, ky, kx : kx + width] for ky in range(3) for kx in range(3)]
    return jnp.concatenate(taps, axis=-1).reshape(-1, 9 * win.shape[-1])


def back_columns(win):
    width = win.shape[2] - 2
    taps = [win[:, 2 - ky, 2 - kx : 2 - kx + width] for ky in range(3) for kx in range(3)]
    return jnp.concatenate(taps, axis=-1).reshape(-1, 9 * win.shape[-1])


def silu_slope(value):
    sig = jax.nn.sigmoid(value)
    return sig * (1.0 + value * (1.0 - sig))


def inner_rows(left, right):
    return lax.dot_general(
        left, right, (((0,), (0,)), ((), ())), preferred_element_type=jnp.float32
    )


def block_classes():
    found = {}
    pairs = []
    where = {}
    for a in range(9):
        for b in range(9):
            first, second, flip = a, b, False
            dy, dx = b // 3 - a // 3, b % 3 - a % 3
            if dy < 0 or (dy == 0 and dx < 0):
                first, second, flip = b, a, True
                dy, dx = -dy, -dx
            key = (dy, dx, first // 3 if dy == 0 else -1, first % 3 if dx == 0 else -1)
            if key not in found:
                found[key] = len(pairs)
                pairs.append((first, second))
            where[a, b] = (found[key], flip)
    return pairs, where


PAIRS, WHERE = block_classes()
NG = len(PAIRS)
HALF_G = 15
HALF_D = 5
HALF = HALF_G + HALF_D
SMEM = pl.BlockSpec(memory_space=pltpu.SMEM)
VMEM = pl.BlockSpec(memory_space=pltpu.VMEM)


def halo_rows(f, top):
    def kernel(f_ref, top_ref, up_ref, down_ref):
        for ref, edge in ((up_ref, 0), (down_ref, 1)):
            ref[0:2] = f_ref[3]
            ref[2] = f_ref[2, edge]
            ref[3] = f_ref[0, edge]
            ref[4] = top_ref[edge]
        up_ref[5:7] = f_ref[1]

    row = f.shape[2:]
    return pl.pallas_call(
        kernel,
        out_shape=(
            jax.ShapeDtypeStruct((7,) + row, f.dtype),
            jax.ShapeDtypeStruct((5,) + row, f.dtype),
        ),
        in_specs=[VMEM, VMEM],
        out_specs=(VMEM, VMEM),
        cost_estimate=pl.CostEstimate(flops=0, bytes_accessed=10**6, transcendentals=0),
    )(f, top)


def gram_half(cols, core):
    chans = cols.shape[1] // 9

    def kernel(core_ref, cols_ref, out_ref):
        def some(mine):
            for a in sorted({first for first, _ in mine}):
                wanted = [b for first, b in mine if first == a]
                low = min(wanted)
                left = cols_ref[:, a * chans : (a + 1) * chans].T
                right = cols_ref[:, low * chans : (max(wanted) + 1) * chans]
                product = jnp.dot(left, right, preferred_element_type=jnp.float32)
                for b in wanted:
                    i = mine.index((a, b))
                    part = product[:, (b - low) * chans : (b - low + 1) * chans]
                    out_ref[i * chans : (i + 1) * chans, :] = part.astype(out_ref.dtype)
            for i in range(len(mine), HALF_G):
                out_ref[i * chans : (i + 1) * chans, :] = jnp.zeros((chans, chans), out_ref.dtype)

        @pl.when(core_ref[0] == 0)
        def _():
            some(PAIRS[:HALF_G])

        @pl.when(core_ref[0] != 0)
        def _():
            some(PAIRS[HALF_G:])

    return pl.pallas_call(
        kernel,
        out_shape=jax.ShapeDtypeStruct((HALF_G * chans, chans), jnp.bfloat16),
        in_specs=[SMEM, VMEM],
        out_specs=VMEM,
        compiler_params=pltpu.CompilerParams(vmem_limit_bytes=24 * 2**20),
        cost_estimate=pl.CostEstimate(
            flops=2 * (HALF_G + HALF_D) * cols.shape[0] * chans * chans,
            bytes_accessed=5 * 10**6,
            transcendentals=0,
        ),
    )(core.reshape(1), cols)


def all_half(gram, cols, dpre, core):
    chans = dpre.shape[-1]

    def kernel(core_ref, gram_ref, cols_ref, dpre_ref, out_ref):
        out_ref[: HALF_G * chans, :] = gram_ref[...]

        def put(i, value):
            out_ref[(HALF_G + i) * chans : (HALF_G + i + 1) * chans, :] = value.astype(out_ref.dtype)

        def some(first, last, own):
            turned = dpre_ref[...].T
            right = cols_ref[:, first * chans : last * chans]
            grad = jnp.dot(turned, right, preferred_element_type=jnp.float32)
            for i in range(last - first):
                put(i, grad[:, i * chans : (i + 1) * chans].T)
            if own:
                put(last - first, jnp.dot(turned, dpre_ref[...], preferred_element_type=jnp.float32))

        @pl.when(core_ref[0] == 0)
        def _():
            some(0, HALF_D, False)

        @pl.when(core_ref[0] != 0)
        def _():
            some(HALF_D, 9, True)

    return pl.pallas_call(
        kernel,
        out_shape=jax.ShapeDtypeStruct((HALF * chans, chans), jnp.bfloat16),
        in_specs=[SMEM, VMEM, VMEM, VMEM],
        out_specs=VMEM,
        compiler_params=pltpu.CompilerParams(vmem_limit_bytes=24 * 2**20),
        cost_estimate=pl.CostEstimate(
            flops=2 * HALF_D * cols.shape[0] * chans * chans,
            bytes_accessed=5 * 10**6,
            transcendentals=0,
        ),
    )(core.reshape(1), gram, cols, dpre)


def owned_rows(blocks, panel, place):
    chans = blocks.shape[-1]
    rows = panel.shape[0]
    wide = 9 * chans
    slots = [i // HALF_G * HALF + i % HALF_G for i in range(NG)]
    index = jnp.array([slots[WHERE[a, b][0]] for a in range(9) for b in range(9)], jnp.int32)
    flips = jnp.array([int(WHERE[a, b][1]) for a in range(9) for b in range(9)], jnp.int32)

    def kernel(index_ref, flip_ref, place_ref, blocks_ref, panel_ref, out_ref, band):
        start = place_ref[2] * rows
        tap = lax.div(start, chans)
        for t in range(2):
            a = jnp.minimum(tap + t, 8)
            for b in range(9):
                block = blocks_ref[index_ref[a * 9 + b]].astype(jnp.float32)
                flip = flip_ref[a * 9 + b] != 0
                band[t * chans : (t + 1) * chans, b * chans : (b + 1) * chans] = jnp.where(
                    flip, block.T, block
                )
        inside = start - tap * chans
        base = pl.multiple_of(lax.div(inside, 8) * 8, 8)
        got = band[pl.ds(base, rows + 4), :]
        odd = inside != base
        out_ref[:, :wide] = jnp.where(odd, got[4:], got[:rows]).astype(out_ref.dtype)
        out_ref[:, wide : wide + chans] = panel_ref[...]
        out_ref[:, wide + chans :] = jnp.zeros((rows, 4 * chans), out_ref.dtype)
        part = chans // 4
        for q in range(4):
            lanes = slice(wide + (q + 1) * chans, wide + (q + 2) * chans)
            out_ref[:part, lanes] = blocks_ref[2 * HALF - 1, q * part : (q + 1) * part, :]

    return pl.pallas_call(
        kernel,
        out_shape=jax.ShapeDtypeStruct((rows, wide + 5 * chans), jnp.bfloat16),
        in_specs=[SMEM, SMEM, SMEM, VMEM, VMEM],
        out_specs=VMEM,
        scratch_shapes=[pltpu.VMEM((2 * chans, wide), jnp.float32)],
        compiler_params=pltpu.CompilerParams(vmem_limit_bytes=16 * 2**20),
        cost_estimate=pl.CostEstimate(flops=10**6, bytes_accessed=2 * 10**6, transcendentals=0),
    )(index, flips, place, blocks, panel)


def results(got, table, place, chans, count):
    layers, rows, _ = got.shape
    wide = 9 * chans

    def kernel(table_ref, place_ref, got_ref, step_ref, fac_ref, own_ref):
        owner = place_ref[1] * Y + place_ref[0]
        lay = jnp.int32(0)
        scale = jnp.float32(0.0)
        for l in range(layers):
            mine = table_ref[l] == owner
            lay = jnp.where(mine, l, lay)
            scale = jnp.where(mine, jnp.float32(1.0 / count), scale)
            step_ref[l] = got_ref[l, :, wide : wide + chans]
        fac_ref[...] = got_ref[lay, :, :wide].astype(jnp.float32) * scale
        part = chans // 4
        for q in range(4):
            lanes = slice(wide + (q + 1) * chans, wide + (q + 2) * chans)
            own_ref[q * part : (q + 1) * part, :] = (
                got_ref[lay, :part, lanes].astype(jnp.float32) * scale
            )

    return pl.pallas_call(
        kernel,
        out_shape=(
            jax.ShapeDtypeStruct((layers, rows, chans), jnp.bfloat16),
            jax.ShapeDtypeStruct((rows, wide), jnp.float32),
            jax.ShapeDtypeStruct((chans, chans), jnp.float32),
        ),
        in_specs=[SMEM, SMEM, VMEM],
        out_specs=(VMEM, VMEM, VMEM),
        cost_estimate=pl.CostEstimate(flops=10**5, bytes_accessed=10**6, transcendentals=0),
    )(table, place, got)


def shards(feats, top_grad, weights, table, a_inv, g_inv):
    num_layers, _, rows_dev, width, chans = feats.shape
    owners = lax.axis_size(OWNER)
    samples = lax.axis_size(DP)
    owner_id = lax.axis_index(OWNER)
    dp_id = lax.axis_index(DP)
    y_id = lax.axis_index("y")
    z_id = lax.axis_index("zh")
    npos = samples * rows_dev * owners * width
    patch = 9 * chans
    inner = owner_id < owners - 1
    f = feats[:, 0]
    top = top_grad[0]

    to_above, to_below = halo_rows(f, top)
    below = shifted(to_above, -1, True)
    above = shifted(to_below, 1, False)
    below1 = below[5:]
    below = jnp.where(inner, below[:5], jnp.zeros_like(below[:5]))
    wide3 = jnp.concatenate([above[:2], f[3], below[:2]])
    strips = [
        jnp.concatenate([above[3:4], f[0], below[3:4]]),
        jnp.concatenate([f[1], below1]),
        jnp.concatenate([above[2:3], f[2], below[2:3]]),
        wide3[1:5],
    ]
    core_id = lax.axis_index("core")

    def to_layers(x):
        return exchange(jnp.broadcast_to(x[None], (CORE,) + x.shape).reshape((-1,) + x.shape[1:]), ("core", "y"))

    flipped = jnp.transpose(weights.reshape(num_layers, 9, chans, chans), (0, 1, 3, 2)).reshape(
        num_layers, patch, chans
    )

    def slope(layer, win):
        pre = jnp.dot(to_columns(win), weights[layer], preferred_element_type=jnp.float32)
        return silu_slope(pre)

    def times(grad_in, slopes):
        return (grad_in.reshape(slopes.shape).astype(jnp.float32) * slopes).astype(jnp.bfloat16)

    def back(layer, win):
        return jnp.dot(
            back_columns(win), flipped[layer], preferred_element_type=jnp.float32
        ).astype(jnp.bfloat16)

    image = (rows_dev, width, chans)
    top_wide = jnp.concatenate([above[4:5], top, below[4:5]])
    dpre3 = times(top_wide, slope(3, windows(wide3))).reshape((rows_dev + 2, width, chans))
    dpre2 = times(back(3, windows(dpre3)), slope(2, windows(strips[2]))).reshape(image)
    after = shifted(dpre2, -1, True)
    dy1 = back(2, cut_windows(jnp.concatenate([dpre2, after]), inner))
    dpre1 = times(dy1, slope(1, cut_windows(strips[1], inner))).reshape(image)
    trimmed = [
        jnp.concatenate([jnp.where(y_id == 0, rows[:1], rows[3:]), rows[1:3]]) for rows in strips
    ]
    local = jnp.concatenate(
        [
            a_inv.reshape(-1, chans),
            g_inv[0].astype(jnp.bfloat16),
            jnp.zeros((12, chans), jnp.bfloat16),
        ]
    )
    inverses = lax.all_gather(local, OWNER, axis=0, tiled=True)
    stacked, dpre1 = lax.optimization_barrier((jnp.stack(trimmed), dpre1))
    before = shifted(dpre1, 1, True)
    layer_strips = to_layers(stacked)
    edge_top = jnp.where(owner_id > 0, before[:1], jnp.zeros_like(before[:1]))
    edge_end = jnp.where(inner, dpre1[1:], jnp.zeros_like(dpre1[1:]))
    dy0 = back(1, windows(jnp.concatenate([edge_top, before[1:], dpre1[:1], edge_end])))
    dpre0 = times(dy0, slope(0, windows(strips[0]))).reshape(image)

    images = layer_strips.reshape((CORE, Y) + layer_strips.shape[1:])
    last_one = (y_id == 1) & (z_id == ZH - 1)
    seam = jnp.zeros((Y * rows_dev, 3), bool).at[-2, 2].set(True).at[-1, 0].set(True)
    cols = []
    for image_rows in images:
        middle = image_rows[:, 1:].reshape((-1,) + image_rows.shape[2:])
        win = windows(jnp.concatenate([image_rows[0, :1], middle, image_rows[-1, :1]]))
        cut = (seam & last_one)[:, :, None, None]
        cols.append(to_columns(jnp.where(cut, jnp.zeros_like(win), win)))
    cols = jnp.concatenate(cols)
    gram = gram_half(cols, core_id)

    layer_dpre = to_layers(jnp.stack([dpre0, dpre1, dpre2, dpre3[1:3]]))
    parts = all_half(gram, cols, layer_dpre.reshape(-1, chans), core_id)

    piece = scatter_sum(parts, ("x", "zl"))
    piece, inverses = lax.optimization_barrier((piece, inverses))
    total = spread(piece, "zh")
    total = jnp.sum(total.astype(jnp.float32), axis=0).astype(jnp.bfloat16)
    summed = spread(spread(spread(total, "zl"), "x"), "core")

    in_grad_win = jnp.concatenate([shifted(dpre0[1:], 1, False), dpre0, shifted(dpre0[:1], -1, False)])
    in_grad = back(0, windows(in_grad_win)).reshape((1,) + image)

    summed = summed.reshape(CORE, HALF * chans, chans)
    grad_sum = jnp.concatenate(
        [summed[0, HALF_G * chans :], summed[1, HALF_G * chans : (HALF - 1) * chans]]
    )
    rows_out = patch // samples
    inverses = inverses.reshape((owners,) + local.shape)
    mine_inv = lax.dynamic_index_in_dim(inverses, table[y_id], 0, keepdims=False)
    a_mine = mine_inv[: rows_out * 9].reshape(rows_out, patch)
    g_mine = mine_inv[rows_out * 9 : rows_out * 9 + chans]
    mixed = jnp.dot(grad_sum, g_mine, preferred_element_type=jnp.float32)
    mixed = mixed / jnp.sqrt(jnp.float32(npos))
    panel = jnp.dot(a_mine.astype(jnp.float32), mixed, precision=lax.Precision.HIGHEST)

    place = jnp.stack([y_id, z_id, dp_id]).astype(jnp.int32)
    rows = owned_rows(summed.reshape(-1, chans, chans), panel.astype(jnp.bfloat16), place)
    step_out, a_out, g_out = results(spread(rows, "y"), table, place, chans, npos)
    return (step_out, a_out[None], g_out[None], in_grad)


def solution(mesh):
    fine = Mesh(mesh.devices.reshape(X, ZL, CORE, ZH, Y), DP + OWNER)
    placed = (
        P(None, DP, OWNER, None, None),
        P(DP, OWNER, None, None),
        P(),
        P(),
        P(OWNER, DP, None),
        P(OWNER, None, None),
    )
    return jax.shard_map(
        shards,
        mesh=fine,
        in_specs=placed,
        out_specs=(
            P(None, DP, None),
            P(OWNER, DP, None),
            P(OWNER, None, None),
            P(DP, OWNER, None, None),
        ),
        check_vma=False,
    )
```

```python
import jax
import jax.numpy as jnp
from jax import lax
from jax.experimental import pallas as pl
from jax.experimental.pallas import tpu as pltpu
from jax.sharding import Mesh, PartitionSpec as P

X, ZL, CORE, ZH, Y = 4, 4, 2, 4, 4
OWNER = ("zh", "y")
DP = ("x", "zl", "core")


def shifted(x, shift, cyclic):
    count = ZH * Y
    pairs = [(i, (i + shift) % count) for i in range(count)]
    if not cyclic:
        pairs = [(a, b) for a, b in pairs if b - a == shift]
    return lax.ppermute(x, OWNER, pairs)


def exchange(x, axis):
    return lax.all_to_all(x, axis, split_axis=0, concat_axis=0, tiled=True)


def spread(x, axis):
    count = lax.axis_size(axis)
    return exchange(jnp.broadcast_to(x[None], (count,) + x.shape), axis)


def scatter_sum(x, axis):
    count = lax.axis_size(axis)
    got = exchange(x.reshape((count, x.shape[0] // count) + x.shape[1:]), axis)
    return jnp.sum(got.astype(jnp.float32), axis=0).astype(jnp.bfloat16)


def windows(rows):
    rows = jnp.pad(rows, ((0, 0), (1, 1), (0, 0)))
    return jnp.stack([rows[i : i + 3] for i in range(rows.shape[0] - 2)])


def cut_windows(rows, whole):
    first, second = rows[:3], rows[1:]
    first = jnp.where(whole, first, first * jnp.array([1, 1, 0], rows.dtype)[:, None, None])
    second = jnp.where(whole, second, second * jnp.array([0, 1, 1], rows.dtype)[:, None, None])
    return jnp.pad(jnp.stack([first, second]), ((0, 0), (0, 0), (1, 1), (0, 0)))


def to_columns(win):
    width = win.shape[2] - 2
    taps = [win[:, ky, kx : kx + width] for ky in range(3) for kx in range(3)]
    return jnp.concatenate(taps, axis=-1).reshape(-1, 9 * win.shape[-1])


def back_columns(win):
    width = win.shape[2] - 2
    taps = [win[:, 2 - ky, 2 - kx : 2 - kx + width] for ky in range(3) for kx in range(3)]
    return jnp.concatenate(taps, axis=-1).reshape(-1, 9 * win.shape[-1])


def silu_slope(value):
    sig = jax.nn.sigmoid(value)
    return sig * (1.0 + value * (1.0 - sig))


def inner_rows(left, right):
    return lax.dot_general(
        left, right, (((0,), (0,)), ((), ())), preferred_element_type=jnp.float32
    )


def block_classes():
    found = {}
    pairs = []
    where = {}
    for a in range(9):
        for b in range(9):
            first, second, flip = a, b, False
            dy, dx = b // 3 - a // 3, b % 3 - a % 3
            if dy < 0 or (dy == 0 and dx < 0):
                first, second, flip = b, a, True
                dy, dx = -dy, -dx
            key = (dy, dx, first // 3 if dy == 0 else -1, first % 3 if dx == 0 else -1)
            if key not in found:
                found[key] = len(pairs)
                pairs.append((first, second))
            where[a, b] = (found[key], flip)
    return pairs, where


PAIRS, WHERE = block_classes()
NG = len(PAIRS)
HALF_G = 15
HALF_D = 5
HALF = HALF_G + HALF_D
SMEM = pl.BlockSpec(memory_space=pltpu.SMEM)
VMEM = pl.BlockSpec(memory_space=pltpu.VMEM)


def halo_rows(f, top):
    def kernel(f_ref, top_ref, up_ref, down_ref):
        for ref, edge in ((up_ref, 0), (down_ref, 1)):
            ref[0:2] = f_ref[3]
            ref[2] = f_ref[2, edge]
            ref[3] = f_ref[0, edge]
            ref[4] = top_ref[edge]
        up_ref[5:7] = f_ref[1]

    row = f.shape[2:]
    return pl.pallas_call(
        kernel,
        out_shape=(
            jax.ShapeDtypeStruct((7,) + row, f.dtype),
            jax.ShapeDtypeStruct((5,) + row, f.dtype),
        ),
        in_specs=[VMEM, VMEM],
        out_specs=(VMEM, VMEM),
        cost_estimate=pl.CostEstimate(flops=0, bytes_accessed=10**6, transcendentals=0),
    )(f, top)


def gram_half(cols, core):
    chans = cols.shape[1] // 9

    def kernel(core_ref, cols_ref, out_ref):
        def some(mine):
            for a in sorted({first for first, _ in mine}):
                wanted = [b for first, b in mine if first == a]
                low = min(wanted)
                left = cols_ref[:, a * chans : (a + 1) * chans].T
                right = cols_ref[:, low * chans : (max(wanted) + 1) * chans]
                product = jnp.dot(left, right, preferred_element_type=jnp.float32)
                for b in wanted:
                    i = mine.index((a, b))
                    part = product[:, (b - low) * chans : (b - low + 1) * chans]
                    out_ref[i * chans : (i + 1) * chans, :] = part.astype(out_ref.dtype)
            for i in range(len(mine), HALF_G):
                out_ref[i * chans : (i + 1) * chans, :] = jnp.zeros((chans, chans), out_ref.dtype)

        @pl.when(core_ref[0] == 0)
        def _():
            some(PAIRS[:HALF_G])

        @pl.when(core_ref[0] != 0)
        def _():
            some(PAIRS[HALF_G:])

    return pl.pallas_call(
        kernel,
        out_shape=jax.ShapeDtypeStruct((HALF_G * chans, chans), jnp.bfloat16),
        in_specs=[SMEM, VMEM],
        out_specs=VMEM,
        compiler_params=pltpu.CompilerParams(vmem_limit_bytes=24 * 2**20),
        cost_estimate=pl.CostEstimate(
            flops=2 * (HALF_G + HALF_D) * cols.shape[0] * chans * chans,
            bytes_accessed=5 * 10**6,
            transcendentals=0,
        ),
    )(core.reshape(1), cols)


def all_half(gram, cols, dpre, parts_g, table, place):
    chans = dpre.shape[-1]

    def kernel(table_ref, place_ref, gram_ref, cols_ref, dpre_ref, parts_ref, out_ref, spare):
        core = place_ref[2] % CORE
        out_ref[: HALF_G * chans, :] = gram_ref[...]

        def put(i, value):
            out_ref[(HALF_G + i) * chans : (HALF_G + i + 1) * chans, :] = value.astype(out_ref.dtype)

        def some(first, last):
            turned = dpre_ref[...].T
            right = cols_ref[:, first * chans : last * chans]
            grad = jnp.dot(turned, right, preferred_element_type=jnp.float32)
            for i in range(last - first):
                put(i, grad[:, i * chans : (i + 1) * chans].T)
            return turned

        @pl.when(core == 0)
        def _():
            some(0, HALF_D)

        @pl.when(core != 0)
        def _():
            turned = some(HALF_D, 9)
            put(9 - HALF_D, jnp.dot(turned, dpre_ref[...], preferred_element_type=jnp.float32))
            owner = table_ref[place_ref[0]]
            mine = lax.div(owner, Y) == place_ref[1]
            rows = parts_ref[lax.rem(owner, Y)].astype(jnp.float32)
            size = chans // (X * ZL)
            first = pl.multiple_of(lax.div(place_ref[2], CORE) * size, size)
            spare[...] = jnp.zeros(spare.shape, spare.dtype)
            spare[pl.ds(first, size), :] = jnp.where(mine, rows[:size], 0.0)
            out_ref[(HALF_G - 1) * chans : HALF_G * chans, :] = spare[...].astype(out_ref.dtype)

    return pl.pallas_call(
        kernel,
        out_shape=jax.ShapeDtypeStruct((HALF * chans, chans), jnp.bfloat16),
        in_specs=[SMEM, SMEM, VMEM, VMEM, VMEM, VMEM],
        out_specs=VMEM,
        scratch_shapes=[pltpu.VMEM((chans, chans), jnp.float32)],
        compiler_params=pltpu.CompilerParams(vmem_limit_bytes=24 * 2**20),
        cost_estimate=pl.CostEstimate(
            flops=2 * HALF_D * cols.shape[0] * chans * chans,
            bytes_accessed=5 * 10**6,
            transcendentals=0,
        ),
    )(table, place, gram, cols, dpre, parts_g)


def owned_rows(blocks, panel, place):
    chans = blocks.shape[-1]
    rows = panel.shape[0]
    wide = 9 * chans
    slots = [i // HALF_G * HALF + i % HALF_G for i in range(NG)]
    index = jnp.array([slots[WHERE[a, b][0]] for a in range(9) for b in range(9)], jnp.int32)
    flips = jnp.array([int(WHERE[a, b][1]) for a in range(9) for b in range(9)], jnp.int32)

    def kernel(index_ref, flip_ref, place_ref, blocks_ref, panel_ref, out_ref, band):
        start = place_ref[2] * rows
        tap = lax.div(start, chans)
        for t in range(2):
            a = jnp.minimum(tap + t, 8)
            for b in range(9):
                block = blocks_ref[index_ref[a * 9 + b]].astype(jnp.float32)
                flip = flip_ref[a * 9 + b] != 0
                band[t * chans : (t + 1) * chans, b * chans : (b + 1) * chans] = jnp.where(
                    flip, block.T, block
                )
        inside = start - tap * chans
        base = pl.multiple_of(lax.div(inside, 8) * 8, 8)
        got = band[pl.ds(base, rows + 4), :]
        odd = inside != base
        out_ref[:, :wide] = jnp.where(odd, got[4:], got[:rows]).astype(out_ref.dtype)
        out_ref[:, wide : wide + chans] = panel_ref[...]
        out_ref[:, wide + chans :] = jnp.zeros((rows, 4 * chans), out_ref.dtype)
        part = chans // 4
        for q in range(4):
            lanes = slice(wide + (q + 1) * chans, wide + (q + 2) * chans)
            out_ref[:part, lanes] = blocks_ref[2 * HALF - 1, q * part : (q + 1) * part, :]

    return pl.pallas_call(
        kernel,
        out_shape=jax.ShapeDtypeStruct((rows, wide + 5 * chans), jnp.bfloat16),
        in_specs=[SMEM, SMEM, SMEM, VMEM, VMEM],
        out_specs=VMEM,
        scratch_shapes=[pltpu.VMEM((2 * chans, wide), jnp.float32)],
        compiler_params=pltpu.CompilerParams(vmem_limit_bytes=16 * 2**20),
        cost_estimate=pl.CostEstimate(flops=10**6, bytes_accessed=2 * 10**6, transcendentals=0),
    )(index, flips, place, blocks, panel)


def results(got, table, place, chans, count):
    layers, rows, _ = got.shape
    wide = 9 * chans

    def kernel(table_ref, place_ref, got_ref, step_ref, fac_ref, own_ref):
        owner = place_ref[1] * Y + place_ref[0]
        lay = jnp.int32(0)
        scale = jnp.float32(0.0)
        for l in range(layers):
            mine = table_ref[l] == owner
            lay = jnp.where(mine, l, lay)
            scale = jnp.where(mine, jnp.float32(1.0 / count), scale)
            step_ref[l] = got_ref[l, :, wide : wide + chans]
        fac_ref[...] = got_ref[lay, :, :wide].astype(jnp.float32) * scale
        part = chans // 4
        for q in range(4):
            lanes = slice(wide + (q + 1) * chans, wide + (q + 2) * chans)
            own_ref[q * part : (q + 1) * part, :] = (
                got_ref[lay, :part, lanes].astype(jnp.float32) * scale
            )

    return pl.pallas_call(
        kernel,
        out_shape=(
            jax.ShapeDtypeStruct((layers, rows, chans), jnp.bfloat16),
            jax.ShapeDtypeStruct((rows, wide), jnp.float32),
            jax.ShapeDtypeStruct((chans, chans), jnp.float32),
        ),
        in_specs=[SMEM, SMEM, VMEM],

        cost_estimate=pl.CostEstimate(flops=10**5, bytes_accessed=10**6, transcendentals=0),
    )(table, place, got)


def shards(feats, top_grad, weights, table, a_inv, g_inv):
    num_layers, _, rows_dev, width, chans = feats.shape
    owners = lax.axis_size(OWNER)
    samples = lax.axis_size(DP)
    owner_id = lax.axis_index(OWNER)
    dp_id = lax.axis_index(DP)
    y_id = lax.axis_index("y")
    z_id = lax.axis_index("zh")
    npos = samples * rows_dev * owners * width
    patch = 9 * chans
    inner = owner_id < owners - 1
    f = feats[:, 0]
    top = top_grad[0]

    own_a = a_inv.reshape(-1, chans)
    own_a = jnp.pad(own_a, ((0, -own_a.shape[0] % 16), (0, 0)))
    own_a, f_first, top_first = lax.optimization_barrier((own_a, f, top))
    inverses = lax.all_gather(own_a, OWNER, axis=0, tiled=True)
    to_above, to_below = halo_rows(f_first, top_first)
    below = shifted(to_above, -1, True)
    above = shifted(to_below, 1, False)
    below1 = below[5:]
    below = jnp.where(inner, below[:5], jnp.zeros_like(below[:5]))
    wide3 = jnp.concatenate([above[:2], f[3], below[:2]])
    strips = [
        jnp.concatenate([above[3:4], f[0], below[3:4]]),
        jnp.concatenate([f[1], below1]),
        jnp.concatenate([above[2:3], f[2], below[2:3]]),
        wide3[1:5],
    ]
    core_id = lax.axis_index("core")

    def to_layers(x):
        return exchange(jnp.broadcast_to(x[None], (CORE,) + x.shape).reshape((-1,) + x.shape[1:]), ("core", "y"))

    flipped = jnp.transpose(weights.reshape(num_layers, 9, chans, chans), (0, 1, 3, 2)).reshape(
        num_layers, patch, chans
    )

    def slope(layer, win):
        pre = jnp.dot(to_columns(win), weights[layer], preferred_element_type=jnp.float32)
        return silu_slope(pre)

    def times(grad_in, slopes):
        return (grad_in.reshape(slopes.shape).astype(jnp.float32) * slopes).astype(jnp.bfloat16)

    def back(layer, win):
        return jnp.dot(
            back_columns(win), flipped[layer], preferred_element_type=jnp.float32
        ).astype(jnp.bfloat16)

    image = (rows_dev, width, chans)
    top_wide = jnp.concatenate([above[4:5], top, below[4:5]])
    dpre3 = times(top_wide, slope(3, windows(wide3))).reshape((rows_dev + 2, width, chans))
    dpre2 = times(back(3, windows(dpre3)), slope(2, windows(strips[2]))).reshape(image)
    after = shifted(dpre2, -1, True)
    dy1 = back(2, cut_windows(jnp.concatenate([dpre2, after]), inner))
    dpre1 = times(dy1, slope(1, cut_windows(strips[1], inner))).reshape(image)
    trimmed = [
        jnp.concatenate([jnp.where(y_id == 0, rows[:1], rows[3:]), rows[1:3]]) for rows in strips
    ]
    place = jnp.stack([y_id, z_id, dp_id]).astype(jnp.int32)
    size = chans // (X * ZL)
    own_g = lax.dynamic_slice_in_dim(g_inv[0], dp_id // CORE * size, size, 0).astype(jnp.bfloat16)
    own_g = jnp.pad(own_g, ((0, -size % 16), (0, 0)))
    strip_rows = (rows_dev + 1) * width
    stacked = jnp.concatenate(
        [
            jnp.stack(trimmed).reshape(num_layers, strip_rows, chans),
            jnp.broadcast_to(own_g[None], (num_layers,) + own_g.shape),
        ],
        axis=1,
    )
    stacked, dpre1 = lax.optimization_barrier((stacked, dpre1))
    before = shifted(dpre1, 1, True)
    from_layers = to_layers(stacked)
    layer_strips = from_layers[:, :strip_rows].reshape(-1, rows_dev + 1, width, chans)
    edge_top = jnp.where(owner_id > 0, before[:1], jnp.zeros_like(before[:1]))
    edge_end = jnp.where(inner, dpre1[1:], jnp.zeros_like(dpre1[1:]))
    dy0 = back(1, windows(jnp.concatenate([edge_top, before[1:], dpre1[:1], edge_end])))
    dpre0 = times(dy0, slope(0, windows(strips[0]))).reshape(image)

    images = layer_strips.reshape((CORE, Y) + layer_strips.shape[1:])
    last_one = (y_id == 1) & (z_id == ZH - 1)
    seam = jnp.zeros((Y * rows_dev, 3), bool).at[-2, 2].set(True).at[-1, 0].set(True)
    cols = []
    for image_rows in images:
        middle = image_rows[:, 1:].reshape((-1,) + image_rows.shape[2:])
        win = windows(jnp.concatenate([image_rows[0, :1], middle, image_rows[-1, :1]]))
        cut = (seam & last_one)[:, :, None, None]
        cols.append(to_columns(jnp.where(cut, jnp.zeros_like(win), win)))
    cols = jnp.concatenate(cols)
    gram = gram_half(cols, core_id)

    layer_dpre = to_layers(jnp.stack([dpre0, dpre1, dpre2, dpre3[1:3]]))
    parts = all_half(
        gram, cols, layer_dpre.reshape(-1, chans), from_layers[:Y, strip_rows:], table, place
    )

    piece = scatter_sum(parts, ("x", "zl"))
    piece, inverses = lax.optimization_barrier((piece, inverses))
    total = spread(piece, "zh")
    total = jnp.sum(total.astype(jnp.float32), axis=0).astype(jnp.bfloat16)
    summed = spread(spread(spread(total, "zl"), "x"), "core")

    in_grad_win = jnp.concatenate([shifted(dpre0[1:], 1, False), dpre0, shifted(dpre0[:1], -1, False)])
    in_grad = back(0, windows(in_grad_win)).reshape((1,) + image)

    summed = summed.reshape(CORE, HALF * chans, chans)
    grad_sum = jnp.concatenate(
        [summed[0, HALF_G * chans :], summed[1, HALF_G * chans : (HALF - 1) * chans]]
    )
    rows_out = patch // samples
    inverses = inverses.reshape((owners,) + own_a.shape)
    mine_inv = lax.dynamic_index_in_dim(inverses, table[y_id], 0, keepdims=False)
    a_mine = mine_inv[: rows_out * 9].reshape(rows_out, patch)
    g_mine = summed[1, (HALF_G - 1) * chans : HALF_G * chans]
    mixed = jnp.dot(grad_sum, g_mine, preferred_element_type=jnp.float32)
    mixed = mixed / jnp.sqrt(jnp.float32(npos))
    panel = jnp.dot(a_mine.astype(jnp.float32), mixed, precision=lax.Precision.HIGHEST)

    rows = owned_rows(summed.reshape(-1, chans, chans), panel.astype(jnp.bfloat16), place)
    step_out, a_out, g_out = results(spread(rows, "y"), table, place, chans, npos)
    return (step_out, a_out[None], g_out[None], in_grad)


def solution(mesh):
    fine = Mesh(mesh.devices.reshape(X, ZL, CORE, ZH, Y), DP + OWNER)
    placed = (
        P(None, DP, OWNER, None, None),
        P(DP, OWNER, None, None),
        P(),
        P(),
        P(OWNER, DP, None),
        P(OWNER, None, None),
    )
    return jax.shard_map(
        shards,
        mesh=fine,
        in_specs=placed,
        out_specs=(
            P(None, DP, None),
            P(OWNER, DP, None),
            P(OWNER, None, None),
            P(DP, OWNER, None, None),
        ),
        check_vma=False,
    )
```

```python
import jax
import jax.numpy as jnp
from jax import lax
from jax.experimental import pallas as pl
from jax.experimental.pallas import tpu as pltpu
from jax.sharding import Mesh, PartitionSpec as P

X, ZL, CORE, ZH, Y = 4, 4, 2, 4, 4
OWNER = ("zh", "y")
DP = ("x", "zl", "core")


def shifted(x, shift, cyclic):
    count = ZH * Y
    pairs = [(i, (i + shift) % count) for i in range(count)]
    if not cyclic:
        pairs = [(a, b) for a, b in pairs if b - a == shift]
    return lax.ppermute(x, OWNER, pairs)


def paired(x, axis, step):
    return lax.ppermute(x, axis, [(i, i ^ 1 if step == 0 else 3 - i) for i in range(4)])


def exchange(x, axis):
    return lax.all_to_all(x, axis, split_axis=0, concat_axis=0, tiled=True)


def spread(x, axis):
    count = lax.axis_size(axis)
    return exchange(jnp.broadcast_to(x[None], (count,) + x.shape), axis)


def scatter_sum(x, axis):
    count = lax.axis_size(axis)
    got = exchange(x.reshape((count, x.shape[0] // count) + x.shape[1:]), axis)
    return jnp.sum(got.astype(jnp.float32), axis=0).astype(jnp.bfloat16)


def windows(rows):
    rows = jnp.pad(rows, ((0, 0), (1, 1), (0, 0)))
    return jnp.stack([rows[i : i + 3] for i in range(rows.shape[0] - 2)])


def cut_windows(rows, whole):
    first, second = rows[:3], rows[1:]
    first = jnp.where(whole, first, first * jnp.array([1, 1, 0], rows.dtype)[:, None, None])
    second = jnp.where(whole, second, second * jnp.array([0, 1, 1], rows.dtype)[:, None, None])
    return jnp.pad(jnp.stack([first, second]), ((0, 0), (0, 0), (1, 1), (0, 0)))


def to_columns(win):
    width = win.shape[2] - 2
    taps = [win[:, ky, kx : kx + width] for ky in range(3) for kx in range(3)]
    return jnp.concatenate(taps, axis=-1).reshape(-1, 9 * win.shape[-1])


def back_columns(win):
    width = win.shape[2] - 2
    taps = [win[:, 2 - ky, 2 - kx : 2 - kx + width] for ky in range(3) for kx in range(3)]
    return jnp.concatenate(taps, axis=-1).reshape(-1, 9 * win.shape[-1])


def silu_slope(value):
    sig = jax.nn.sigmoid(value)
    return sig * (1.0 + value * (1.0 - sig))


def inner_rows(left, right):
    return lax.dot_general(
        left, right, (((0,), (0,)), ((), ())), preferred_element_type=jnp.float32
    )


def block_classes():
    found = {}
    pairs = []
    where = {}
    for a in range(9):
        for b in range(9):
            first, second, flip = a, b, False
            dy, dx = b // 3 - a // 3, b % 3 - a % 3
            if dy < 0 or (dy == 0 and dx < 0):
                first, second, flip = b, a, True
                dy, dx = -dy, -dx
            key = (dy, dx, first // 3 if dy == 0 else -1, first % 3 if dx == 0 else -1)
            if key not in found:
                found[key] = len(pairs)
                pairs.append((first, second))
            where[a, b] = (found[key], flip)
    return pairs, where


PAIRS, WHERE = block_classes()
NG = len(PAIRS)
HALF_G = 16
HALF_D = 5
FAC_ROWS = 128
GRAD_ROWS = 40
PIECE_ROWS = 176
SMEM = pl.BlockSpec(memory_space=pltpu.SMEM)
VMEM = pl.BlockSpec(memory_space=pltpu.VMEM)


def halo_rows(f, top):
    def kernel(f_ref, top_ref, up_ref, down_ref):
        for ref, edge in ((up_ref, 0), (down_ref, 1)):
            ref[0:2] = f_ref[3]
            ref[2] = f_ref[2, edge]
            ref[3] = f_ref[0, edge]
            ref[4] = top_ref[edge]
        up_ref[5:7] = f_ref[1]

    row = f.shape[2:]
    return pl.pallas_call(
        kernel,
        out_shape=(
            jax.ShapeDtypeStruct((7,) + row, f.dtype),
            jax.ShapeDtypeStruct((5,) + row, f.dtype),
        ),
        in_specs=[VMEM, VMEM],
        out_specs=(VMEM, VMEM),
        cost_estimate=pl.CostEstimate(flops=0, bytes_accessed=10**6, transcendentals=0),
    )(f, top)


def gram_half(cols, core):
    chans = cols.shape[1] // 9

    def kernel(core_ref, cols_ref, out_ref):
        def some(mine):
            for a in sorted({first for first, _ in mine}):
                wanted = [b for first, b in mine if first == a]
                low = min(wanted)
                left = cols_ref[:, a * chans : (a + 1) * chans].T
                right = cols_ref[:, low * chans : (max(wanted) + 1) * chans]
                product = jnp.dot(left, right, preferred_element_type=jnp.float32)
                for b in wanted:
                    i = mine.index((a, b))
                    part = product[:, (b - low) * chans : (b - low + 1) * chans]
                    out_ref[i * chans : (i + 1) * chans, :] = part.astype(out_ref.dtype)
            for i in range(len(mine), HALF_G):
                out_ref[i * chans : (i + 1) * chans, :] = jnp.zeros((chans, chans), out_ref.dtype)

        @pl.when(core_ref[0] == 0)
        def _():
            some(PAIRS[:HALF_G])

        @pl.when(core_ref[0] != 0)
        def _():
            some(PAIRS[HALF_G:])

    return pl.pallas_call(
        kernel,
        out_shape=jax.ShapeDtypeStruct((HALF_G * chans, chans), jnp.bfloat16),
        in_specs=[SMEM, VMEM],
        out_specs=VMEM,
        compiler_params=pltpu.CompilerParams(vmem_limit_bytes=24 * 2**20),
        cost_estimate=pl.CostEstimate(
            flops=2 * (HALF_G + HALF_D) * cols.shape[0] * chans * chans,
            bytes_accessed=5 * 10**6,
            transcendentals=0,
        ),
    )(core.reshape(1), cols)


def all_half(gram, cols, dpre, core):
    chans = dpre.shape[-1]

    def kernel(core_ref, gram_ref, cols_ref, dpre_ref, out_ref, dense):
        for k in range(HALF_G):
            out_ref[k, :FAC_ROWS, :] = gram_ref[k * chans : (k + 1) * chans, :]
        dense[...] = jnp.zeros(dense.shape, dense.dtype)

        def some(first, last):
            turned = dpre_ref[...].T
            right = cols_ref[:, first * chans : last * chans]
            grad = jnp.dot(turned, right, preferred_element_type=jnp.float32)
            for i in range(last - first):
                dense[i * chans : (i + 1) * chans, :] = grad[:, i * chans : (i + 1) * chans].T
            return turned

        @pl.when(core_ref[0] == 0)
        def _():
            some(0, HALF_D)

        @pl.when(core_ref[0] != 0)
        def _():
            turned = some(HALF_D, 9)
            own = jnp.dot(turned, dpre_ref[...], preferred_element_type=jnp.float32)
            out_ref[NG - HALF_G, :FAC_ROWS, :] = own.astype(out_ref.dtype)

        for k in range(HALF_G):
            rows = dense[k * GRAD_ROWS : k * GRAD_ROWS + PIECE_ROWS - FAC_ROWS, :]
            out_ref[k, FAC_ROWS:, :] = rows.astype(out_ref.dtype)

    return pl.pallas_call(
        kernel,
        out_shape=jax.ShapeDtypeStruct((HALF_G, PIECE_ROWS, chans), jnp.bfloat16),
        in_specs=[SMEM, VMEM, VMEM, VMEM],
        out_specs=VMEM,
        scratch_shapes=[pltpu.VMEM((HALF_D * chans + 16, chans), jnp.float32)],
        compiler_params=pltpu.CompilerParams(vmem_limit_bytes=24 * 2**20),
        cost_estimate=pl.CostEstimate(
            flops=2 * HALF_D * cols.shape[0] * chans * chans,
            bytes_accessed=5 * 10**6,
            transcendentals=0,
        ),
    )(core.reshape(1), gram, cols, dpre)


def choose(which, table, place, *arrays):
    def kernel(table_ref, place_ref, *refs):
        number = which(table_ref, place_ref[0], place_ref[1])
        for k, ref in enumerate(refs[:-1]):

            @pl.when(number == k)
            def _(ref=ref):
                refs[-1][...] = ref[...]

    return pl.pallas_call(
        kernel,
        out_shape=jax.ShapeDtypeStruct(arrays[0].shape, arrays[0].dtype),
        in_specs=[SMEM, SMEM] + [VMEM] * len(arrays),
        out_specs=VMEM,
        cost_estimate=pl.CostEstimate(flops=0, bytes_accessed=500000, transcendentals=0),
    )(table, place, *arrays)


def layer_at(table_ref, owner):
    lay = jnp.int32(0)
    for l in range(1, table_ref.shape[0]):
        lay = jnp.where(table_ref[l] == owner, l, lay)
    return lay


def for_groups(table, place, held, piece):
    def kernel(table_ref, place_ref, held_ref, piece_ref, out_ref):
        for z in range(ZH):
            out_ref[z, :, :FAC_ROWS, :] = held_ref[layer_at(table_ref, z * Y + place_ref[0])]
            out_ref[z, :, FAC_ROWS:, :] = piece_ref[:, FAC_ROWS:, :]

    return pl.pallas_call(
        kernel,
        out_shape=jax.ShapeDtypeStruct((ZH,) + piece.shape, piece.dtype),
        in_specs=[SMEM, SMEM, VMEM, VMEM],
        out_specs=VMEM,
        cost_estimate=pl.CostEstimate(flops=0, bytes_accessed=500000, transcendentals=0),
    )(table, place, held, piece)


def factor_rows(blocks, table, place, rows, count):
    chans = blocks.shape[-1]
    index = jnp.array([WHERE[a, b][0] for a in range(9) for b in range(9)], jnp.int32)
    flips = jnp.array([int(WHERE[a, b][1]) for a in range(9) for b in range(9)], jnp.int32)

    def kernel(index_ref, flip_ref, table_ref, place_ref, blocks_ref, out_ref, own_ref, band):
        owner = place_ref[1] * Y + place_ref[0]
        scale = jnp.float32(0.0)
        for l in range(table_ref.shape[0]):
            scale = jnp.where(table_ref[l] == owner, jnp.float32(1.0 / count), scale)
        start = place_ref[2] * rows
        tap = lax.div(start, chans)
        for t in range(2):
            a = jnp.minimum(tap + t, 8)
            for b in range(9):
                block = blocks_ref[index_ref[a * 9 + b], :chans, :].astype(jnp.float32)
                flip = flip_ref[a * 9 + b] != 0
                band[t * chans : (t + 1) * chans, b * chans : (b + 1) * chans] = jnp.where(
                    flip, block.T, block
                )
        inside = start - tap * chans
        base = pl.multiple_of(lax.div(inside, 8) * 8, 8)
        got = band[pl.ds(base, rows + 4), :]
        odd = inside != base
        out_ref[...] = jnp.where(odd, got[4:], got[:rows]) * scale
        own_ref[...] = blocks_ref[NG, :chans, :].astype(jnp.float32) * scale

    return pl.pallas_call(
        kernel,
        out_shape=(
            jax.ShapeDtypeStruct((rows, 9 * chans), jnp.float32),
            jax.ShapeDtypeStruct((chans, chans), jnp.float32),
        ),
        in_specs=[SMEM, SMEM, SMEM, SMEM, VMEM],
        out_specs=(VMEM, VMEM),
        scratch_shapes=[pltpu.VMEM((2 * chans, 9 * chans), jnp.float32)],
        compiler_params=pltpu.CompilerParams(vmem_limit_bytes=16 * 2**20),
        cost_estimate=pl.CostEstimate(flops=10**6, bytes_accessed=2 * 10**6, transcendentals=0),
    )(index, flips, table, place, blocks)


def shards(feats, top_grad, weights, table, a_inv, g_inv):
    num_layers, _, rows_dev, width, chans = feats.shape
    owners = lax.axis_size(OWNER)
    samples = lax.axis_size(DP)
    owner_id = lax.axis_index(OWNER)
    dp_id = lax.axis_index(DP)
    y_id = lax.axis_index("y")
    z_id = lax.axis_index("zh")
    npos = samples * rows_dev * owners * width
    patch = 9 * chans
    inner = owner_id < owners - 1
    f = feats[:, 0]
    top = top_grad[0]

    to_above, to_below = halo_rows(f, top)
    below = shifted(to_above, -1, True)
    above = shifted(to_below, 1, False)
    below1 = below[5:]
    below = jnp.where(inner, below[:5], jnp.zeros_like(below[:5]))
    wide3 = jnp.concatenate([above[:2], f[3], below[:2]])
    strips = [
        jnp.concatenate([above[3:4], f[0], below[3:4]]),
        jnp.concatenate([f[1], below1]),
        jnp.concatenate([above[2:3], f[2], below[2:3]]),
        wide3[1:5],
    ]
    core_id = lax.axis_index("core")

    def to_layers(x):
        return exchange(jnp.broadcast_to(x[None], (CORE,) + x.shape).reshape((-1,) + x.shape[1:]), ("core", "y"))

    flipped = jnp.transpose(weights.reshape(num_layers, 9, chans, chans), (0, 1, 3, 2)).reshape(
        num_layers, patch, chans
    )

    def slope(layer, win):
        pre = jnp.dot(to_columns(win), weights[layer], preferred_element_type=jnp.float32)
        return silu_slope(pre)

    def times(grad_in, slopes):
        return (grad_in.reshape(slopes.shape).astype(jnp.float32) * slopes).astype(jnp.bfloat16)

    def back(layer, win):
        return jnp.dot(
            back_columns(win), flipped[layer], preferred_element_type=jnp.float32
        ).astype(jnp.bfloat16)

    image = (rows_dev, width, chans)
    top_wide = jnp.concatenate([above[4:5], top, below[4:5]])
    dpre3 = times(top_wide, slope(3, windows(wide3))).reshape((rows_dev + 2, width, chans))
    dpre2 = times(back(3, windows(dpre3)), slope(2, windows(strips[2]))).reshape(image)
    after = shifted(dpre2, -1, True)
    dy1 = back(2, cut_windows(jnp.concatenate([dpre2, after]), inner))
    dpre1 = times(dy1, slope(1, cut_windows(strips[1], inner))).reshape(image)
    trimmed = [
        jnp.concatenate([jnp.where(y_id == 0, rows[:1], rows[3:]), rows[1:3]]) for rows in strips
    ]
    local = jnp.concatenate([a_inv.reshape(-1, chans), g_inv[0].astype(jnp.bfloat16)])
    stacked, dpre1, local = lax.optimization_barrier((jnp.stack(trimmed), dpre1, local))
    before = shifted(dpre1, 1, True)
    layer_strips = to_layers(stacked)
    near = paired(local, "y", 0)
    edge_top = jnp.where(owner_id > 0, before[:1], jnp.zeros_like(before[:1]))
    edge_end = jnp.where(inner, dpre1[1:], jnp.zeros_like(dpre1[1:]))
    dy0 = back(1, windows(jnp.concatenate([edge_top, before[1:], dpre1[:1], edge_end])))
    dpre0 = times(dy0, slope(0, windows(strips[0]))).reshape(image)

    images = layer_strips.reshape((CORE, Y) + layer_strips.shape[1:])
    last_one = (y_id == 1) & (z_id == ZH - 1)
    seam = jnp.zeros((Y * rows_dev, 3), bool).at[-2, 2].set(True).at[-1, 0].set(True)
    cols = []
    for image_rows in images:
        middle = image_rows[:, 1:].reshape((-1,) + image_rows.shape[2:])
        win = windows(jnp.concatenate([image_rows[0, :1], middle, image_rows[-1, :1]]))
        cut = (seam & last_one)[:, :, None, None]
        cols.append(to_columns(jnp.where(cut, jnp.zeros_like(win), win)))
    cols = jnp.concatenate(cols)
    gram = gram_half(cols, core_id)

    def for_partner(table_ref, y, z):
        return jnp.where((table_ref[3 - y] & 3) == y, 0, 1)

    def in_group(table_ref, y, z):
        want = table_ref[y] & 3
        return jnp.where(want == y, 0, jnp.where(want == (y ^ 1), 1, 2))

    def beside(table_ref, y, z):
        return jnp.where((table_ref[y] >> 2) == (z ^ 1), 1, 0)

    layer_dpre = to_layers(jnp.stack([dpre0, dpre1, dpre2, dpre3[1:3]]))
    parts = all_half(gram, cols, layer_dpre.reshape(-1, chans), core_id)

    place = jnp.stack([y_id, z_id, dp_id]).astype(jnp.int32)
    parts, local, near = lax.optimization_barrier((parts, local, near))
    away = choose(for_partner, table, place, local, near)
    found = choose(in_group, table, place, local, near, paired(away, "y", 1))
    found = choose(beside, table, place, found, paired(found, "zh", 0))
    piece = scatter_sum(parts, ("x", "zl"))
    piece, found = lax.optimization_barrier((piece, found))
    source = jnp.sum(jnp.where(jnp.arange(num_layers) == y_id, table, 0))
    inverses = jnp.where((source >> 3) == (z_id >> 1), found, paired(found, "zh", 1))
    held = spread(piece[:, :FAC_ROWS], "y")
    total = exchange(for_groups(table, place, held, piece), "zh")
    total = jnp.sum(total.astype(jnp.float32), axis=0).astype(jnp.bfloat16)
    summed = spread(spread(spread(total, "zl"), "x"), "core")

    in_grad_win = jnp.concatenate([shifted(dpre0[1:], 1, False), dpre0, shifted(dpre0[:1], -1, False)])
    in_grad = back(0, windows(in_grad_win)).reshape((1,) + image)

    stats = summed.reshape(CORE * HALF_G, PIECE_ROWS, chans)
    grad_sum = stats[:, FAC_ROWS : FAC_ROWS + GRAD_ROWS].reshape(-1, chans)[:patch]
    rows_out = patch // samples
    a_mine = inverses[: rows_out * 9].reshape(rows_out, patch)
    mixed = jnp.dot(grad_sum, inverses[rows_out * 9 :], preferred_element_type=jnp.float32)
    mixed = mixed / jnp.sqrt(jnp.float32(npos))
    panel = jnp.dot(a_mine.astype(jnp.float32), mixed, precision=lax.Precision.HIGHEST)
    step_out = spread(panel.astype(jnp.bfloat16), "y")

    a_out, g_out = factor_rows(stats, table, place, rows_out, npos)
    a_out, g_out = a_out[None], g_out[None]
    return (step_out, a_out, g_out, in_grad)


def solution(mesh):
    fine = Mesh(mesh.devices.reshape(X, ZL, CORE, ZH, Y), DP + OWNER)
    placed = (
        P(None, DP, OWNER, None, None),
        P(DP, OWNER, None, None),
        P(),
        P(),
        P(OWNER, DP, None),
        P(OWNER, None, None),
    )
    return jax.shard_map(
        shards,
        mesh=fine,
        in_specs=placed,
        out_specs=(
            P(None, DP, None),
            P(OWNER, DP, None),
            P(OWNER, None, None),
            P(DP, OWNER, None, None),
        ),
        check_vma=False,
    )
```

```python
import jax
import jax.numpy as jnp
from jax import lax
from jax.experimental import pallas as pl
from jax.experimental.pallas import tpu as pltpu
from jax.sharding import Mesh, PartitionSpec as P

X, ZL, CORE, ZH, Y = 4, 4, 2, 4, 4
OWNER = ("zh", "y")
DP = ("x", "zl", "core")


def shifted(x, shift, cyclic):
    count = ZH * Y
    pairs = [(i, (i + shift) % count) for i in range(count)]
    if not cyclic:
        pairs = [(a, b) for a, b in pairs if b - a == shift]
    return lax.ppermute(x, OWNER, pairs)


def paired(x, axis, step):
    return lax.ppermute(x, axis, [(i, i ^ 1 if step == 0 else 3 - i) for i in range(4)])


def exchange(x, axis):
    return lax.all_to_all(x, axis, split_axis=0, concat_axis=0, tiled=True)


def spread(x, axis):
    count = lax.axis_size(axis)
    return exchange(jnp.broadcast_to(x[None], (count,) + x.shape), axis)


def scatter_sum(x, axis):
    count = lax.axis_size(axis)
    got = exchange(x.reshape((count, x.shape[0] // count) + x.shape[1:]), axis)
    return jnp.sum(got.astype(jnp.float32), axis=0).astype(jnp.bfloat16)


def windows(rows):
    rows = jnp.pad(rows, ((0, 0), (1, 1), (0, 0)))
    return jnp.stack([rows[i : i + 3] for i in range(rows.shape[0] - 2)])


def cut_windows(rows, whole):
    first, second = rows[:3], rows[1:]
    first = jnp.where(whole, first, first * jnp.array([1, 1, 0], rows.dtype)[:, None, None])
    second = jnp.where(whole, second, second * jnp.array([0, 1, 1], rows.dtype)[:, None, None])
    return jnp.pad(jnp.stack([first, second]), ((0, 0), (0, 0), (1, 1), (0, 0)))


def to_columns(win):
    width = win.shape[2] - 2
    taps = [win[:, ky, kx : kx + width] for ky in range(3) for kx in range(3)]
    return jnp.concatenate(taps, axis=-1).reshape(-1, 9 * win.shape[-1])


def back_columns(win):
    width = win.shape[2] - 2
    taps = [win[:, 2 - ky, 2 - kx : 2 - kx + width] for ky in range(3) for kx in range(3)]
    return jnp.concatenate(taps, axis=-1).reshape(-1, 9 * win.shape[-1])


def silu_slope(value):
    sig = jax.nn.sigmoid(value)
    return sig * (1.0 + value * (1.0 - sig))


def inner_rows(left, right):
    return lax.dot_general(
        left, right, (((0,), (0,)), ((), ())), preferred_element_type=jnp.float32
    )


def block_classes():
    found = {}
    pairs = []
    where = {}
    for a in range(9):
        for b in range(9):
            first, second, flip = a, b, False
            dy, dx = b // 3 - a // 3, b % 3 - a % 3
            if dy < 0 or (dy == 0 and dx < 0):
                first, second, flip = b, a, True
                dy, dx = -dy, -dx
            key = (dy, dx, first // 3 if dy == 0 else -1, first % 3 if dx == 0 else -1)
            if key not in found:
                found[key] = len(pairs)
                pairs.append((first, second))
            where[a, b] = (found[key], flip)
    return pairs, where


PAIRS, WHERE = block_classes()
NG = len(PAIRS)
HALF_G = 16
HALF_D = 5
FAC_ROWS = 128
GRAD_ROWS = 40
PIECE_ROWS = 176
SMEM = pl.BlockSpec(memory_space=pltpu.SMEM)
VMEM = pl.BlockSpec(memory_space=pltpu.VMEM)


def halo_rows(f, top):
    def kernel(f_ref, top_ref, up_ref, down_ref):
        for ref, edge in ((up_ref, 0), (down_ref, 1)):
            ref[0:2] = f_ref[3]
            ref[2] = f_ref[2, edge]
            ref[3] = f_ref[0, edge]
            ref[4] = top_ref[edge]
        up_ref[5:7] = f_ref[1]

    row = f.shape[2:]
    return pl.pallas_call(
        kernel,
        out_shape=(
            jax.ShapeDtypeStruct((7,) + row, f.dtype),
            jax.ShapeDtypeStruct((5,) + row, f.dtype),
        ),
        in_specs=[VMEM, VMEM],
        out_specs=(VMEM, VMEM),
        cost_estimate=pl.CostEstimate(flops=0, bytes_accessed=10**6, transcendentals=0),
    )(f, top)


def gram_half(cols, core):
    chans = cols.shape[1] // 9

    def kernel(core_ref, cols_ref, out_ref):
        def some(mine):
            for a in sorted({first for first, _ in mine}):
                wanted = [b for first, b in mine if first == a]
                low = min(wanted)
                left = cols_ref[:, a * chans : (a + 1) * chans].T
                right = cols_ref[:, low * chans : (max(wanted) + 1) * chans]
                product = jnp.dot(left, right, preferred_element_type=jnp.float32)
                for b in wanted:
                    i = mine.index((a, b))
                    part = product[:, (b - low) * chans : (b - low + 1) * chans]
                    out_ref[i * chans : (i + 1) * chans, :] = part.astype(out_ref.dtype)
            for i in range(len(mine), HALF_G):
                out_ref[i * chans : (i + 1) * chans, :] = jnp.zeros((chans, chans), out_ref.dtype)

        @pl.when(core_ref[0] == 0)
        def _():
            some(PAIRS[:HALF_G])

        @pl.when(core_ref[0] != 0)
        def _():
            some(PAIRS[HALF_G:])

    return pl.pallas_call(
        kernel,
        out_shape=jax.ShapeDtypeStruct((HALF_G * chans, chans), jnp.bfloat16),
        in_specs=[SMEM, VMEM],
        out_specs=VMEM,
        compiler_params=pltpu.CompilerParams(vmem_limit_bytes=24 * 2**20),
        cost_estimate=pl.CostEstimate(
            flops=2 * (HALF_G + HALF_D) * cols.shape[0] * chans * chans,
            bytes_accessed=5 * 10**6,
            transcendentals=0,
        ),
    )(core.reshape(1), cols)


def all_half(gram, cols, dpre, core):
    chans = dpre.shape[-1]

    def kernel(core_ref, gram_ref, cols_ref, dpre_ref, out_ref, dense):
        for k in range(HALF_G):
            out_ref[k, :FAC_ROWS, :] = gram_ref[k * chans : (k + 1) * chans, :]
        dense[...] = jnp.zeros(dense.shape, dense.dtype)

        def some(first, last):
            turned = dpre_ref[...].T
            right = cols_ref[:, first * chans : last * chans]
            grad = jnp.dot(turned, right, preferred_element_type=jnp.float32)
            for i in range(last - first):
                dense[i * chans : (i + 1) * chans, :] = grad[:, i * chans : (i + 1) * chans].T
            return turned

        @pl.when(core_ref[0] == 0)
        def _():
            some(0, HALF_D)

        @pl.when(core_ref[0] != 0)
        def _():
            turned = some(HALF_D, 9)
            own = jnp.dot(turned, dpre_ref[...], preferred_element_type=jnp.float32)
            out_ref[NG - HALF_G, :FAC_ROWS, :] = own.astype(out_ref.dtype)

        for k in range(HALF_G):
            rows = dense[k * GRAD_ROWS : k * GRAD_ROWS + PIECE_ROWS - FAC_ROWS, :]
            out_ref[k, FAC_ROWS:, :] = rows.astype(out_ref.dtype)

    return pl.pallas_call(
        kernel,
        out_shape=jax.ShapeDtypeStruct((HALF_G, PIECE_ROWS, chans), jnp.bfloat16),
        in_specs=[SMEM, VMEM, VMEM, VMEM],
        out_specs=VMEM,
        scratch_shapes=[pltpu.VMEM((HALF_D * chans + 16, chans), jnp.float32)],
        compiler_params=pltpu.CompilerParams(vmem_limit_bytes=24 * 2**20),
        cost_estimate=pl.CostEstimate(
            flops=2 * HALF_D * cols.shape[0] * chans * chans,
            bytes_accessed=5 * 10**6,
            transcendentals=0,
        ),
    )(core.reshape(1), gram, cols, dpre)


def choose(which, table, place, *arrays):
    def kernel(table_ref, place_ref, *refs):
        number = which(table_ref, place_ref[0], place_ref[1])
        for k, ref in enumerate(refs[:-1]):

            @pl.when(number == k)
            def _(ref=ref):
                refs[-1][...] = ref[...]

    return pl.pallas_call(
        kernel,
        out_shape=jax.ShapeDtypeStruct(arrays[0].shape, arrays[0].dtype),
        in_specs=[SMEM, SMEM] + [VMEM] * len(arrays),
        out_specs=VMEM,
        cost_estimate=pl.CostEstimate(flops=0, bytes_accessed=500000, transcendentals=0),
    )(table, place, *arrays)


def layer_at(table_ref, owner):
    lay = jnp.int32(0)
    for l in range(1, table_ref.shape[0]):
        lay = jnp.where(table_ref[l] == owner, l, lay)
    return lay


def for_groups(table, place, held, piece):
    def kernel(table_ref, place_ref, held_ref, piece_ref, out_ref):
        for z in range(ZH):
            out_ref[z, :, :FAC_ROWS, :] = held_ref[layer_at(table_ref, z * Y + place_ref[0])]
            out_ref[z, :, FAC_ROWS:, :] = piece_ref[:, FAC_ROWS:, :]

    return pl.pallas_call(
        kernel,
        out_shape=jax.ShapeDtypeStruct((ZH,) + piece.shape, piece.dtype),
        in_specs=[SMEM, SMEM, VMEM, VMEM],
        out_specs=VMEM,
        cost_estimate=pl.CostEstimate(flops=0, bytes_accessed=500000, transcendentals=0),
    )(table, place, held, piece)


def factor_rows(blocks, table, place, rows, count):
    chans = blocks.shape[-1]
    index = jnp.array([WHERE[a, b][0] for a in range(9) for b in range(9)], jnp.int32)
    flips = jnp.array([int(WHERE[a, b][1]) for a in range(9) for b in range(9)], jnp.int32)

    def kernel(index_ref, flip_ref, table_ref, place_ref, blocks_ref, out_ref, own_ref, band):
        owner = place_ref[1] * Y + place_ref[0]
        scale = jnp.float32(0.0)
        for l in range(table_ref.shape[0]):
            scale = jnp.where(table_ref[l] == owner, jnp.float32(1.0 / count), scale)
        start = place_ref[2] * rows
        tap = lax.div(start, chans)
        for t in range(2):
            a = jnp.minimum(tap + t, 8)
            for b in range(9):
                block = blocks_ref[index_ref[a * 9 + b], :chans, :].astype(jnp.float32)
                flip = flip_ref[a * 9 + b] != 0
                band[t * chans : (t + 1) * chans, b * chans : (b + 1) * chans] = jnp.where(
                    flip, block.T, block
                )
        inside = start - tap * chans
        base = pl.multiple_of(lax.div(inside, 8) * 8, 8)
        got = band[pl.ds(base, rows + 4), :]
        odd = inside != base
        out_ref[...] = jnp.where(odd, got[4:], got[:rows]) * scale
        own_ref[...] = blocks_ref[NG, :chans, :].astype(jnp.float32) * scale

    return pl.pallas_call(
        kernel,
        out_shape=(
            jax.ShapeDtypeStruct((rows, 9 * chans), jnp.float32),
            jax.ShapeDtypeStruct((chans, chans), jnp.float32),
        ),
        in_specs=[SMEM, SMEM, SMEM, SMEM, VMEM],
        out_specs=(VMEM, VMEM),
        scratch_shapes=[pltpu.VMEM((2 * chans, 9 * chans), jnp.float32)],
        compiler_params=pltpu.CompilerParams(vmem_limit_bytes=16 * 2**20),
        cost_estimate=pl.CostEstimate(flops=10**6, bytes_accessed=2 * 10**6, transcendentals=0),
    )(index, flips, table, place, blocks)


def shards(feats, top_grad, weights, table, a_inv, g_inv):
    num_layers, _, rows_dev, width, chans = feats.shape
    owners = lax.axis_size(OWNER)
    samples = lax.axis_size(DP)
    owner_id = lax.axis_index(OWNER)
    dp_id = lax.axis_index(DP)
    y_id = lax.axis_index("y")
    z_id = lax.axis_index("zh")
    npos = samples * rows_dev * owners * width
    patch = 9 * chans
    inner = owner_id < owners - 1
    f = feats[:, 0]
    top = top_grad[0]

    to_above, to_below = halo_rows(f, top)
    below = shifted(to_above, -1, True)
    above = shifted(to_below, 1, False)
    below1 = below[5:]
    below = jnp.where(inner, below[:5], jnp.zeros_like(below[:5]))
    wide3 = jnp.concatenate([above[:2], f[3], below[:2]])
    strips = [
        jnp.concatenate([above[3:4], f[0], below[3:4]]),
        jnp.concatenate([f[1], below1]),
        jnp.concatenate([above[2:3], f[2], below[2:3]]),
        wide3[1:5],
    ]
    core_id = lax.axis_index("core")

    def to_layers(x):
        return exchange(jnp.broadcast_to(x[None], (CORE,) + x.shape).reshape((-1,) + x.shape[1:]), ("core", "y"))

    flipped = jnp.transpose(weights.reshape(num_layers, 9, chans, chans), (0, 1, 3, 2)).reshape(
        num_layers, patch, chans
    )

    def slope(layer, win):
        pre = jnp.dot(to_columns(win), weights[layer], preferred_element_type=jnp.float32)
        return silu_slope(pre)

    def times(grad_in, slopes):
        return (grad_in.reshape(slopes.shape).astype(jnp.float32) * slopes).astype(jnp.bfloat16)

    def back(layer, win):
        return jnp.dot(
            back_columns(win), flipped[layer], preferred_element_type=jnp.float32
        ).astype(jnp.bfloat16)

    image = (rows_dev, width, chans)
    top_wide = jnp.concatenate([above[4:5], top, below[4:5]])
    dpre3 = times(top_wide, slope(3, windows(wide3))).reshape((rows_dev + 2, width, chans))
    dpre2 = times(back(3, windows(dpre3)), slope(2, windows(strips[2]))).reshape(image)
    after = shifted(dpre2, -1, True)
    dy1 = back(2, cut_windows(jnp.concatenate([dpre2, after]), inner))
    dpre1 = times(dy1, slope(1, cut_windows(strips[1], inner))).reshape(image)
    trimmed = [
        jnp.concatenate([jnp.where(y_id == 0, rows[:1], rows[3:]), rows[1:3]]) for rows in strips
    ]
    local = jnp.concatenate([a_inv.reshape(-1, chans), g_inv[0].astype(jnp.bfloat16)])
    stacked, dpre1, local = lax.optimization_barrier((jnp.stack(trimmed), dpre1, local))
    before = shifted(dpre1, 1, True)
    layer_strips = to_layers(stacked)
    near = paired(local, "y", 0)
    edge_top = jnp.where(owner_id > 0, before[:1], jnp.zeros_like(before[:1]))
    edge_end = jnp.where(inner, dpre1[1:], jnp.zeros_like(dpre1[1:]))
    dy0 = back(1, windows(jnp.concatenate([edge_top, before[1:], dpre1[:1], edge_end])))
    dpre0 = times(dy0, slope(0, windows(strips[0]))).reshape(image)

    images = layer_strips.reshape((CORE, Y) + layer_strips.shape[1:])
    last_one = (y_id == 1) & (z_id == ZH - 1)
    seam = jnp.zeros((Y * rows_dev, 3), bool).at[-2, 2].set(True).at[-1, 0].set(True)
    cols = []
    for image_rows in images:
        middle = image_rows[:, 1:].reshape((-1,) + image_rows.shape[2:])
        win = windows(jnp.concatenate([image_rows[0, :1], middle, image_rows[-1, :1]]))
        cut = (seam & last_one)[:, :, None, None]
        cols.append(to_columns(jnp.where(cut, jnp.zeros_like(win), win)))
    cols = jnp.concatenate(cols)
    gram = gram_half(cols, core_id)

    def for_partner(table_ref, y, z):
        return jnp.where((table_ref[3 - y] & 3) == y, 0, 1)

    def in_group(table_ref, y, z):
        want = table_ref[y] & 3
        return jnp.where(want == y, 0, jnp.where(want == (y ^ 1), 1, 2))

    def beside(table_ref, y, z):
        return jnp.where((table_ref[y] >> 2) == (z ^ 1), 1, 0)

    layer_dpre = to_layers(jnp.stack([dpre0, dpre1, dpre2, dpre3[1:3]]))
    parts = all_half(gram, cols, layer_dpre.reshape(-1, chans), core_id)

    place = jnp.stack([y_id, z_id, dp_id]).astype(jnp.int32)
    parts, local, near = lax.optimization_barrier((parts, local, near))
    away = choose(for_partner, table, place, local, near)
    found = choose(in_group, table, place, local, near, paired(away, "y", 1))
    other = paired(found, "zh", 0)
    piece = scatter_sum(parts, ("x", "zl"))
    piece, other = lax.optimization_barrier((piece, other))
    found = choose(beside, table, place, found, other)
    source = jnp.sum(jnp.where(jnp.arange(num_layers) == y_id, table, 0))
    inverses = jnp.where((source >> 3) == (z_id >> 1), found, paired(found, "zh", 1))
    held = spread(piece[:, :FAC_ROWS], "y")
    total = exchange(for_groups(table, place, held, piece), "zh")
    total = jnp.sum(total.astype(jnp.float32), axis=0).astype(jnp.bfloat16)
    summed = spread(spread(spread(total, "zl"), "x"), "core")

    in_grad_win = jnp.concatenate([shifted(dpre0[1:], 1, False), dpre0, shifted(dpre0[:1], -1, False)])
    in_grad = back(0, windows(in_grad_win)).reshape((1,) + image)

    stats = summed.reshape(CORE * HALF_G, PIECE_ROWS, chans)
    grad_sum = stats[:, FAC_ROWS : FAC_ROWS + GRAD_ROWS].reshape(-1, chans)[:patch]
    rows_out = patch // samples
    a_mine = inverses[: rows_out * 9].reshape(rows_out, patch)
    mixed = jnp.dot(grad_sum, inverses[rows_out * 9 :], preferred_element_type=jnp.float32)
    mixed = mixed / jnp.sqrt(jnp.float32(npos))
    panel = jnp.dot(a_mine.astype(jnp.float32), mixed, precision=lax.Precision.HIGHEST)
    step_out = spread(panel.astype(jnp.bfloat16), "y")

    a_out, g_out = factor_rows(stats, table, place, rows_out, npos)
    a_out, g_out = a_out[None], g_out[None]
    return (step_out, a_out, g_out, in_grad)


def solution(mesh):
    fine = Mesh(mesh.devices.reshape(X, ZL, CORE, ZH, Y), DP + OWNER)
    placed = (
        P(None, DP, OWNER, None, None),
        P(DP, OWNER, None, None),
        P(),
        P(),
        P(OWNER, DP, None),
        P(OWNER, None, None),
    )
    return jax.shard_map(
        shards,
        mesh=fine,
        in_specs=placed,
        out_specs=(
            P(None, DP, None),
            P(OWNER, DP, None),
            P(OWNER, None, None),
            P(DP, OWNER, None, None),
        ),
        check_vma=False,
    )
```
